32 devices in a mesh: case: 2 (over y), span: 8 (over z, x), sect: 2 (over core).
Axes of the slice: x: 2, y: 2, z: 4, core: 2. Of those that a mesh axis runs over, the one named last changes fastest.
Arguments:
- fine_field: bfloat16 [16, 3, 32, 128, 128], P('case', None, 'sect', 'span'), parts along dimension 0, may hold values from -16 to 16
- stored: bfloat16 [248, 49152], P(None, ('case', 'span', 'sect')), parts along dimension 1, may hold values from -16 to 16
- filter_taps: float32 [3, 17], replicated, may hold values from 0.1 to 0.5
Outputs:
- coarse_new: bfloat16 [8, 49152], P(None, ('case', 'span', 'sect')), parts along dimension 1
- factor: float32 [512, 256], P('case'), parts along dimension 0
- basis: float32 [256, 49152], P(None, ('case', 'span', 'sect')), parts along dimension 1
The draws below stay inside these ranges and needn't reach their ends.
There are 2 independent parts, one for each index of `case`. The reference program is written for one: setup_inputs(seed, part) draws one part's arguments, and reference() takes and returns one part's arrays. A program takes and returns all parts, laid end to end along the dimension named above; an argument that names none is the same for every part. Nothing has to cross between parts.
All inputs are finite; a program needn't handle non-finite values.
Results may differ from the reference program's by a relative error of at most 0.011.
Values may be sent and summed in bfloat16 or wider, within the bound.
No kernel may reach another device: no remote copies, remote signals or barrier semaphores. Data moves between devices by JAX's collectives and lax.ppermute only.
A program may use at most 64 MiB of HBM per device.

```python
import jax
import jax.numpy as jnp
from jax import lax

NEW = 8
WIN_OLD = 248
FX = 128
FY = 16
FZ = 16
NY = 32
NZ = 128
ROWS = 24576
N_SPAN = 8
N_SECT = 2


def draw_stored(key, part):
    key = jax.random.fold_in(key, 11)
    keys = jax.random.split(key, 3)
    column_scale = jnp.exp(jax.random.uniform(keys[0], (WIN_OLD, 1), jnp.float32, jnp.log(0.5), jnp.log(2.0)))
    row_scale = jnp.exp(jax.random.uniform(keys[1], (1, ROWS), jnp.float32, 0.0, jnp.log(3.0)))
    rising = 1.0 + 2.0 * jnp.arange(ROWS, dtype=jnp.float32)[None, :] / ROWS
    base = jnp.clip(jax.random.normal(keys[2], (WIN_OLD, ROWS), jnp.float32), -4.0, 4.0)
    values = jnp.clip(base * column_scale * row_scale * rising, -16.0, 16.0)
    return values.astype(jnp.bfloat16)


def draw_fine_field(key, part):
    key = jax.random.fold_in(key, 23)
    keys = jax.random.split(key, 2)
    shape = (NEW, 3, NY, NZ, FX)
    rising = 1.0 + 2.0 * jnp.arange(NZ, dtype=jnp.float32)[:, None] / NZ
    rough = jnp.exp(jax.random.uniform(keys[1], shape, jnp.float32, -0.5, 0.5))
    base = jnp.clip(jax.random.normal(keys[0], shape, jnp.float32), -4.0, 4.0)
    values = jnp.clip(base * rough * rising, -16.0, 16.0)
    return values.astype(jnp.bfloat16)


def setup_inputs(seed: int = 0, part: int = 0) -> dict:
    arg_keys = jax.random.split(jax.random.key(seed), 4)
    part_keys = jax.random.split(jax.random.fold_in(arg_keys[3], part), 4)
    return {
        "fine_field": draw_fine_field(jax.random.fold_in(jax.random.fold_in(arg_keys[3], part), 71), part),
        "stored": draw_stored(jax.random.fold_in(jax.random.fold_in(arg_keys[3], part), 71), part),
        "filter_taps": jnp.clip(jax.random.uniform(arg_keys[2], (3, 17), jnp.float32, 0.1, 0.5), 0.1, 0.5),
    }


def strided_taps(values, weights, along, length):
    summed = weights[0] * lax.slice_in_dim(values, 0, 4 * (length - 1) + 1, 4, along)
    for offset in range(1, 17):
        summed = summed + weights[offset] * lax.slice_in_dim(values, offset, offset + 4 * (length - 1) + 1, 4, along)
    return summed

def pad_along(values, along):
    widths = [(0, 0)] * values.ndim
    widths[along] = (8, 8)
    return jnp.pad(values, widths)

def reference(fine_field, stored, filter_taps):
    coarse = strided_taps(pad_along(fine_field, 4), filter_taps[2], 4, FX // 4)
    coarse = strided_taps(pad_along(coarse, 2), filter_taps[0], 2, NY // 4)
    coarse = strided_taps(pad_along(coarse, 3), filter_taps[1], 3, NZ // 4)
    coarse = coarse.astype(jnp.bfloat16)
    coarse = coarse.reshape(NEW, 3, N_SECT, FY // 4, N_SPAN, FZ // 4, FX // 4)
    coarse_new = coarse.transpose(0, 4, 2, 1, 3, 5, 6).reshape(NEW, ROWS)
    window = jnp.concatenate([stored, coarse_new], axis=0)
    gram = jnp.dot(window.astype(jnp.float32), window.T.astype(jnp.float32), preferred_element_type=jnp.float32) / ROWS
    factor = jnp.linalg.cholesky(gram)
    basis = jax.scipy.linalg.solve_triangular(factor, window.astype(jnp.float32), lower=True)
    return (coarse_new, factor, basis)
```

```python
import jax
import jax.numpy as jnp
from jax import lax
from jax.sharding import PartitionSpec as P


def with_halo(cells, sides, width):
    for axis, dim in sides:
        count = lax.axis_size(axis)
        ends = count - 1
        head = lax.slice_in_dim(cells, 0, width, axis=dim)
        tail = lax.slice_in_dim(cells, cells.shape[dim] - width, cells.shape[dim], axis=dim)
        cells = jnp.concatenate(
            [
                lax.ppermute(tail, axis, [(i, (i + 1) % count) for i in range(ends)]),
                cells,
                lax.ppermute(head, axis, [((i + 1) % count, i) for i in range(ends)]),
            ],
            axis=dim,
        )
    return cells


def band_matrix(weights, n_in, n_out, shift):
    rows_in = jnp.arange(n_in, dtype=jnp.int32)[:, None]
    cols_out = jnp.arange(n_out, dtype=jnp.int32)[None, :]
    offset = rows_in - 4 * cols_out + shift
    taps = jnp.arange(17, dtype=jnp.int32)
    hits = offset[:, :, None] == taps[None, None, :]
    return jnp.sum(jnp.where(hits, weights[None, None, :], 0.0), axis=2)


def contract(form, values, matrix):
    return jnp.einsum(
        form, values, matrix, precision=lax.Precision.HIGHEST, preferred_element_type=jnp.float32
    )


def swap(values, axis, bit):
    count = lax.axis_size(axis)
    return lax.ppermute(values, axis, [(i, i ^ bit) for i in range(count)])


def sum_over_group(terms):
    spans = lax.axis_size("span")
    if spans & (spans - 1) or lax.axis_size("sect") != 2:
        return lax.psum(terms, ("span", "sect"))
    me = lax.axis_index("sect")
    half = terms.shape[0] // 2
    kept = lax.dynamic_slice_in_dim(terms, me * half, half, 0)
    sent = lax.dynamic_slice_in_dim(terms, (1 - me) * half, half, 0)
    kept = kept + swap(sent, "sect", 1)
    bit = 1
    while bit < spans:
        kept = kept + swap(kept, "span", bit)
        bit *= 2
    other = swap(kept, "sect", 1)
    first = jnp.where(me == 0, kept, other)
    second = jnp.where(me == 0, other, kept)
    return jnp.concatenate([first, second], axis=0)


def local(fine_field, stored, filter_taps):
    snapshots, comps, cells_y, cells_z, cells_x = fine_field.shape
    coarse_y, coarse_z, coarse_x = (cells_y // 4, cells_z // 4, cells_x // 4)
    stream_matrix = band_matrix(filter_taps[2], cells_x, coarse_x, 8)
    padded = with_halo(fine_field, (("span", 3), ("sect", 2)), 8)
    coarse = contract("ncyzx,xj->ncyzj", padded, stream_matrix)
    coarse = contract(
        "ncyzj,yk->nckzj", coarse, band_matrix(filter_taps[0], cells_y + 16, coarse_y, 0)
    )
    coarse = contract(
        "nckzj,zl->ncklj", coarse, band_matrix(filter_taps[1], cells_z + 16, coarse_z, 0)
    )
    rows_dev = comps * coarse_y * coarse_z * coarse_x
    coarse_new = coarse.astype(jnp.bfloat16).reshape(snapshots, rows_dev)
    window = jnp.concatenate([stored, coarse_new], axis=0)
    groups = lax.axis_size("span") * lax.axis_size("sect")
    total_rows = rows_dev * groups
    local_gram = jnp.dot(window, window.T, preferred_element_type=jnp.float32) / total_rows
    gram = sum_over_group(local_gram)
    lower = jnp.linalg.cholesky(gram)
    basis = jax.scipy.linalg.solve_triangular(lower, window.astype(jnp.float32), lower=True)
    return (coarse_new, lower, basis)


def solution(mesh):
    in_specs = (P("case", None, "sect", "span", None), P(None, ("case", "span", "sect")), P())
    out_specs = (
        P(None, ("case", "span", "sect")),
        P("case", None),
        P(None, ("case", "span", "sect")),
    )
    return jax.shard_map(local, mesh=mesh, in_specs=in_specs, out_specs=out_specs, check_vma=False)
```

```python
import functools

import jax
import jax.numpy as jnp
from jax import lax
from jax.experimental import pallas as pl
from jax.experimental.pallas import tpu as pltpu
from jax.sharding import PartitionSpec as P

F32 = jnp.float32
BF16 = jnp.bfloat16
TAPS = 17
LANES = 128
PANEL = 64


def iota(shape, dim):
    return lax.broadcasted_iota(jnp.int32, shape, dim)


def split2(values):
    high = values.astype(BF16)
    return high, (values - high.astype(F32)).astype(BF16)


def split3(values):
    high = values.astype(BF16)
    rest = values - high.astype(F32)
    middle = rest.astype(BF16)
    return high, middle, (rest - middle.astype(F32)).astype(BF16)


def weights_at(offset, taps_ref, row):
    total = jnp.zeros(offset.shape, F32)
    for tap in range(TAPS):
        total = jnp.where(offset == tap, taps_ref[row, tap], total)
    return total


def filter_kernel(place_ref, fine_ref, taps_ref, own_ref, ext_ref, send_ref, plane_ref, row_ref):
    first = place_ref[0] == 0
    fields = fine_ref.shape[0]
    slot, cell = iota((64, 256), 0), iota((64, 256), 1)
    span_slot, sect_slot = slot // 8, slot % 8
    span_cell = jnp.where(span_slot < 6, span_slot, span_slot - 8)
    sect_cell = jnp.where((sect_slot < 4) | first, sect_slot, sect_slot - 6)
    span_tap = cell % 16 - 4 * span_cell + 8
    sect_tap = jnp.where(sect_slot < 6, cell // 16 - 4 * sect_cell + 8, -1)
    plane = weights_at(span_tap, taps_ref, 1) * weights_at(sect_tap, taps_ref, 0)
    plane = jnp.concatenate(split2(plane), axis=0)
    for field in range(fields):
        both = jnp.dot(plane, fine_ref[field], preferred_element_type=F32)
        summed = both[:64] + both[64:]
        for s in range(8):
            plane_ref[s, 8 * field : 8 * field + 8, :] = summed[8 * s : 8 * s + 8]
    cell, lane = iota((LANES, LANES), 0), iota((LANES, LANES), 1)
    stream = weights_at(cell - 4 * (lane % 32) + 8, taps_ref, 2)
    parts = [
        jnp.concatenate([jnp.where(lane // 32 == s, part, 0.0) for s in range(4)], axis=0).astype(BF16)
        for part in (stream.astype(BF16).astype(F32), stream - stream.astype(BF16).astype(F32))
    ]
    matrix = jnp.concatenate([parts[0], parts[0], parts[1]], axis=0)
    for half in range(2):
        values = jnp.concatenate([plane_ref[4 * half + s] for s in range(4)], axis=1)
        high, low = split2(values)
        row_ref[half] = jnp.dot(
            jnp.concatenate([high, low, high], axis=1), matrix, preferred_element_type=F32
        )
    for comp in range(3):
        for k in range(4):
            rows = pl.ds(8 * comp + k, 8, stride=24)
            own_ref[4 * comp + k] = row_ref[0, rows, :]
            ext_ref[4 * comp + k] = row_ref[1, rows, :]
        for k in range(2):
            rows = pl.ds(8 * comp + 4 + k, 8, stride=24)
            for half in range(2):
                send_ref[6 * half + 2 * comp + k] = row_ref[half, rows, :]


def gram_kernel(
    total, place_ref, stored_ref, own_ref, partner_ref, left_ref, right_ref, coarse_ref, window_ref, kept_ref, sent_ref
):
    first = place_ref[0] == 0
    old = stored_ref.shape[0]
    lane = iota((8, LANES), 1)
    cells = []
    for comp in range(3):
        for k in range(4):
            at = 4 * comp + k
            value = own_ref[at] + jnp.where(lane < 64, left_ref[at], right_ref[at])
            here = first if k >= 2 else jnp.logical_not(first)
            cells.append(value + jnp.where(here, partner_ref[2 * comp + k % 2], 0.0))
    coarse = jnp.concatenate(cells, axis=1).astype(BF16)
    coarse_ref[...] = coarse
    window_ref[: old - 8, :] = stored_ref[: old - 8, :]
    window_ref[old - 8 :, :] = jnp.concatenate(
        [stored_ref[old - 8 :, :].astype(F32), coarse.astype(F32)], axis=0
    ).astype(BF16)
    window = window_ref[...]
    gram = lax.dot_general(window, window, (((1,), (1,)), ((), ())), preferred_element_type=F32) / total
    row, col = iota((LANES, LANES), 0), iota((LANES, LANES), 1)
    upper, lower = gram[:LANES, :LANES], gram[LANES:, LANES:]
    packed = jnp.where(row >= col, upper, lower)
    corner = jnp.sum(jnp.where(row == col, lower, 0.0), axis=0, keepdims=True)
    corner = jnp.broadcast_to(corner, (8, LANES))
    across = gram[:LANES, LANES:]
    kept_ref[:LANES] = jnp.where(first, packed, across)
    kept_ref[LANES:] = corner
    sent_ref[:LANES] = jnp.where(first, across, packed)
    sent_ref[LANES:] = corner


def eliminate(groups, at, lane):
    count = len(groups)
    width = groups[at].shape[1]
    wide = lambda column: jnp.concatenate([column] * (width // LANES), axis=1)
    spread = lambda row: jnp.broadcast_to(row, (8, row.shape[1]))
    sub = iota((8, LANES), 0)
    sub_wide = iota((8, width), 0)
    cols = {
        (j, g): jnp.broadcast_to(groups[g][:, lane + j : lane + j + 1], (8, LANES))
        for j in range(8)
        for g in range(at, count)
    }
    for k in range(8):
        scale = lax.rsqrt(spread(cols[k, at][k : k + 1, :]))
        row = spread(groups[at][k : k + 1, :]) * wide(scale)
        heads = {j: spread(cols[j, at][k : k + 1, :]) * scale for j in range(k + 1, 8)}
        for g in range(at, count):
            share = cols[k, g] * scale
            if g == at:
                share = jnp.where(sub > k, share, 0.0)
            for j in range(k + 1, 8):
                cols[j, g] = cols[j, g] - share * heads[j]
            updated = groups[g] - wide(share) * row
            groups[g] = jnp.where(sub_wide == k, row, updated) if g == at else updated
    return groups


def factor_kernel(place_ref, kept_ref, other_ref, window_ref, factor_ref, basis_ref, left_ref, inverse_ref, upper_ref):
    first = place_ref[0] == 0
    size = left_ref.shape[0]
    row, col = iota((LANES, LANES), 0), iota((LANES, LANES), 1)
    packed = jnp.where(first, kept_ref[:LANES], other_ref[:LANES])
    across = jnp.where(first, other_ref[:LANES], kept_ref[:LANES])
    corner = jnp.where(first, kept_ref[LANES : LANES + 1], other_ref[LANES : LANES + 1])
    turned = packed.T
    left_ref[:LANES, :LANES] = jnp.where(row >= col, packed, turned)
    left_ref[:LANES, LANES:] = across
    left_ref[LANES:, :LANES] = jnp.zeros((LANES, LANES), F32)
    left_ref[LANES:, LANES:] = jnp.where(
        row == col, jnp.broadcast_to(corner, (LANES, LANES)), jnp.where(row > col, turned, packed)
    )
    row, col = iota((size, size), 0), iota((size, size), 1)
    inverse_ref[...] = jnp.where(row == col, 1.0, 0.0)
    upper_ref[...] = jnp.zeros((size, size), F32)
    for begin in range(0, size, PANEL):
        end = begin + PANEL
        skip = 0 if begin < LANES else LANES
        reach = LANES if end <= LANES else size
        groups = [
            jnp.concatenate([left_ref[g : g + 8, skip:], inverse_ref[g : g + 8, :reach]], axis=1)
            for g in range(begin, end, 8)
        ]
        for g in range(PANEL // 8):
            groups = eliminate(groups, g, begin + 8 * g - skip)
        panel = jnp.concatenate(groups, axis=0)
        upper_ref[begin:end, skip:] = panel[:, : size - skip]
        inverse_ref[begin:end, :reach] = panel[:, size - skip :]
        if end < size:
            high, middle, low = split3(panel)
            right = jnp.concatenate([high, middle, high, low, high, middle], axis=0)
            high, middle, low = split3(panel[:, : size - skip].T[end - skip :, :])
            left = jnp.concatenate([high, high, middle, high, low, middle], axis=1)
            share = jnp.dot(left, right, preferred_element_type=F32)
            left_ref[end:, skip:] = left_ref[end:, skip:] - share[:, : size - skip]
            inverse_ref[end:, :reach] = inverse_ref[end:, :reach] - share[:, size - skip :]
    factor_ref[...] = jnp.where(row >= col, upper_ref[...].T, 0.0)
    high, low = split2(jnp.where(row >= col, inverse_ref[...], 0.0))
    left = jnp.concatenate([high, low], axis=1)
    wide = 512
    for at in range(0, window_ref.shape[1], wide):
        cells = window_ref[:, at : at + wide]
        basis_ref[:, at : at + wide] = jnp.dot(
            left, jnp.concatenate([cells, cells], axis=0), preferred_element_type=F32
        )


VMEM = pl.BlockSpec(memory_space=pltpu.VMEM)
SMEM = pl.BlockSpec(memory_space=pltpu.SMEM)
LIMIT = pltpu.CompilerParams(vmem_limit_bytes=48 * 2**20)


def shaped(shape, dtype=F32):
    return jax.ShapeDtypeStruct(shape, dtype)


def swap(values, axis, bit):
    count = lax.axis_size(axis)
    return lax.ppermute(values, axis, [(i, i ^ bit) for i in range(count)])


def shift(values, axis, step):
    count = lax.axis_size(axis)
    return lax.ppermute(values, axis, [(i, i + step) for i in range(count) if 0 <= i + step < count])


def sum_over_span(values):
    count = lax.axis_size("span")
    if count & (count - 1):
        return lax.psum(values, "span")
    bit = 1
    while bit < count:
        values = values + swap(values, "span", bit)
        bit *= 2
    return values


def local(fine_field, stored, filter_taps):
    snapshots, comps, cells_y, cells_z, cells_x = fine_field.shape
    assert (snapshots, comps, cells_y, cells_z, cells_x) == (8, 3, 16, 16, 128)
    assert lax.axis_size("sect") == 2
    old, rows_dev = stored.shape
    size = old + snapshots
    total = rows_dev * lax.axis_size("span") * lax.axis_size("sect")
    place = lax.axis_index("sect").astype(jnp.int32).reshape(1)
    fields = snapshots * comps
    own, ext, send = pl.pallas_call(
        filter_kernel,
        out_shape=[shaped((12, 8, LANES))] * 3,
        in_specs=[SMEM, VMEM, SMEM],
        out_specs=[VMEM] * 3,
        scratch_shapes=[pltpu.VMEM((8, 8 * fields, LANES), F32), pltpu.VMEM((2, 8 * fields, LANES), F32)],
        compiler_params=LIMIT,
        name="filter",
    )(place, fine_field.reshape(fields, cells_y * cells_z, cells_x), filter_taps)
    partner = swap(send, "sect", 1)
    own_share, ext_share = partner[:6], partner[6:].reshape(3, 2, 8, LANES)
    none = jnp.zeros_like(ext_share)
    ext_share = jnp.where(
        place[0] == 0,
        jnp.concatenate([none, ext_share], axis=1),
        jnp.concatenate([ext_share, none], axis=1),
    )
    ext = ext + ext_share.reshape(12, 8, LANES)
    from_left = shift(ext, "span", 1)
    from_right = shift(ext, "span", -1)
    coarse_new, window, kept, sent = pl.pallas_call(
        functools.partial(gram_kernel, total),
        out_shape=[
            shaped((snapshots, rows_dev), BF16),
            shaped((size, rows_dev), BF16),
            shaped((LANES + 8, LANES)),
            shaped((LANES + 8, LANES)),
        ],
        in_specs=[SMEM] + [VMEM] * 5,
        out_specs=[VMEM] * 4,
        compiler_params=LIMIT,
        name="gram",
    )(place, stored, own, own_share, from_left, from_right)
    kept = sum_over_span(kept + swap(sent, "sect", 1))
    other = swap(kept, "sect", 1)
    factor, basis = pl.pallas_call(
        factor_kernel,
        out_shape=[shaped((size, size)), shaped((size, rows_dev))],
        in_specs=[SMEM] + [VMEM] * 3,
        out_specs=[VMEM] * 2,
        scratch_shapes=[pltpu.VMEM((size, size), F32)] * 3,
        compiler_params=LIMIT,
        name="factor",
    )(place, kept, other, window)
    return (coarse_new, factor, basis)


def solution(mesh):
    in_specs = (P("case", None, "sect", "span", None), P(None, ("case", "span", "sect")), P())
    out_specs = (
        P(None, ("case", "span", "sect")),
        P("case", None),
        P(None, ("case", "span", "sect")),
    )
    return jax.shard_map(local, mesh=mesh, in_specs=in_specs, out_specs=out_specs, check_vma=False)
```

```python
import functools

import jax
import jax.numpy as jnp
from jax import lax
from jax.experimental import pallas as pl
from jax.experimental.pallas import tpu as pltpu
from jax.sharding import PartitionSpec as P

F32 = jnp.float32
BF16 = jnp.bfloat16
TAPS = 17
LANES = 128
PANEL = 64
NEAR = 8
FAR = 8


def iota(shape, dim):
    return lax.broadcasted_iota(jnp.int32, shape, dim)


def split2(values):
    high = values.astype(BF16)
    return high, (values - high.astype(F32)).astype(BF16)


def split3(values):
    high = values.astype(BF16)
    rest = values - high.astype(F32)
    middle = rest.astype(BF16)
    return high, middle, (rest - middle.astype(F32)).astype(BF16)


def weights_at(offset, taps_ref, row):
    total = jnp.zeros(offset.shape, F32)
    for tap in range(TAPS):
        total = jnp.where(offset == tap, taps_ref[row, tap], total)
    return total


def filter_kernel(place_ref, fine_ref, taps_ref, own_ref, ext_ref, send_ref, plane_ref, row_ref):
    first = place_ref[0] == 0
    fields = fine_ref.shape[0]
    slot, cell = iota((64, 256), 0), iota((64, 256), 1)
    span_slot, sect_slot = slot // 8, slot % 8
    span_cell = jnp.where(span_slot < 6, span_slot, span_slot - 8)
    sect_cell = jnp.where((sect_slot < 4) | first, sect_slot, sect_slot - 6)
    span_tap = cell % 16 - 4 * span_cell + 8
    sect_tap = jnp.where(sect_slot < 6, cell // 16 - 4 * sect_cell + 8, -1)
    plane = weights_at(span_tap, taps_ref, 1) * weights_at(sect_tap, taps_ref, 0)
    plane = jnp.concatenate(split2(plane), axis=0)
    for field in range(fields):
        both = jnp.dot(plane, fine_ref[field], preferred_element_type=F32)
        summed = both[:64] + both[64:]
        for s in range(8):
            plane_ref[s, 8 * field : 8 * field + 8, :] = summed[8 * s : 8 * s + 8]
    cell, lane = iota((LANES, LANES), 0), iota((LANES, LANES), 1)
    stream = weights_at(cell - 4 * (lane % 32) + 8, taps_ref, 2)
    parts = [
        jnp.concatenate([jnp.where(lane // 32 == s, part, 0.0) for s in range(4)], axis=0).astype(BF16)
        for part in (stream.astype(BF16).astype(F32), stream - stream.astype(BF16).astype(F32))
    ]
    matrix = jnp.concatenate([parts[0], parts[0], parts[1]], axis=0)
    for half in range(2):
        values = jnp.concatenate([plane_ref[4 * half + s] for s in range(4)], axis=1)
        high, low = split2(values)
        row_ref[half] = jnp.dot(
            jnp.concatenate([high, low, high], axis=1), matrix, preferred_element_type=F32
        )
    for comp in range(3):
        for k in range(4):
            rows = pl.ds(8 * comp + k, 8, stride=24)
            own_ref[4 * comp + k] = row_ref[0, rows, :]
            ext_ref[4 * comp + k] = row_ref[1, rows, :]
        for k in range(2):
            rows = pl.ds(8 * comp + 4 + k, 8, stride=24)
            for half in range(2):
                send_ref[6 * half + 2 * comp + k] = row_ref[half, rows, :]


def gram_kernel(
    total, place_ref, stored_ref, own_ref, partner_ref, left_ref, right_ref, coarse_ref, window_ref, kept_ref, sent_ref
):
    first = place_ref[0] == 0
    old = stored_ref.shape[0]
    lane = iota((8, LANES), 1)
    cells = []
    for comp in range(3):
        for k in range(4):
            at = 4 * comp + k
            value = own_ref[at] + jnp.where(lane < 64, left_ref[at], right_ref[at])
            here = first if k >= 2 else jnp.logical_not(first)
            cells.append(value + jnp.where(here, partner_ref[2 * comp + k % 2], 0.0))
    coarse = jnp.concatenate(cells, axis=1).astype(BF16)
    coarse_ref[...] = coarse
    window_ref[: old - 8, :] = stored_ref[: old - 8, :]
    window_ref[old - 8 :, :] = jnp.concatenate(
        [stored_ref[old - 8 :, :].astype(F32), coarse.astype(F32)], axis=0
    ).astype(BF16)
    window = window_ref[...]
    gram = lax.dot_general(window, window, (((1,), (1,)), ((), ())), preferred_element_type=F32) / total
    row, col = iota((LANES, LANES), 0), iota((LANES, LANES), 1)
    upper, lower = gram[:LANES, :LANES], gram[LANES:, LANES:]
    packed = jnp.where(row >= col, upper, lower)
    corner = jnp.sum(jnp.where(row == col, lower, 0.0), axis=0, keepdims=True)
    corner = jnp.broadcast_to(corner, (8, LANES))
    across = gram[:LANES, LANES:]
    kept_ref[:LANES] = jnp.where(first, packed, across)
    kept_ref[LANES:] = corner
    sent_ref[:LANES] = jnp.where(first, across, packed)
    sent_ref[LANES:] = corner


def eliminate(groups, at, lane, none, scale_ref):
    count = len(groups)
    width = groups[at].shape[1]
    wide = lambda column: jnp.concatenate([column] * (width // LANES), axis=1)
    spread = lambda values, k: jnp.broadcast_to(values[k : k + 1, :], (8, values.shape[1]))
    column = lambda g, j: jnp.broadcast_to(groups[g][:, lane + j : lane + j + 1], (8, LANES))
    sub = iota((8, LANES), 0)
    cols = {(j, g): column(g, j) for g in (at, at + 1) for j in range(8 * (g - at) + 8)}
    for g in (at, at + 1):
        cols[0, g] = cols[0, g] + none
    for k in range(16):
        home, k_sub = at + k // 8, k % 8
        for g in range(at + 2, count):
            step = NEAR if g < at + 4 else FAR
            if k % step == 0:
                for j in range(k, k + step):
                    cols[j, g] = column(g, j)
        scale = lax.rsqrt(spread(cols[k, home], k_sub))
        square = scale * scale
        scale_ref[8 * home + k_sub : 8 * home + k_sub + 1, :] = scale[k_sub : k_sub + 1, :]
        share = {g: cols[k, g] * square for g in range(home, count)}
        share[home] = jnp.where(sub > k_sub, share[home], 0.0)
        for j in range(k + 1, 16):
            j_home, j_sub = at + j // 8, j % 8
            head = spread(cols[k, j_home], j_sub)
            for g in range(j_home, count):
                step = 16 if g < at + 2 else NEAR if g < at + 4 else FAR
                if j // step == k // step:
                    if j == k + 1 and g == j_home:
                        cols[j, g] = cols[j, g] - (cols[k, g] * head) * square
                    else:
                        cols[j, g] = cols[j, g] - share[g] * head
        row = spread(groups[home], k_sub)
        for g in range(home, count):
            groups[g] = groups[g] - wide(share[g]) * row
    for g in (at, at + 1):
        groups[g] = groups[g] * wide(scale_ref[8 * g : 8 * g + 8, :])
    return groups


def factor_kernel(
    place_ref, kept_ref, other_ref, window_ref, factor_hbm, basis_hbm,
    left_ref, inverse_ref, upper_ref, factor_ref, basis_ref, scale_ref, sems,
):
    first = place_ref[0] == 0
    none = jnp.full((8, LANES), jnp.minimum(place_ref[0], 0).astype(F32))
    size = left_ref.shape[0]
    row, col = iota((LANES, LANES), 0), iota((LANES, LANES), 1)
    packed = jnp.where(first, kept_ref[:LANES], other_ref[:LANES])
    across = jnp.where(first, other_ref[:LANES], kept_ref[:LANES])
    corner = jnp.where(first, kept_ref[LANES : LANES + 1], other_ref[LANES : LANES + 1])
    turned = packed.T
    left_ref[:LANES, :LANES] = jnp.where(row >= col, packed, turned)
    left_ref[:LANES, LANES:] = across
    left_ref[LANES:, :LANES] = jnp.zeros((LANES, LANES), F32)
    left_ref[LANES:, LANES:] = jnp.where(
        row == col, jnp.broadcast_to(corner, (LANES, LANES)), jnp.where(row > col, turned, packed)
    )
    inverse_ref[...] = jnp.where(iota((size, size), 0) == iota((size, size), 1), 1.0, 0.0)
    upper_ref[...] = jnp.zeros((size, size), F32)
    copies = []

    def send(source, target, begin, end):
        copies.append(pltpu.make_async_copy(source.at[begin:end], target.at[begin:end], sems.at[len(copies)]))
        copies[-1].start()

    for begin in range(0, size, PANEL):
        end = begin + PANEL
        skip = 0 if begin < LANES else LANES
        reach = LANES if end <= LANES else size
        groups = [
            jnp.concatenate([left_ref[g : g + 8, skip:], inverse_ref[g : g + 8, :reach]], axis=1)
            for g in range(begin, end, 8)
        ]
        for g in range(0, PANEL // 8, 2):
            groups = eliminate(groups, g, begin + 8 * g - skip, none, scale_ref)
        panel = jnp.concatenate(groups, axis=0)
        upper_ref[begin:end, skip:] = panel[:, : size - skip]
        if end < size:
            high, middle, low = split3(panel)
            right = jnp.concatenate([high, middle, high, low, high, middle], axis=0)
            lost = LANES if end == LANES else skip
            turned = panel[:, lost - skip : size - skip]
            turned = jnp.concatenate([turned, turned], axis=0).T[end - lost :, :]
            high = turned.astype(BF16).astype(F32)
            rest = turned - high
            middle = rest.astype(BF16).astype(F32)
            low = rest - middle
            early = iota(turned.shape, 1) < PANEL
            left = jnp.concatenate(
                [high, jnp.where(early, middle, high), jnp.where(early, low, middle)], axis=1
            ).astype(BF16)
            apart = lost - skip
            near = jnp.dot(left[:PANEL], right[:, apart : size - skip], preferred_element_type=F32)
            left_ref[end : end + PANEL, lost:] = left_ref[end : end + PANEL, lost:] - near
            near = jnp.dot(left[:PANEL], right[:, size - skip :], preferred_element_type=F32)
            inverse_ref[end : end + PANEL, :reach] = inverse_ref[end : end + PANEL, :reach] - near
            if end + PANEL < size:
                far = jnp.dot(left[PANEL:], right[:, apart:], preferred_element_type=F32)
                left_ref[end + PANEL :, lost:] = left_ref[end + PANEL :, lost:] - far[:, : size - lost]
                inverse_ref[end + PANEL :, :reach] = inverse_ref[end + PANEL :, :reach] - far[:, size - lost :]
        inverse = panel[:, size - skip :]
        inverse = jnp.where(iota(inverse.shape, 0) + begin >= iota(inverse.shape, 1), inverse, 0.0)
        high, low = split2(inverse)
        cells = window_ref[:reach, :]
        basis_ref[begin:end, :] = jnp.dot(
            jnp.concatenate([high, low], axis=1), jnp.concatenate([cells, cells], axis=0), preferred_element_type=F32
        )
        send(basis_ref, basis_hbm, begin, end)
        if end == LANES:
            factor_ref[:LANES, :LANES] = jnp.where(row >= col, upper_ref[:LANES, :LANES].T, 0.0)
            factor_ref[:LANES, LANES:] = jnp.zeros((LANES, LANES), F32)
            factor_ref[LANES:, :LANES] = upper_ref[:LANES, LANES:].T
            send(factor_ref, factor_hbm, 0, LANES)
    factor_ref[LANES:, LANES:] = jnp.where(row >= col, upper_ref[LANES:, LANES:].T, 0.0)
    send(factor_ref, factor_hbm, LANES, size)
    for copy in copies:
        copy.wait()


def factorise(place, kept, other, window):
    size, rows_dev = window.shape
    return pl.pallas_call(
        factor_kernel,
        out_shape=[shaped((size, size)), shaped((size, rows_dev))],
        in_specs=[SMEM] + [VMEM] * 3,
        out_specs=[pl.BlockSpec(memory_space=pl.ANY)] * 2,
        scratch_shapes=[pltpu.VMEM((size, size), F32)] * 4
        + [pltpu.VMEM((size, rows_dev), F32), pltpu.VMEM((PANEL, LANES), F32), pltpu.SemaphoreType.DMA((size // PANEL + 2,))],
        compiler_params=LIMIT,
        name="factor",
    )(place, kept, other, window)


VMEM = pl.BlockSpec(memory_space=pltpu.VMEM)
SMEM = pl.BlockSpec(memory_space=pltpu.SMEM)
LIMIT = pltpu.CompilerParams(vmem_limit_bytes=48 * 2**20)


def shaped(shape, dtype=F32):
    return jax.ShapeDtypeStruct(shape, dtype)


def swap(values, axis, bit):
    count = lax.axis_size(axis)
    return lax.ppermute(values, axis, [(i, i ^ bit) for i in range(count)])


def shift(values, axis, step):
    count = lax.axis_size(axis)
    return lax.ppermute(values, axis, [(i, i + step) for i in range(count) if 0 <= i + step < count])


def sum_over_span(values):
    count = lax.axis_size("span")
    if count & (count - 1):
        return lax.psum(values, "span")
    bit = 1
    while bit < count:
        values = values + swap(values, "span", bit)
        bit *= 2
    return values


def local(fine_field, stored, filter_taps):
    snapshots, comps, cells_y, cells_z, cells_x = fine_field.shape
    assert (snapshots, comps, cells_y, cells_z, cells_x) == (8, 3, 16, 16, 128)
    assert lax.axis_size("sect") == 2
    old, rows_dev = stored.shape
    size = old + snapshots
    total = rows_dev * lax.axis_size("span") * lax.axis_size("sect")
    place = lax.axis_index("sect").astype(jnp.int32).reshape(1)
    fields = snapshots * comps
    own, ext, send = pl.pallas_call(
        filter_kernel,
        out_shape=[shaped((12, 8, LANES))] * 3,
        in_specs=[SMEM, VMEM, SMEM],
        out_specs=[VMEM] * 3,
        scratch_shapes=[pltpu.VMEM((8, 8 * fields, LANES), F32), pltpu.VMEM((2, 8 * fields, LANES), F32)],
        compiler_params=LIMIT,
        name="filter",
    )(place, fine_field.reshape(fields, cells_y * cells_z, cells_x), filter_taps)
    partner = swap(send, "sect", 1)
    own_share, ext_share = partner[:6], partner[6:].reshape(3, 2, 8, LANES)
    none = jnp.zeros_like(ext_share)
    ext_share = jnp.where(
        place[0] == 0,
        jnp.concatenate([none, ext_share], axis=1),
        jnp.concatenate([ext_share, none], axis=1),
    )
    ext = ext + ext_share.reshape(12, 8, LANES)
    from_left = shift(ext, "span", 1)
    from_right = shift(ext, "span", -1)
    coarse_new, window, kept, sent = pl.pallas_call(
        functools.partial(gram_kernel, total),
        out_shape=[
            shaped((snapshots, rows_dev), BF16),
            shaped((size, rows_dev), BF16),
            shaped((LANES + 8, LANES)),
            shaped((LANES + 8, LANES)),
        ],
        in_specs=[SMEM] + [VMEM] * 5,
        out_specs=[VMEM] * 4,
        compiler_params=LIMIT,
        name="gram",
    )(place, stored, own, own_share, from_left, from_right)
    kept = sum_over_span(kept + swap(sent, "sect", 1))
    other = swap(kept, "sect", 1)
    factor, basis = factorise(place, kept, other, window)
    return (coarse_new, factor, basis)


def solution(mesh):
    in_specs = (P("case", None, "sect", "span", None), P(None, ("case", "span", "sect")), P())
    out_specs = (
        P(None, ("case", "span", "sect")),
        P("case", None),
        P(None, ("case", "span", "sect")),
    )
    return jax.shard_map(local, mesh=mesh, in_specs=in_specs, out_specs=out_specs, check_vma=False)
```

```python
import functools

import jax
import jax.numpy as jnp
from jax import lax
from jax.experimental import pallas as pl
from jax.experimental.pallas import tpu as pltpu
from jax.sharding import PartitionSpec as P

F32 = jnp.float32
BF16 = jnp.bfloat16
TAPS = 17
LANES = 128
PANEL = 64
NEAR = 8
FAR = 8
PARTS = 6
HALF = LANES + 8


def iota(shape, dim):
    return lax.broadcasted_iota(jnp.int32, shape, dim)


def split2(values):
    high = values.astype(BF16)
    return high, (values - high.astype(F32)).astype(BF16)


def split3(values):
    high = values.astype(BF16)
    rest = values - high.astype(F32)
    middle = rest.astype(BF16)
    return high, middle, (rest - middle.astype(F32)).astype(BF16)


def weights_at(offset, taps_ref, row):
    total = jnp.zeros(offset.shape, F32)
    for tap in range(TAPS):
        total = jnp.where(offset == tap, taps_ref[row, tap], total)
    return total


def filter_kernel(
    place_ref, fine_hbm, taps_hbm, own_ref, ext_ref, fine_ref, taps_ref, plane_ref, row_ref, sems
):
    fields = fine_ref.shape[0]
    part = fields // PARTS
    taps_copy = pltpu.make_async_copy(taps_hbm, taps_ref, sems.at[PARTS])
    taps_copy.start()
    copies = [
        pltpu.make_async_copy(fine_hbm.at[p * part : (p + 1) * part], fine_ref.at[p * part : (p + 1) * part], sems.at[p])
        for p in range(PARTS)
    ]
    for copy in copies:
        copy.start()
    first = place_ref[0] == 0
    slot, cell = iota((64, 256), 0), iota((64, 256), 1)
    span_slot, sect_slot = slot // 8, slot % 8
    span_cell = jnp.where(span_slot < 6, span_slot, span_slot - 8)
    sect_cell = jnp.where((sect_slot < 4) | first, sect_slot, sect_slot - 6)
    span_tap = cell % 16 - 4 * span_cell + 8
    sect_tap = jnp.where(sect_slot < 6, cell // 16 - 4 * sect_cell + 8, -1)
    taps_copy.wait()
    plane = weights_at(span_tap, taps_ref, 1) * weights_at(sect_tap, taps_ref, 0)
    plane = jnp.concatenate(split2(plane), axis=0)
    cell, lane = iota((LANES, LANES), 0), iota((LANES, LANES), 1)
    stream = weights_at(cell - 4 * (lane % 32) + 8, taps_ref, 2)
    parts = [
        jnp.concatenate([jnp.where(lane // 32 == s, term, 0.0) for s in range(4)], axis=0).astype(BF16)
        for term in (stream.astype(BF16).astype(F32), stream - stream.astype(BF16).astype(F32))
    ]
    matrix = jnp.concatenate([parts[0], parts[0], parts[1]], axis=0)
    for p in range(PARTS):
        copies[p].wait()
        for field in range(p * part, (p + 1) * part):
            both = jnp.dot(plane, fine_ref[field], preferred_element_type=F32)
            summed = both[:64] + both[64:]
            for s in range(8):
                plane_ref[s, 8 * field : 8 * field + 8, :] = summed[8 * s : 8 * s + 8]
    for half, out_ref in enumerate((own_ref, ext_ref)):
        values = jnp.concatenate([plane_ref[4 * half + s] for s in range(4)], axis=1)
        high, low = split2(values)
        row_ref[half] = jnp.dot(
            jnp.concatenate([high, low, high], axis=1), matrix, preferred_element_type=F32
        )
        for comp in range(3):
            for k in range(6):
                out_ref[comp, k] = row_ref[half, pl.ds(8 * comp + k, 8, stride=24), :]


def fold(gram, kept_ref, sent_ref, first):
    row, col = iota((LANES, LANES), 0), iota((LANES, LANES), 1)
    across, lower = gram[LANES:, :LANES], gram[LANES:, LANES:]
    packed = jnp.where(row <= col, gram[:LANES, :LANES], lower)
    corner = jnp.sum(jnp.where(row == col, lower, 0.0), axis=0, keepdims=True)
    corner = jnp.broadcast_to(corner, (8, LANES))
    kept_ref[:LANES] = jnp.where(first, packed, across)
    kept_ref[LANES:] = corner
    sent_ref[:LANES] = jnp.where(first, across, packed)
    sent_ref[LANES:] = corner


def old_kernel(total, place_ref, stored_ref, after_ref, kept_ref, sent_ref):
    old, cells = stored_ref.shape
    rows = jnp.concatenate([stored_ref[...], jnp.zeros((8, cells), BF16)], axis=0)
    gram = lax.dot_general(rows, rows, (((1,), (1,)), ((), ())), preferred_element_type=F32) / total
    fold(gram, kept_ref, sent_ref, place_ref[0] == 0)


def new_kernel(
    total, place_ref, stored_ref, own_ref, left_ref, right_ref, partner_ref, kept_ref, coarse_ref, sums_ref
):
    first = place_ref[0] == 0
    half = kept_ref.shape[0]
    lane = iota((8, LANES), 1)
    cells = []
    for comp in range(3):
        for k in range(4):
            value = own_ref[comp, k] + jnp.where(lane < 64, left_ref[comp, k], right_ref[comp, k])
            here = first if k >= 2 else jnp.logical_not(first)
            at = half + 8 * (2 * comp + k % 2)
            cells.append(value + jnp.where(here, partner_ref[at : at + 8, :], 0.0))
    coarse = jnp.concatenate(cells, axis=1).astype(BF16)
    coarse_ref[...] = coarse
    rows = jnp.concatenate([stored_ref[...], coarse], axis=0)
    gram = lax.dot_general(coarse, rows, (((1,), (1,)), ((), ())), preferred_element_type=F32) / total
    sums_ref[:half] = kept_ref[...] + partner_ref[:half, :]
    sums_ref[half : half + 8] = gram[:, :LANES]
    sums_ref[half + 8 :] = gram[:, LANES:]


def eliminate(groups, at, lane, none, scale_ref):
    count = len(groups)
    width = groups[at].shape[1]
    wide = lambda column: jnp.concatenate([column] * (width // LANES), axis=1)
    spread = lambda values, k: jnp.broadcast_to(values[k : k + 1, :], (8, values.shape[1]))
    column = lambda g, j: jnp.broadcast_to(groups[g][:, lane + j : lane + j + 1], (8, LANES))
    sub = iota((8, LANES), 0)
    cols = {(j, g): column(g, j) for g in (at, at + 1) for j in range(8 * (g - at) + 8)}
    for g in (at, at + 1):
        cols[0, g] = cols[0, g] + none
    for k in range(16):
        home, k_sub = at + k // 8, k % 8
        for g in range(at + 2, count):
            step = NEAR if g < at + 4 else FAR
            if k % step == 0:
                for j in range(k, k + step):
                    cols[j, g] = column(g, j)
        scale = lax.rsqrt(spread(cols[k, home], k_sub))
        square = scale * scale
        scale_ref[8 * home + k_sub : 8 * home + k_sub + 1, :] = scale[k_sub : k_sub + 1, :]
        share = {g: cols[k, g] * square for g in range(home, count)}
        share[home] = jnp.where(sub > k_sub, share[home], 0.0)
        for j in range(k + 1, 16):
            j_home, j_sub = at + j // 8, j % 8
            head = spread(cols[k, j_home], j_sub)
            for g in range(j_home, count):
                step = 16 if g < at + 2 else NEAR if g < at + 4 else FAR
                if j // step == k // step:
                    if j == k + 1 and g == j_home:
                        cols[j, g] = cols[j, g] - (cols[k, g] * head) * square
                    else:
                        cols[j, g] = cols[j, g] - share[g] * head
        row = spread(groups[home], k_sub)
        for g in range(home, count):
            groups[g] = groups[g] - wide(share[g]) * row
    for g in (at, at + 1):
        groups[g] = groups[g] * wide(scale_ref[8 * g : 8 * g + 8, :])
    return groups


def factor_kernel(
    place_ref, mine_ref, other_ref, stored_ref, coarse_ref, factor_hbm, basis_hbm,
    left_ref, inverse_ref, upper_ref, factor_ref, basis_ref, scale_ref, window_ref, sems,
):
    first = place_ref[0] == 0
    none = jnp.full((8, LANES), jnp.minimum(place_ref[0], 0).astype(F32))
    size = left_ref.shape[0]
    row, col = iota((LANES, LANES), 0), iota((LANES, LANES), 1)
    packed = jnp.where(first, mine_ref[:LANES], other_ref[:LANES])
    across = jnp.where(first, other_ref[:LANES], mine_ref[:LANES])
    corner = jnp.where(first, mine_ref[LANES : LANES + 1], other_ref[LANES : LANES + 1])
    added = mine_ref[HALF : HALF + 8] + other_ref[HALF : HALF + 8]
    across = jnp.concatenate([across[:-8], across[-8:] + added], axis=0)
    added = mine_ref[HALF + 8 :] + other_ref[HALF + 8 :]
    added = jnp.concatenate([jnp.zeros((LANES - 8, LANES), F32), added], axis=0)
    corner = corner + jnp.sum(jnp.where(row == col, added, 0.0), axis=0, keepdims=True)
    packed = packed + jnp.where(row > col, added, 0.0)
    turned = packed.T
    window_ref[: size - 8, :] = stored_ref[...]
    window_ref[size - 8 :, :] = coarse_ref[...]
    left_ref[:LANES, :LANES] = jnp.where(row <= col, packed, turned)
    left_ref[:LANES, LANES:] = across.T
    left_ref[LANES:, :LANES] = jnp.zeros((LANES, LANES), F32)
    left_ref[LANES:, LANES:] = jnp.where(
        row == col, jnp.broadcast_to(corner, (LANES, LANES)), jnp.where(row < col, turned, packed)
    )
    inverse_ref[...] = jnp.where(iota((size, size), 0) == iota((size, size), 1), 1.0, 0.0)
    upper_ref[...] = jnp.zeros((size, size), F32)
    copies = []

    def send(source, target, begin, end):
        copies.append(pltpu.make_async_copy(source.at[begin:end], target.at[begin:end], sems.at[len(copies)]))
        copies[-1].start()

    for begin in range(0, size, PANEL):
        end = begin + PANEL
        skip = 0 if begin < LANES else LANES
        reach = LANES if end <= LANES else size
        groups = [
            jnp.concatenate([left_ref[g : g + 8, skip:], inverse_ref[g : g + 8, :reach]], axis=1)
            for g in range(begin, end, 8)
        ]
        for g in range(0, PANEL // 8, 2):
            groups = eliminate(groups, g, begin + 8 * g - skip, none, scale_ref)
        panel = jnp.concatenate(groups, axis=0)
        upper_ref[begin:end, skip:] = panel[:, : size - skip]
        if end < size:
            high, middle, low = split3(panel)
            right = jnp.concatenate([high, middle, high, low, high, middle], axis=0)
            lost = LANES if end == LANES else skip
            turned = panel[:, lost - skip : size - skip]
            turned = jnp.concatenate([turned, turned], axis=0).T[end - lost :, :]
            high = turned.astype(BF16).astype(F32)
            rest = turned - high
            middle = rest.astype(BF16).astype(F32)
            low = rest - middle
            early = iota(turned.shape, 1) < PANEL
            left = jnp.concatenate(
                [high, jnp.where(early, middle, high), jnp.where(early, low, middle)], axis=1
            ).astype(BF16)
            apart = lost - skip
            near = jnp.dot(left[:PANEL], right[:, apart : size - skip], preferred_element_type=F32)
            left_ref[end : end + PANEL, lost:] = left_ref[end : end + PANEL, lost:] - near
            near = jnp.dot(left[:PANEL], right[:, size - skip :], preferred_element_type=F32)
            inverse_ref[end : end + PANEL, :reach] = inverse_ref[end : end + PANEL, :reach] - near
            if end + PANEL < size:
                far = jnp.dot(left[PANEL:], right[:, apart:], preferred_element_type=F32)
                left_ref[end + PANEL :, lost:] = left_ref[end + PANEL :, lost:] - far[:, : size - lost]
                inverse_ref[end + PANEL :, :reach] = inverse_ref[end + PANEL :, :reach] - far[:, size - lost :]
        inverse = panel[:, size - skip :]
        inverse = jnp.where(iota(inverse.shape, 0) + begin >= iota(inverse.shape, 1), inverse, 0.0)
        high, low = split2(inverse)
        cells = window_ref[:reach, :]
        basis_ref[begin:end, :] = jnp.dot(
            jnp.concatenate([high, low], axis=1), jnp.concatenate([cells, cells], axis=0), preferred_element_type=F32
        )
        send(basis_ref, basis_hbm, begin, end)
        if end == LANES:
            factor_ref[:LANES, :LANES] = jnp.where(row >= col, upper_ref[:LANES, :LANES].T, 0.0)
            factor_ref[:LANES, LANES:] = jnp.zeros((LANES, LANES), F32)
            factor_ref[LANES:, :LANES] = upper_ref[:LANES, LANES:].T
            send(factor_ref, factor_hbm, 0, LANES)
    factor_ref[LANES:, LANES:] = jnp.where(row >= col, upper_ref[LANES:, LANES:].T, 0.0)
    send(factor_ref, factor_hbm, LANES, size)
    for copy in copies:
        copy.wait()


def factorise(place, mine, other, stored, coarse):
    old, rows_dev = stored.shape
    size = old + coarse.shape[0]
    return pl.pallas_call(
        factor_kernel,
        out_shape=[shaped((size, size)), shaped((size, rows_dev))],
        in_specs=[SMEM] + [VMEM] * 4,
        out_specs=[ANY] * 2,
        scratch_shapes=[pltpu.VMEM((size, size), F32)] * 4
        + [
            pltpu.VMEM((size, rows_dev), F32),
            pltpu.VMEM((PANEL, LANES), F32),
            pltpu.VMEM((size, rows_dev), BF16),
            pltpu.SemaphoreType.DMA((size // PANEL + 2,)),
        ],
        compiler_params=LIMIT,
        name="factor",
    )(place, mine, other, stored, coarse)


VMEM = pl.BlockSpec(memory_space=pltpu.VMEM)
ANY = pl.BlockSpec(memory_space=pl.ANY)
SMEM = pl.BlockSpec(memory_space=pltpu.SMEM)
LIMIT = pltpu.CompilerParams(vmem_limit_bytes=48 * 2**20)


def shaped(shape, dtype=F32):
    return jax.ShapeDtypeStruct(shape, dtype)


def swap(values, axis, bit):
    count = lax.axis_size(axis)
    return lax.ppermute(values, axis, [(i, i ^ bit) for i in range(count)])


def shift(values, axis, step):
    count = lax.axis_size(axis)
    return lax.ppermute(values, axis, [(i, i + step) for i in range(count) if 0 <= i + step < count])


def sum_over_span(values):
    count = lax.axis_size("span")
    if count & (count - 1):
        return lax.psum(values, "span")
    bit = 1
    while bit < count:
        values = values + swap(values, "span", bit)
        bit *= 2
    return values


def local(fine_field, stored, filter_taps):
    snapshots, comps, cells_y, cells_z, cells_x = fine_field.shape
    assert (snapshots, comps, cells_y, cells_z, cells_x) == (8, 3, 16, 16, 128)
    assert lax.axis_size("sect") == 2
    old, rows_dev = stored.shape
    total = rows_dev * lax.axis_size("span") * lax.axis_size("sect")
    place = lax.axis_index("sect").astype(jnp.int32).reshape(1)
    fields = snapshots * comps
    own, ext = pl.pallas_call(
        filter_kernel,
        out_shape=[shaped((comps, 6, snapshots, LANES))] * 2,
        in_specs=[SMEM, ANY, ANY],
        out_specs=[VMEM] * 2,
        scratch_shapes=[
            pltpu.VMEM((fields, cells_y * cells_z, cells_x), BF16),
            pltpu.SMEM(filter_taps.shape, F32),
            pltpu.VMEM((8, 8 * fields, LANES), F32),
            pltpu.VMEM((2, 8 * fields, LANES), F32),
            pltpu.SemaphoreType.DMA((PARTS + 1,)),
        ],
        compiler_params=LIMIT,
        name="filter",
    )(place, fine_field.reshape(fields, cells_y * cells_z, cells_x), filter_taps)
    left = shift(ext, "span", 1)
    right = shift(ext, "span", -1)
    kept, sent = pl.pallas_call(
        functools.partial(old_kernel, total),
        out_shape=[shaped((HALF, LANES))] * 2,
        in_specs=[SMEM, VMEM, VMEM],
        out_specs=[VMEM] * 2,
        compiler_params=LIMIT,
        name="gram_stored",
    )(place, stored, own)
    lanes = lax.broadcasted_iota(jnp.int32, (1, 1, 1, LANES), 3)
    halo = own[:, 4:] + jnp.where(lanes < 64, left[:, 4:], right[:, 4:])
    partner = swap(jnp.concatenate([sent, halo.reshape(-1, LANES)], axis=0), "sect", 1)
    coarse_new, sums = pl.pallas_call(
        functools.partial(new_kernel, total),
        out_shape=[shaped((snapshots, rows_dev), BF16), shaped((HALF + 2 * snapshots, LANES))],
        in_specs=[SMEM] + [VMEM] * 6,
        out_specs=[VMEM] * 2,
        compiler_params=LIMIT,
        name="gram_new",
    )(place, stored, own, left, right, partner, kept)
    sums = sum_over_span(sums)
    factor, basis = factorise(place, sums, swap(sums, "sect", 1), stored, coarse_new)
    return (coarse_new, factor, basis)


def solution(mesh):
    in_specs = (P("case", None, "sect", "span", None), P(None, ("case", "span", "sect")), P())
    out_specs = (
        P(None, ("case", "span", "sect")),
        P("case", None),
        P(None, ("case", "span", "sect")),
    )
    return jax.shard_map(local, mesh=mesh, in_specs=in_specs, out_specs=out_specs, check_vma=False)
```

```python
import functools

import jax
import jax.numpy as jnp
from jax import lax
from jax.experimental import pallas as pl
from jax.experimental.pallas import tpu as pltpu
from jax.sharding import PartitionSpec as P

F32 = jnp.float32
BF16 = jnp.bfloat16
TAPS = 17
LANES = 128
PANEL = 64
NEAR = 8
FAR = 8
PARTS = 6
HALF = LANES + 8


def iota(shape, dim):
    return lax.broadcasted_iota(jnp.int32, shape, dim)


def split2(values):
    high = values.astype(BF16)
    return high, (values - high.astype(F32)).astype(BF16)


def split3(values):
    high = values.astype(BF16)
    rest = values - high.astype(F32)
    middle = rest.astype(BF16)
    return high, middle, (rest - middle.astype(F32)).astype(BF16)


def weights_at(offset, taps_ref, row):
    total = jnp.zeros(offset.shape, F32)
    for tap in range(TAPS):
        total = jnp.where(offset == tap, taps_ref[row, tap], total)
    return total


def filter_kernel(
    place_ref, fine_hbm, taps_hbm, own_ref, ext_ref, fine_ref, taps_ref, plane_ref, row_ref, sems
):
    fields = fine_ref.shape[0]
    part = fields // PARTS
    taps_copy = pltpu.make_async_copy(taps_hbm, taps_ref, sems.at[PARTS])
    taps_copy.start()
    copies = [
        pltpu.make_async_copy(fine_hbm.at[p * part : (p + 1) * part], fine_ref.at[p * part : (p + 1) * part], sems.at[p])
        for p in range(PARTS)
    ]
    for copy in copies:
        copy.start()
    first = place_ref[0] == 0
    slot, cell = iota((64, 256), 0), iota((64, 256), 1)
    span_slot, sect_slot = slot // 8, slot % 8
    span_cell = jnp.where(span_slot < 6, span_slot, span_slot - 8)
    sect_cell = jnp.where((sect_slot < 4) | first, sect_slot, sect_slot - 6)
    span_tap = cell % 16 - 4 * span_cell + 8
    sect_tap = jnp.where(sect_slot < 6, cell // 16 - 4 * sect_cell + 8, -1)
    taps_copy.wait()
    plane = weights_at(span_tap, taps_ref, 1) * weights_at(sect_tap, taps_ref, 0)
    plane = jnp.concatenate(split2(plane), axis=0)
    cell, lane = iota((LANES, LANES), 0), iota((LANES, LANES), 1)
    stream = weights_at(cell - 4 * (lane % 32) + 8, taps_ref, 2)
    parts = [
        jnp.concatenate([jnp.where(lane // 32 == s, term, 0.0) for s in range(4)], axis=0).astype(BF16)
        for term in (stream.astype(BF16).astype(F32), stream - stream.astype(BF16).astype(F32))
    ]
    matrix = jnp.concatenate([parts[0], parts[0], parts[1]], axis=0)
    for p in range(PARTS):
        copies[p].wait()
        for field in range(p * part, (p + 1) * part):
            both = jnp.dot(plane, fine_ref[field], preferred_element_type=F32)
            summed = both[:64] + both[64:]
            for s in range(8):
                plane_ref[s, 8 * field : 8 * field + 8, :] = summed[8 * s : 8 * s + 8]
    for half, out_ref in enumerate((own_ref, ext_ref)):
        values = jnp.concatenate([plane_ref[4 * half + s] for s in range(4)], axis=1)
        high, low = split2(values)
        row_ref[half] = jnp.dot(
            jnp.concatenate([high, low, high], axis=1), matrix, preferred_element_type=F32
        )
        for comp in range(3):
            for k in range(6):
                out_ref[comp, k] = row_ref[half, pl.ds(8 * comp + k, 8, stride=24), :]


def fold(gram, kept_ref, sent_ref, first):
    row, col = iota((LANES, LANES), 0), iota((LANES, LANES), 1)
    across, lower = gram[LANES:, :LANES], gram[LANES:, LANES:]
    packed = jnp.where(row <= col, gram[:LANES, :LANES], lower)
    corner = jnp.sum(jnp.where(row == col, lower, 0.0), axis=0, keepdims=True)
    corner = jnp.broadcast_to(corner, (8, LANES))
    kept_ref[:LANES] = jnp.where(first, packed, across)
    kept_ref[LANES:] = corner
    sent_ref[:LANES] = jnp.where(first, across, packed)
    sent_ref[LANES:] = corner


def old_kernel(total, place_ref, stored_ref, after_ref, kept_ref, sent_ref):
    old, cells = stored_ref.shape
    rows = jnp.concatenate([stored_ref[...], jnp.zeros((8, cells), BF16)], axis=0)
    gram = lax.dot_general(rows, rows, (((1,), (1,)), ((), ())), preferred_element_type=F32) / total
    fold(gram, kept_ref, sent_ref, place_ref[0] == 0)


def new_kernel(
    total, place_ref, stored_ref, own_ref, left_ref, right_ref, partner_ref, kept_ref, coarse_ref, sums_ref
):
    first = place_ref[0] == 0
    half = kept_ref.shape[0]
    lane = iota((8, LANES), 1)
    cells = []
    for comp in range(3):
        for k in range(4):
            value = own_ref[comp, k] + jnp.where(lane < 64, left_ref[comp, k], right_ref[comp, k])
            here = first if k >= 2 else jnp.logical_not(first)
            at = half + 8 * (2 * comp + k % 2)
            cells.append(value + jnp.where(here, partner_ref[at : at + 8, :], 0.0))
    coarse = jnp.concatenate(cells, axis=1).astype(BF16)
    coarse_ref[...] = coarse
    rows = jnp.concatenate([stored_ref[...], coarse], axis=0)
    gram = lax.dot_general(coarse, rows, (((1,), (1,)), ((), ())), preferred_element_type=F32) / total
    sums_ref[:half] = kept_ref[...] + partner_ref[:half, :]
    sums_ref[half : half + 8] = gram[:, :LANES]
    sums_ref[half + 8 :] = gram[:, LANES:]


def eliminate(groups, at, lane, none, scale_ref):
    count = len(groups)
    width = groups[at].shape[1]
    wide = lambda column: jnp.concatenate([column] * (width // LANES), axis=1)
    spread = lambda values, k: jnp.broadcast_to(values[k : k + 1, :], (8, values.shape[1]))
    column = lambda g, j: jnp.broadcast_to(groups[g][:, lane + j : lane + j + 1], (8, LANES))
    sub = iota((8, LANES), 0)
    cols = {(j, g): column(g, j) for g in (at, at + 1) for j in range(8 * (g - at) + 8)}
    for g in (at, at + 1):
        cols[0, g] = cols[0, g] + none
    for k in range(16):
        home, k_sub = at + k // 8, k % 8
        for g in range(at + 2, count):
            step = NEAR if g < at + 4 else FAR
            if k % step == 0:
                for j in range(k, k + step):
                    cols[j, g] = column(g, j)
        scale = lax.rsqrt(spread(cols[k, home], k_sub))
        square = scale * scale
        scale_ref[8 * home + k_sub : 8 * home + k_sub + 1, :] = scale[k_sub : k_sub + 1, :]
        share = {g: cols[k, g] * square for g in range(home, count)}
        share[home] = jnp.where(sub > k_sub, share[home], 0.0)
        for j in range(k + 1, 16):
            j_home, j_sub = at + j // 8, j % 8
            head = spread(cols[k, j_home], j_sub)
            for g in range(j_home, count):
                step = 16 if g < at + 2 else NEAR if g < at + 4 else FAR
                if j // step == k // step:
                    if j == k + 1 and g == j_home:
                        cols[j, g] = cols[j, g] - (cols[k, g] * head) * square
                    else:
                        cols[j, g] = cols[j, g] - share[g] * head
        row = spread(groups[home], k_sub)
        for g in range(home, count):
            groups[g] = groups[g] - wide(share[g]) * row
    for g in (at, at + 1):
        groups[g] = groups[g] * wide(scale_ref[8 * g : 8 * g + 8, :])
    return groups


def factor_kernel(
    place_ref, mine_ref, other_ref, stored_ref, coarse_ref, new_hbm, factor_hbm, basis_hbm,
    left_ref, inverse_ref, upper_ref, factor_ref, basis_ref, scale_ref, window_ref, sems,
):
    first = place_ref[0] == 0
    none = jnp.full((8, LANES), jnp.minimum(place_ref[0], 0).astype(F32))
    size = left_ref.shape[0]
    row, col = iota((LANES, LANES), 0), iota((LANES, LANES), 1)
    packed = jnp.where(first, mine_ref[:LANES], other_ref[:LANES])
    across = jnp.where(first, other_ref[:LANES], mine_ref[:LANES])
    corner = jnp.where(first, mine_ref[LANES : LANES + 1], other_ref[LANES : LANES + 1])
    added = mine_ref[HALF : HALF + 8] + other_ref[HALF : HALF + 8]
    across = jnp.concatenate([across[:-8], across[-8:] + added], axis=0)
    added = mine_ref[HALF + 8 :] + other_ref[HALF + 8 :]
    added = jnp.concatenate([jnp.zeros((LANES - 8, LANES), F32), added], axis=0)
    corner = corner + jnp.sum(jnp.where(row == col, added, 0.0), axis=0, keepdims=True)
    packed = packed + jnp.where(row > col, added, 0.0)
    turned = packed.T
    copies = [pltpu.make_async_copy(coarse_ref, new_hbm, sems.at[0])]
    copies[0].start()
    window_ref[: size - 8, :] = stored_ref[...]
    window_ref[size - 8 :, :] = coarse_ref[...]
    left_ref[:LANES, :LANES] = jnp.where(row <= col, packed, turned)
    left_ref[:LANES, LANES:] = across.T
    left_ref[LANES:, :LANES] = jnp.zeros((LANES, LANES), F32)
    left_ref[LANES:, LANES:] = jnp.where(
        row == col, jnp.broadcast_to(corner, (LANES, LANES)), jnp.where(row < col, turned, packed)
    )
    inverse_ref[...] = jnp.where(iota((size, size), 0) == iota((size, size), 1), 1.0, 0.0)
    upper_ref[...] = jnp.zeros((size, size), F32)

    def send(source, target, begin, end):
        copies.append(pltpu.make_async_copy(source.at[begin:end], target.at[begin:end], sems.at[len(copies)]))
        copies[-1].start()

    for begin in range(0, size, PANEL):
        end = begin + PANEL
        skip = 0 if begin < LANES else LANES
        reach = LANES if end <= LANES else size
        groups = [
            jnp.concatenate([left_ref[g : g + 8, skip:], inverse_ref[g : g + 8, :reach]], axis=1)
            for g in range(begin, end, 8)
        ]
        for g in range(0, PANEL // 8, 2):
            groups = eliminate(groups, g, begin + 8 * g - skip, none, scale_ref)
        panel = jnp.concatenate(groups, axis=0)
        upper_ref[begin:end, skip:] = panel[:, : size - skip]
        if end < size:
            high, middle, low = split3(panel)
            right = jnp.concatenate([high, middle, high, low, high, middle], axis=0)
            lost = LANES if end == LANES else skip
            turned = panel[:, lost - skip : size - skip]
            turned = jnp.concatenate([turned, turned], axis=0).T[end - lost :, :]
            high = turned.astype(BF16).astype(F32)
            rest = turned - high
            middle = rest.astype(BF16).astype(F32)
            low = rest - middle
            early = iota(turned.shape, 1) < PANEL
            left = jnp.concatenate(
                [high, jnp.where(early, middle, high), jnp.where(early, low, middle)], axis=1
            ).astype(BF16)
            apart = lost - skip
            near = jnp.dot(left[:PANEL], right[:, apart : size - skip], preferred_element_type=F32)
            left_ref[end : end + PANEL, lost:] = left_ref[end : end + PANEL, lost:] - near
            near = jnp.dot(left[:PANEL], right[:, size - skip :], preferred_element_type=F32)
            inverse_ref[end : end + PANEL, :reach] = inverse_ref[end : end + PANEL, :reach] - near
            if end + PANEL < size:
                far = jnp.dot(left[PANEL:], right[:, apart:], preferred_element_type=F32)
                left_ref[end + PANEL :, lost:] = left_ref[end + PANEL :, lost:] - far[:, : size - lost]
                inverse_ref[end + PANEL :, :reach] = inverse_ref[end + PANEL :, :reach] - far[:, size - lost :]
        inverse = panel[:, size - skip :]
        inverse = jnp.where(iota(inverse.shape, 0) + begin >= iota(inverse.shape, 1), inverse, 0.0)
        high, low = split2(inverse)
        cells = window_ref[:reach, :]
        basis_ref[begin:end, :] = jnp.dot(
            jnp.concatenate([high, low], axis=1), jnp.concatenate([cells, cells], axis=0), preferred_element_type=F32
        )
        send(basis_ref, basis_hbm, begin, end)
        if end == LANES:
            factor_ref[:LANES, :LANES] = jnp.where(row >= col, upper_ref[:LANES, :LANES].T, 0.0)
            factor_ref[:LANES, LANES:] = jnp.zeros((LANES, LANES), F32)
            factor_ref[LANES:, :LANES] = upper_ref[:LANES, LANES:].T
            send(factor_ref, factor_hbm, 0, LANES)
    factor_ref[LANES:, LANES:] = jnp.where(row >= col, upper_ref[LANES:, LANES:].T, 0.0)
    send(factor_ref, factor_hbm, LANES, size)
    for copy in copies:
        copy.wait()


def factorise(place, mine, other, stored, coarse):
    old, rows_dev = stored.shape
    size = old + coarse.shape[0]
    return pl.pallas_call(
        factor_kernel,
        out_shape=[shaped(coarse.shape, BF16), shaped((size, size)), shaped((size, rows_dev))],
        in_specs=[SMEM] + [VMEM] * 4,
        out_specs=[HBM] * 3,
        scratch_shapes=[pltpu.VMEM((size, size), F32)] * 4
        + [
            pltpu.VMEM((size, rows_dev), F32),
            pltpu.VMEM((PANEL, LANES), F32),
            pltpu.VMEM((size, rows_dev), BF16),
            pltpu.SemaphoreType.DMA((size // PANEL + 3,)),
        ],
        compiler_params=LIMIT,
        name="factor",
    )(place, mine, other, stored, coarse)


VMEM = pl.BlockSpec(memory_space=pltpu.VMEM)
HBM = pl.BlockSpec(memory_space=pltpu.HBM)
SMEM = pl.BlockSpec(memory_space=pltpu.SMEM)
LIMIT = pltpu.CompilerParams(vmem_limit_bytes=48 * 2**20)


def shaped(shape, dtype=F32):
    return jax.ShapeDtypeStruct(shape, dtype)


def swap(values, axis, bit):
    count = lax.axis_size(axis)
    return lax.ppermute(values, axis, [(i, i ^ bit) for i in range(count)])


def shift(values, axis, step):
    count = lax.axis_size(axis)
    return lax.ppermute(values, axis, [(i, i + step) for i in range(count) if 0 <= i + step < count])


def sum_over_span(values):
    count = lax.axis_size("span")
    if count & (count - 1):
        return lax.psum(values, "span")
    bit = 1
    while bit < count:
        values = values + swap(values, "span", bit)
        bit *= 2
    return values


def local(fine_field, stored, filter_taps):
    snapshots, comps, cells_y, cells_z, cells_x = fine_field.shape
    assert (snapshots, comps, cells_y, cells_z, cells_x) == (8, 3, 16, 16, 128)
    assert lax.axis_size("sect") == 2
    old, rows_dev = stored.shape
    total = rows_dev * lax.axis_size("span") * lax.axis_size("sect")
    place = lax.axis_index("sect").astype(jnp.int32).reshape(1)
    fields = snapshots * comps
    own, ext = pl.pallas_call(
        filter_kernel,
        out_shape=[shaped((comps, 6, snapshots, LANES))] * 2,
        in_specs=[SMEM, HBM, HBM],
        out_specs=[VMEM] * 2,
        scratch_shapes=[
            pltpu.VMEM((fields, cells_y * cells_z, cells_x), BF16),
            pltpu.SMEM(filter_taps.shape, F32),
            pltpu.VMEM((8, 8 * fields, LANES), F32),
            pltpu.VMEM((2, 8 * fields, LANES), F32),
            pltpu.SemaphoreType.DMA((PARTS + 1,)),
        ],
        compiler_params=pltpu.CompilerParams(vmem_limit_bytes=55 * 2**20),
        name="filter",
    )(place, fine_field.reshape(fields, cells_y * cells_z, cells_x), filter_taps)
    left = shift(ext, "span", 1)
    right = shift(ext, "span", -1)
    kept, sent = pl.pallas_call(
        functools.partial(old_kernel, total),
        out_shape=[shaped((HALF, LANES))] * 2,
        in_specs=[SMEM, VMEM, VMEM],
        out_specs=[VMEM] * 2,
        compiler_params=LIMIT,
        name="gram_stored",
    )(place, stored, own)
    lanes = lax.broadcasted_iota(jnp.int32, (1, 1, 1, LANES), 3)
    halo = own[:, 4:] + jnp.where(lanes < 64, left[:, 4:], right[:, 4:])
    partner = swap(jnp.concatenate([sent, halo.reshape(-1, LANES)], axis=0), "sect", 1)
    coarse, sums = pl.pallas_call(
        functools.partial(new_kernel, total),
        out_shape=[shaped((snapshots, rows_dev), BF16), shaped((HALF + 2 * snapshots, LANES))],
        in_specs=[SMEM] + [VMEM] * 6,
        out_specs=[VMEM] * 2,
        compiler_params=LIMIT,
        name="gram_new",
    )(place, stored, own, left, right, partner, kept)
    sums = sum_over_span(sums)
    return tuple(factorise(place, sums, swap(sums, "sect", 1), stored, coarse))


def solution(mesh):
    in_specs = (P("case", None, "sect", "span", None), P(None, ("case", "span", "sect")), P())
    out_specs = (
        P(None, ("case", "span", "sect")),
        P("case", None),
        P(None, ("case", "span", "sect")),
    )
    return jax.shard_map(local, mesh=mesh, in_specs=in_specs, out_specs=out_specs, check_vma=False)
```

```python
import functools

import jax
import jax.numpy as jnp
from jax import lax
from jax.experimental import pallas as pl
from jax.experimental.pallas import tpu as pltpu
from jax.sharding import PartitionSpec as P

F32 = jnp.float32
BF16 = jnp.bfloat16
TAPS = 17
LANES = 128
PANEL = 64
NEAR = 8
FAR = 8
PARTS = 6
OUTSIDE = -64
HALF = LANES + 8


def iota(shape, dim):
    return lax.broadcasted_iota(jnp.int32, shape, dim)


def split2(values):
    high = values.astype(BF16)
    return high, (values - high.astype(F32)).astype(BF16)


def split3(values):
    high = values.astype(BF16)
    rest = values - high.astype(F32)
    middle = rest.astype(BF16)
    return high, middle, (rest - middle.astype(F32)).astype(BF16)


def weights_at(offset, taps_ref, row):
    total = jnp.zeros(offset.shape, F32)
    for tap in range(TAPS):
        total = jnp.where(offset == tap, taps_ref[row, tap], total)
    return total


def start_copies(pairs, sems):
    copies = [pltpu.make_async_copy(source, target, sems.at[i]) for i, (source, target) in enumerate(pairs)]
    for copy in copies:
        copy.start()
    return copies


def cells_of(fine_hbm, fine_ref):
    part = fine_ref.shape[0] // PARTS
    return [
        (fine_hbm.at[p * part : (p + 1) * part], fine_ref.at[p * part : (p + 1) * part]) for p in range(PARTS)
    ]


def plane_matrix(span_cells, sect_cells, taps_ref):
    row, cell = iota((8, 256), 0), iota((8, 256), 1)
    pick = lambda cells: sum(jnp.where(row == s, at, 0) for s, at in enumerate(cells))
    span = weights_at(cell % 16 - 4 * pick(span_cells) + 8, taps_ref, 1)
    sect = weights_at(cell // 16 - 4 * pick(sect_cells) + 8, taps_ref, 0)
    rows = [jnp.broadcast_to(span[s : s + 1], (8, 256)) * sect for s in range(len(span_cells))]
    return jnp.concatenate(split2(jnp.concatenate(rows, axis=0)), axis=0)


def stream_matrix(taps_ref):
    cell, lane = iota((LANES, LANES), 0), iota((LANES, LANES), 1)
    stream = weights_at(cell - 4 * (lane % 32) + 8, taps_ref, 2)
    high = stream.astype(BF16).astype(F32)
    parts = [
        jnp.concatenate([jnp.where(lane // 32 == s, term, 0.0) for s in range(4)], axis=0).astype(BF16)
        for term in (high, stream - high)
    ]
    return jnp.concatenate([parts[0], parts[0], parts[1]], axis=0)


def filter_plane(matrix, fine_ref, plane_ref, copies=None):
    part = fine_ref.shape[0] // PARTS
    half = matrix.shape[0] // 2
    for p in range(PARTS):
        if copies:
            copies[p].wait()
        for field in range(p * part, (p + 1) * part):
            both = jnp.dot(matrix, fine_ref[field], preferred_element_type=F32)
            summed = both[:half] + both[half:]
            for s in range(half // 8):
                plane_ref[s, 8 * field : 8 * field + 8, :] = summed[8 * s : 8 * s + 8]


def filter_stream(plane_ref, tiles, matrix):
    rows = [
        jnp.concatenate([plane_ref[s, pl.ds(8 * comp + k, 8, stride=24), :] for s, k in slots], axis=1)
        for comp, slots in tiles
    ]
    high, low = split2(jnp.concatenate(rows, axis=0))
    return jnp.dot(jnp.concatenate([high, low, high], axis=1), matrix, preferred_element_type=F32)


def sect_cells(first):
    return [0, 1, 2, 3, jnp.where(first, 4, -2), jnp.where(first, 5, -1), OUTSIDE, OUTSIDE]


def sent_kernel(fine_hbm, taps_hbm, near_ref, far_ref, fine_ref, taps_ref, plane_ref, sems):
    *copies, taps_copy = start_copies(cells_of(fine_hbm, fine_ref) + [(taps_hbm, taps_ref)], sems)
    even = lax.axis_index("span") % 2 == 0
    span_cells = [jnp.where(even, at, at - 6) for at in (4, 5)] + [jnp.where(even, at - 6, at) for at in (4, 5)]
    taps_copy.wait()
    matrix = plane_matrix(span_cells, sect_cells(lax.axis_index("sect") == 0), taps_ref)
    filter_plane(matrix, fine_ref, plane_ref, copies)
    matrix = stream_matrix(taps_ref)
    for base, out_ref in ((0, near_ref), (2, far_ref)):
        tiles = [
            (comp, [(base + s, 2 * pair + k) for k in range(2) for s in range(2)])
            for comp in range(3)
            for pair in range(3)
        ]
        result = filter_stream(plane_ref, tiles, matrix)
        for t in range(len(tiles)):
            out_ref[t] = result[8 * t : 8 * t + 8]


def fold(gram, kept_ref, sent_ref, first):
    row, col = iota((LANES, LANES), 0), iota((LANES, LANES), 1)
    across, lower = gram[LANES:, :LANES], gram[LANES:, LANES:]
    packed = jnp.where(row <= col, gram[:LANES, :LANES], lower)
    corner = jnp.sum(jnp.where(row == col, lower, 0.0), axis=0, keepdims=True)
    corner = jnp.broadcast_to(corner, (8, LANES))
    kept_ref[:LANES] = jnp.where(first, packed, across)
    kept_ref[LANES:] = corner
    sent_ref[:LANES] = jnp.where(first, across, packed)
    sent_ref[LANES:] = corner


def own_kernel(
    total, stored_ref, fine_ref, taps_hbm, own_ref, kept_ref, sent_ref, taps_ref, plane_ref, sems
):
    (taps_copy,) = start_copies([(taps_hbm, taps_ref)], sems)
    old, cells = stored_ref.shape
    rows = jnp.concatenate([stored_ref[...], jnp.zeros((8, cells), BF16)], axis=0)
    gram = lax.dot_general(rows, rows, (((1,), (1,)), ((), ())), preferred_element_type=F32) / total
    fold(gram, kept_ref, sent_ref, lax.axis_index("sect") == 0)
    taps_copy.wait()
    matrix = plane_matrix([0, 1, 2, 3], sect_cells(lax.axis_index("sect") == 0), taps_ref)
    filter_plane(matrix, fine_ref, plane_ref)
    tiles = [(comp, [(s, k) for s in range(4)]) for comp in range(3) for k in range(6)]
    result = filter_stream(plane_ref, tiles, stream_matrix(taps_ref))
    for t in range(len(tiles)):
        own_ref[t] = result[8 * t : 8 * t + 8]


def join_kernel(own_ref, near_ref, far_ref, sent_ref, cells_ref, swap_ref):
    even = lax.axis_index("span") % 2 == 0
    half = sent_ref.shape[0]
    lane = iota((8, LANES), 1)
    swap_ref[:half] = sent_ref[...]
    for comp in range(3):
        for pair in range(3):
            near, far = near_ref[3 * comp + pair], far_ref[3 * comp + pair]
            before, after = jnp.where(even, far, near), jnp.where(even, near, far)
            shares = (
                jnp.where(lane < 64, before, pltpu.roll(after, 64, 1)),
                jnp.where(lane < 64, pltpu.roll(before, 64, 1), after),
            )
            for k in range(2):
                value = own_ref[6 * comp + 2 * pair + k] + shares[k]
                if pair < 2:
                    cells_ref[4 * comp + 2 * pair + k] = value
                else:
                    at = half + 8 * (2 * comp + k)
                    swap_ref[at : at + 8, :] = value


def new_kernel(total, stored_ref, cells_ref, partner_ref, kept_ref, coarse_ref, sums_ref):
    first = lax.axis_index("sect") == 0
    half = kept_ref.shape[0]
    cells = []
    for comp in range(3):
        for k in range(4):
            here = first if k >= 2 else jnp.logical_not(first)
            at = half + 8 * (2 * comp + k % 2)
            cells.append(cells_ref[4 * comp + k] + jnp.where(here, partner_ref[at : at + 8, :], 0.0))
    coarse = jnp.concatenate(cells, axis=1).astype(BF16)
    coarse_ref[...] = coarse
    rows = jnp.concatenate([stored_ref[...], coarse], axis=0)
    gram = lax.dot_general(coarse, rows, (((1,), (1,)), ((), ())), preferred_element_type=F32) / total
    sums_ref[:half] = kept_ref[...] + partner_ref[:half, :]
    sums_ref[half : half + 8] = gram[:, :LANES]
    sums_ref[half + 8 :] = gram[:, LANES:]


def eliminate(groups, at, lane, none, scale_ref):
    count = len(groups)
    width = groups[at].shape[1]
    wide = lambda column: jnp.concatenate([column] * (width // LANES), axis=1)
    spread = lambda values, k: jnp.broadcast_to(values[k : k + 1, :], (8, values.shape[1]))
    column = lambda g, j: jnp.broadcast_to(groups[g][:, lane + j : lane + j + 1], (8, LANES))
    sub = iota((8, LANES), 0)
    cols = {(j, g): column(g, j) for g in (at, at + 1) for j in range(8 * (g - at) + 8)}
    for g in (at, at + 1):
        cols[0, g] = cols[0, g] + none
    for k in range(16):
        home, k_sub = at + k // 8, k % 8
        for g in range(at + 2, count):
            step = NEAR if g < at + 4 else FAR
            if k % step == 0:
                for j in range(k, k + step):
                    cols[j, g] = column(g, j)
        scale = lax.rsqrt(spread(cols[k, home], k_sub))
        square = scale * scale
        scale_ref[8 * home + k_sub : 8 * home + k_sub + 1, :] = scale[k_sub : k_sub + 1, :]
        share = {g: cols[k, g] * square for g in range(home, count)}
        share[home] = jnp.where(sub > k_sub, share[home], 0.0)
        for j in range(k + 1, 16):
            j_home, j_sub = at + j // 8, j % 8
            head = spread(cols[k, j_home], j_sub)
            for g in range(j_home, count):
                step = 16 if g < at + 2 else NEAR if g < at + 4 else FAR
                if j // step == k // step:
                    if j == k + 1 and g == j_home:
                        cols[j, g] = cols[j, g] - (cols[k, g] * head) * square
                    else:
                        cols[j, g] = cols[j, g] - share[g] * head
        row = spread(groups[home], k_sub)
        for g in range(home, count):
            groups[g] = groups[g] - wide(share[g]) * row
    for g in (at, at + 1):
        groups[g] = groups[g] * wide(scale_ref[8 * g : 8 * g + 8, :])
    return groups


def factor_kernel(
    mine_ref, other_ref, stored_ref, coarse_ref, new_hbm, factor_hbm, basis_hbm,
    left_ref, inverse_ref, upper_ref, factor_ref, basis_ref, scale_ref, window_ref, sems,
):
    first = lax.axis_index("sect") == 0
    none = jnp.full((8, LANES), jnp.minimum(lax.axis_index("sect"), 0).astype(F32))
    size = left_ref.shape[0]
    row, col = iota((LANES, LANES), 0), iota((LANES, LANES), 1)
    packed = jnp.where(first, mine_ref[:LANES], other_ref[:LANES])
    across = jnp.where(first, other_ref[:LANES], mine_ref[:LANES])
    corner = jnp.where(first, mine_ref[LANES : LANES + 1], other_ref[LANES : LANES + 1])
    added = mine_ref[HALF : HALF + 8] + other_ref[HALF : HALF + 8]
    across = jnp.concatenate([across[:-8], across[-8:] + added], axis=0)
    added = mine_ref[HALF + 8 :] + other_ref[HALF + 8 :]
    added = jnp.concatenate([jnp.zeros((LANES - 8, LANES), F32), added], axis=0)
    corner = corner + jnp.sum(jnp.where(row == col, added, 0.0), axis=0, keepdims=True)
    packed = packed + jnp.where(row > col, added, 0.0)
    turned = packed.T
    copies = [pltpu.make_async_copy(coarse_ref, new_hbm, sems.at[0])]
    copies[0].start()
    window_ref[: size - 8, :] = stored_ref[...]
    window_ref[size - 8 :, :] = coarse_ref[...]
    left_ref[:LANES, :LANES] = jnp.where(row <= col, packed, turned)
    left_ref[:LANES, LANES:] = across.T
    left_ref[LANES:, :LANES] = jnp.zeros((LANES, LANES), F32)
    left_ref[LANES:, LANES:] = jnp.where(
        row == col, jnp.broadcast_to(corner, (LANES, LANES)), jnp.where(row < col, turned, packed)
    )
    inverse_ref[...] = jnp.where(iota((size, size), 0) == iota((size, size), 1), 1.0, 0.0)
    upper_ref[...] = jnp.zeros((size, size), F32)

    def send(source, target, begin, end):
        copies.append(pltpu.make_async_copy(source.at[begin:end], target.at[begin:end], sems.at[len(copies)]))
        copies[-1].start()

    for begin in range(0, size, PANEL):
        end = begin + PANEL
        skip = 0 if begin < LANES else LANES
        reach = LANES if end <= LANES else size
        groups = [
            jnp.concatenate([left_ref[g : g + 8, skip:], inverse_ref[g : g + 8, :reach]], axis=1)
            for g in range(begin, end, 8)
        ]
        for g in range(0, PANEL // 8, 2):
            groups = eliminate(groups, g, begin + 8 * g - skip, none, scale_ref)
        panel = jnp.concatenate(groups, axis=0)
        upper_ref[begin:end, skip:] = panel[:, : size - skip]
        if end < size:
            high, middle, low = split3(panel)
            right = jnp.concatenate([high, middle, high, low, high, middle], axis=0)
            lost = LANES if end == LANES else skip
            turned = panel[:, lost - skip : size - skip]
            turned = jnp.concatenate([turned, turned], axis=0).T[end - lost :, :]
            high = turned.astype(BF16).astype(F32)
            rest = turned - high
            middle = rest.astype(BF16).astype(F32)
            low = rest - middle
            early = iota(turned.shape, 1) < PANEL
            left = jnp.concatenate(
                [high, jnp.where(early, middle, high), jnp.where(early, low, middle)], axis=1
            ).astype(BF16)
            apart = lost - skip
            near = jnp.dot(left[:PANEL], right[:, apart : size - skip], preferred_element_type=F32)
            left_ref[end : end + PANEL, lost:] = left_ref[end : end + PANEL, lost:] - near
            near = jnp.dot(left[:PANEL], right[:, size - skip :], preferred_element_type=F32)
            inverse_ref[end : end + PANEL, :reach] = inverse_ref[end : end + PANEL, :reach] - near
            if end + PANEL < size:
                far = jnp.dot(left[PANEL:], right[:, apart:], preferred_element_type=F32)
                left_ref[end + PANEL :, lost:] = left_ref[end + PANEL :, lost:] - far[:, : size - lost]
                inverse_ref[end + PANEL :, :reach] = inverse_ref[end + PANEL :, :reach] - far[:, size - lost :]
        inverse = panel[:, size - skip :]
        inverse = jnp.where(iota(inverse.shape, 0) + begin >= iota(inverse.shape, 1), inverse, 0.0)
        high, low = split2(inverse)
        cells = window_ref[:reach, :]
        basis_ref[begin:end, :] = jnp.dot(
            jnp.concatenate([high, low], axis=1), jnp.concatenate([cells, cells], axis=0), preferred_element_type=F32
        )
        send(basis_ref, basis_hbm, begin, end)
        if end == LANES:
            factor_ref[:LANES, :LANES] = jnp.where(row >= col, upper_ref[:LANES, :LANES].T, 0.0)
            factor_ref[:LANES, LANES:] = jnp.zeros((LANES, LANES), F32)
            factor_ref[LANES:, :LANES] = upper_ref[:LANES, LANES:].T
            send(factor_ref, factor_hbm, 0, LANES)
    factor_ref[LANES:, LANES:] = jnp.where(row >= col, upper_ref[LANES:, LANES:].T, 0.0)
    send(factor_ref, factor_hbm, LANES, size)
    for copy in copies:
        copy.wait()


def factorise(mine, other, stored, coarse):
    old, rows_dev = stored.shape
    size = old + coarse.shape[0]
    return pl.pallas_call(
        factor_kernel,
        out_shape=[shaped(coarse.shape, BF16), shaped((size, size)), shaped((size, rows_dev))],
        in_specs=[VMEM] * 4,
        out_specs=[HBM] * 3,
        scratch_shapes=[pltpu.VMEM((size, size), F32)] * 4
        + [
            pltpu.VMEM((size, rows_dev), F32),
            pltpu.VMEM((PANEL, LANES), F32),
            pltpu.VMEM((size, rows_dev), BF16),
            pltpu.SemaphoreType.DMA((size // PANEL + 3,)),
        ],
        compiler_params=LIMIT,
        name="factor",
    )(mine, other, stored, coarse)


VMEM = pl.BlockSpec(memory_space=pltpu.VMEM)
HBM = pl.BlockSpec(memory_space=pltpu.HBM)
LIMIT = pltpu.CompilerParams(vmem_limit_bytes=48 * 2**20)


def shaped(shape, dtype=F32):
    return jax.ShapeDtypeStruct(shape, dtype)


def swap(values, axis, bit):
    count = lax.axis_size(axis)
    return lax.ppermute(values, axis, [(i, i ^ bit) for i in range(count)])


def swap_pairs(values, axis, begin):
    count = lax.axis_size(axis)
    pairs = [(i, i + 1) for i in range(begin, count - 1, 2)]
    return lax.ppermute(values, axis, pairs + [(j, i) for i, j in pairs])


def sum_over_span(values):
    count = lax.axis_size("span")
    if count & (count - 1):
        return lax.psum(values, "span")
    bit = 1
    while bit < count:
        values = values + swap(values, "span", bit)
        bit *= 2
    return values


def local(fine_field, stored, filter_taps):
    snapshots, comps, cells_y, cells_z, cells_x = fine_field.shape
    assert (snapshots, comps, cells_y, cells_z, cells_x) == (8, 3, 16, 16, 128)
    assert lax.axis_size("sect") == 2
    old, rows_dev = stored.shape
    total = rows_dev * lax.axis_size("span") * lax.axis_size("sect")
    fields = snapshots * comps
    fine = fine_field.reshape(fields, cells_y * cells_z, cells_x)
    fine = pltpu.with_memory_space_constraint(fine, pltpu.HBM)
    taps = pltpu.with_memory_space_constraint(filter_taps, pltpu.HBM)
    room = [pltpu.SMEM(taps.shape, F32), pltpu.VMEM((4, 8 * fields, LANES), F32)]
    near, far, fine = pl.pallas_call(
        sent_kernel,
        out_shape=[pltpu.VMEM((9, snapshots, LANES), F32)] * 2 + [pltpu.VMEM(fine.shape, BF16)],
        in_specs=[HBM, HBM],
        out_specs=[VMEM] * 3,
        scratch_shapes=room + [pltpu.SemaphoreType.DMA((PARTS + 1,))],
        compiler_params=LIMIT,
        name="filter_sent",
    )(fine, taps)
    from_far = swap_pairs(far, "span", 1)
    from_near = swap_pairs(near, "span", 0)
    own, kept, sent = pl.pallas_call(
        functools.partial(own_kernel, total),
        out_shape=[shaped((18, snapshots, LANES))] + [shaped((HALF, LANES))] * 2,
        in_specs=[VMEM, VMEM, HBM],
        out_specs=[VMEM] * 3,
        scratch_shapes=room + [pltpu.SemaphoreType.DMA((1,))],
        compiler_params=LIMIT,
        name="filter_own",
    )(stored, fine, taps)
    cells, crossing = pl.pallas_call(
        join_kernel,
        out_shape=[shaped((12, snapshots, LANES)), shaped((HALF + 6 * snapshots, LANES))],
        in_specs=[VMEM] * 4,
        out_specs=[VMEM] * 2,
        compiler_params=LIMIT,
        name="join",
    )(own, from_near, from_far, sent)
    coarse, sums = pl.pallas_call(
        functools.partial(new_kernel, total),
        out_shape=[shaped((snapshots, rows_dev), BF16), shaped((HALF + 2 * snapshots, LANES))],
        in_specs=[VMEM] * 4,
        out_specs=[VMEM] * 2,
        compiler_params=LIMIT,
        name="gram_new",
    )(stored, cells, swap(crossing, "sect", 1), kept)
    sums = sum_over_span(sums)
    return tuple(factorise(sums, swap(sums, "sect", 1), stored, coarse))


def solution(mesh):
    in_specs = (P("case", None, "sect", "span", None), P(None, ("case", "span", "sect")), P())
    out_specs = (
        P(None, ("case", "span", "sect")),
        P("case", None),
        P(None, ("case", "span", "sect")),
    )
    return jax.shard_map(local, mesh=mesh, in_specs=in_specs, out_specs=out_specs, check_vma=False)
```

```python
import functools

import jax
import jax.numpy as jnp
from jax import lax
from jax.experimental import pallas as pl
from jax.experimental.pallas import tpu as pltpu
from jax.sharding import PartitionSpec as P

F32 = jnp.float32
BF16 = jnp.bfloat16
TAPS = 17
LANES = 128
PANEL = 64
NEAR = 8
FAR = 8
PARTS = 2
OUTSIDE = -64
HALF = LANES + 8


def iota(shape, dim):
    return lax.broadcasted_iota(jnp.int32, shape, dim)


def split2(values):
    high = values.astype(BF16)
    return high, (values - high.astype(F32)).astype(BF16)


def split3(values):
    high = values.astype(BF16)
    rest = values - high.astype(F32)
    middle = rest.astype(BF16)
    return high, middle, (rest - middle.astype(F32)).astype(BF16)


def weights_at(offset, taps_ref, row):
    total = jnp.zeros(offset.shape, F32)
    for tap in range(TAPS):
        total = jnp.where(offset == tap, taps_ref[row, tap], total)
    return total


def start_copies(pairs, sems):
    copies = [pltpu.make_async_copy(source, target, sems.at[i]) for i, (source, target) in enumerate(pairs)]
    for copy in copies:
        copy.start()
    return copies


def cells_of(fine_hbm, fine_ref):
    part = fine_ref.shape[0] // PARTS
    return [
        (fine_hbm.at[p * part : (p + 1) * part], fine_ref.at[p * part : (p + 1) * part]) for p in range(PARTS)
    ]


def plane_matrix(span_cells, sect_cells, taps_ref):
    row, cell = iota((8, 256), 0), iota((8, 256), 1)
    pick = lambda cells: sum(jnp.where(row == s, at, 0) for s, at in enumerate(cells))
    span = weights_at(cell % 16 - 4 * pick(span_cells) + 8, taps_ref, 1)
    sect = weights_at(cell // 16 - 4 * pick(sect_cells) + 8, taps_ref, 0)
    rows = [jnp.broadcast_to(span[s : s + 1], (8, 256)) * sect for s in range(len(span_cells))]
    return jnp.concatenate(split2(jnp.concatenate(rows, axis=0)), axis=0)


def stream_matrix(taps_ref):
    cell, lane = iota((LANES, LANES), 0), iota((LANES, LANES), 1)
    stream = weights_at(cell - 4 * (lane % 32) + 8, taps_ref, 2)
    high = stream.astype(BF16).astype(F32)
    parts = [
        jnp.concatenate([jnp.where(lane // 32 == s, term, 0.0) for s in range(4)], axis=0).astype(BF16)
        for term in (high, stream - high)
    ]
    return jnp.concatenate([parts[0], parts[0], parts[1]], axis=0)


def filter_plane(matrix, fine_ref, plane_ref, copies=None):
    part = fine_ref.shape[0] // PARTS
    half = matrix.shape[0] // 2
    for p in range(PARTS):
        if copies:
            copies[p].wait()
        for field in range(p * part, (p + 1) * part):
            both = jnp.dot(matrix, fine_ref[field], preferred_element_type=F32)
            summed = both[:half] + both[half:]
            for s in range(half // 8):
                plane_ref[s, 8 * field : 8 * field + 8, :] = summed[8 * s : 8 * s + 8]


def filter_stream(plane_ref, tiles, matrix):
    rows = [
        jnp.concatenate([plane_ref[s, pl.ds(8 * comp + k, 8, stride=24), :] for s, k in slots], axis=1)
        for comp, slots in tiles
    ]
    high, low = split2(jnp.concatenate(rows, axis=0))
    return jnp.dot(jnp.concatenate([high, low, high], axis=1), matrix, preferred_element_type=F32)


def sect_cells(first):
    return [0, 1, 2, 3, jnp.where(first, 4, -2), jnp.where(first, 5, -1), OUTSIDE, OUTSIDE]


def sent_kernel(
    fine_hbm, taps_hbm, near_ref, far_ref, fine_ref, own_matrix_ref, stream_ref, taps_ref, plane_ref, sems
):
    taps_copy, *copies = start_copies([(taps_hbm, taps_ref)] + cells_of(fine_hbm, fine_ref), sems)
    even = lax.axis_index("span") % 2 == 0
    span_cells = [jnp.where(even, at, at - 6) for at in (4, 5)] + [jnp.where(even, at - 6, at) for at in (4, 5)]
    taps_copy.wait()
    sect = sect_cells(lax.axis_index("sect") == 0)
    matrix = plane_matrix(span_cells, sect, taps_ref)
    stream_ref[...] = stream_matrix(taps_ref)
    own_matrix_ref[...] = plane_matrix([0, 1, 2, 3], sect, taps_ref)
    filter_plane(matrix, fine_ref, plane_ref, copies)
    matrix = stream_ref[...]
    for base, out_ref in ((0, near_ref), (2, far_ref)):
        tiles = [
            (comp, [(base + s, 2 * pair + k) for k in range(2) for s in range(2)])
            for comp in range(3)
            for pair in range(3)
        ]
        result = filter_stream(plane_ref, tiles, matrix)
        for t in range(len(tiles)):
            out_ref[t] = result[8 * t : 8 * t + 8]


def fold(gram, kept_ref, sent_ref, first):
    row, col = iota((LANES, LANES), 0), iota((LANES, LANES), 1)
    across, lower = gram[LANES:, :LANES], gram[LANES:, LANES:]
    packed = jnp.where(row <= col, gram[:LANES, :LANES], lower)
    corner = jnp.sum(jnp.where(row == col, lower, 0.0), axis=0, keepdims=True)
    corner = jnp.broadcast_to(corner, (8, LANES))
    kept_ref[:LANES] = jnp.where(first, packed, across)
    kept_ref[LANES:] = corner
    sent_ref[:LANES] = jnp.where(first, across, packed)
    sent_ref[LANES:] = corner


def own_kernel(
    total, stored_hbm, fine_ref, matrix_ref, stream_ref, own_ref, kept_ref, sent_ref, stored_ref, plane_ref, sems
):
    (copy,) = start_copies([(stored_hbm, stored_ref)], sems)
    filter_plane(matrix_ref[...], fine_ref, plane_ref)
    tiles = [(comp, [(s, k) for s in range(4)]) for comp in range(3) for k in range(6)]
    result = filter_stream(plane_ref, tiles, stream_ref[...])
    for t in range(len(tiles)):
        own_ref[t] = result[8 * t : 8 * t + 8]
    copy.wait()
    old, cells = stored_ref.shape
    rows = jnp.concatenate([stored_ref[...], jnp.zeros((8, cells), BF16)], axis=0)
    gram = lax.dot_general(rows, rows, (((1,), (1,)), ((), ())), preferred_element_type=F32) / total
    fold(gram, kept_ref, sent_ref, lax.axis_index("sect") == 0)


def place_shares(shares, before):
    lane = iota((8, LANES), 1)
    turned = pltpu.roll(shares, 64, 1)
    here = jnp.where(before, lane, LANES - 1 - lane) < 64
    return [jnp.where(here, jnp.where(before == (k == 0), shares, turned), 0.0) for k in range(2)]


def join_far_kernel(own_ref, far_ref, cells_ref):
    before = lax.axis_index("span") % 2 == 0
    for comp in range(3):
        for pair in range(3):
            shares = place_shares(far_ref[3 * comp + pair], before)
            for k in range(2):
                at = 6 * comp + 2 * pair + k
                cells_ref[at] = own_ref[at] + shares[k]


def join_near_kernel(own_ref, near_ref, sent_ref, cells_ref, swap_ref):
    before = lax.axis_index("span") % 2 == 1
    half = sent_ref.shape[0]
    swap_ref[:half] = sent_ref[...]
    for comp in range(3):
        for pair in range(3):
            shares = place_shares(near_ref[3 * comp + pair], before)
            for k in range(2):
                value = own_ref[6 * comp + 2 * pair + k] + shares[k]
                if pair < 2:
                    cells_ref[4 * comp + 2 * pair + k] = value
                else:
                    at = half + 8 * (2 * comp + k)
                    swap_ref[at : at + 8, :] = value


def new_kernel(total, stored_ref, cells_ref, partner_ref, kept_ref, coarse_ref, sums_ref):
    first = lax.axis_index("sect") == 0
    half = kept_ref.shape[0]
    cells = []
    for comp in range(3):
        for k in range(4):
            here = first if k >= 2 else jnp.logical_not(first)
            at = half + 8 * (2 * comp + k % 2)
            cells.append(cells_ref[4 * comp + k] + jnp.where(here, partner_ref[at : at + 8, :], 0.0))
    coarse = jnp.concatenate(cells, axis=1).astype(BF16)
    coarse_ref[...] = coarse
    rows = jnp.concatenate([stored_ref[...], coarse], axis=0)
    gram = lax.dot_general(coarse, rows, (((1,), (1,)), ((), ())), preferred_element_type=F32) / total
    sums_ref[:half] = kept_ref[...] + partner_ref[:half, :]
    sums_ref[half : half + 8] = gram[:, :LANES]
    sums_ref[half + 8 :] = gram[:, LANES:]


def eliminate(groups, at, lane, none, scale_ref):
    count = len(groups)
    width = groups[at].shape[1]
    wide = lambda column: jnp.concatenate([column] * (width // LANES), axis=1)
    spread = lambda values, k: jnp.broadcast_to(values[k : k + 1, :], (8, values.shape[1]))
    column = lambda g, j: jnp.broadcast_to(groups[g][:, lane + j : lane + j + 1], (8, LANES))
    sub = iota((8, LANES), 0)
    cols = {(j, g): column(g, j) for g in (at, at + 1) for j in range(8 * (g - at) + 8)}
    for g in (at, at + 1):
        cols[0, g] = cols[0, g] + none
    for k in range(16):
        home, k_sub = at + k // 8, k % 8
        for g in range(at + 2, count):
            step = NEAR if g < at + 4 else FAR
            if k % step == 0:
                for j in range(k, k + step):
                    cols[j, g] = column(g, j)
        scale = lax.rsqrt(spread(cols[k, home], k_sub))
        square = scale * scale
        scale_ref[8 * home + k_sub : 8 * home + k_sub + 1, :] = scale[k_sub : k_sub + 1, :]
        share = {g: cols[k, g] * square for g in range(home, count)}
        share[home] = jnp.where(sub > k_sub, share[home], 0.0)
        for j in range(k + 1, 16):
            j_home, j_sub = at + j // 8, j % 8
            head = spread(cols[k, j_home], j_sub)
            for g in range(j_home, count):
                step = 16 if g < at + 2 else NEAR if g < at + 4 else FAR
                if j // step == k // step:
                    if j == k + 1 and g == j_home:
                        cols[j, g] = cols[j, g] - (cols[k, g] * head) * square
                    else:
                        cols[j, g] = cols[j, g] - share[g] * head
        row = spread(groups[home], k_sub)
        for g in range(home, count):
            groups[g] = groups[g] - wide(share[g]) * row
    for g in (at, at + 1):
        groups[g] = groups[g] * wide(scale_ref[8 * g : 8 * g + 8, :])
    return groups


def factor_kernel(
    mine_ref, other_ref, stored_ref, coarse_ref, new_hbm, factor_hbm, basis_hbm,
    left_ref, inverse_ref, upper_ref, factor_ref, basis_ref, scale_ref, window_ref, sems,
):
    first = lax.axis_index("sect") == 0
    none = jnp.full((8, LANES), jnp.minimum(lax.axis_index("sect"), 0).astype(F32))
    size = left_ref.shape[0]
    row, col = iota((LANES, LANES), 0), iota((LANES, LANES), 1)
    packed = jnp.where(first, mine_ref[:LANES], other_ref[:LANES])
    across = jnp.where(first, other_ref[:LANES], mine_ref[:LANES])
    corner = jnp.where(first, mine_ref[LANES : LANES + 1], other_ref[LANES : LANES + 1])
    added = mine_ref[HALF : HALF + 8] + other_ref[HALF : HALF + 8]
    across = jnp.concatenate([across[:-8], across[-8:] + added], axis=0)
    added = mine_ref[HALF + 8 :] + other_ref[HALF + 8 :]
    added = jnp.concatenate([jnp.zeros((LANES - 8, LANES), F32), added], axis=0)
    corner = corner + jnp.sum(jnp.where(row == col, added, 0.0), axis=0, keepdims=True)
    packed = packed + jnp.where(row > col, added, 0.0)
    turned = packed.T
    copies = [pltpu.make_async_copy(coarse_ref, new_hbm, sems.at[0])]
    copies[0].start()
    window_ref[: size - 8, :] = stored_ref[...]
    window_ref[size - 8 :, :] = coarse_ref[...]
    left_ref[:LANES, :LANES] = jnp.where(row <= col, packed, turned)
    left_ref[:LANES, LANES:] = across.T
    left_ref[LANES:, :LANES] = jnp.zeros((LANES, LANES), F32)
    left_ref[LANES:, LANES:] = jnp.where(
        row == col, jnp.broadcast_to(corner, (LANES, LANES)), jnp.where(row < col, turned, packed)
    )
    inverse_ref[...] = jnp.where(iota((size, size), 0) == iota((size, size), 1), 1.0, 0.0)
    upper_ref[...] = jnp.zeros((size, size), F32)

    def send(source, target, begin, end):
        copies.append(pltpu.make_async_copy(source.at[begin:end], target.at[begin:end], sems.at[len(copies)]))
        copies[-1].start()

    for begin in range(0, size, PANEL):
        end = begin + PANEL
        skip = 0 if begin < LANES else LANES
        reach = LANES if end <= LANES else size
        groups = [
            jnp.concatenate([left_ref[g : g + 8, skip:], inverse_ref[g : g + 8, :reach]], axis=1)
            for g in range(begin, end, 8)
        ]
        for g in range(0, PANEL // 8, 2):
            groups = eliminate(groups, g, begin + 8 * g - skip, none, scale_ref)
        panel = jnp.concatenate(groups, axis=0)
        upper_ref[begin:end, skip:] = panel[:, : size - skip]
        if end < size:
            high, middle, low = split3(panel)
            right = jnp.concatenate([high, middle, high, low, high, middle], axis=0)
            lost = LANES if end == LANES else skip
            turned = panel[:, lost - skip : size - skip]
            turned = jnp.concatenate([turned, turned], axis=0).T[end - lost :, :]
            high = turned.astype(BF16).astype(F32)
            rest = turned - high
            middle = rest.astype(BF16).astype(F32)
            low = rest - middle
            early = iota(turned.shape, 1) < PANEL
            left = jnp.concatenate(
                [high, jnp.where(early, middle, high), jnp.where(early, low, middle)], axis=1
            ).astype(BF16)
            apart = lost - skip
            near = jnp.dot(left[:PANEL], right[:, apart : size - skip], preferred_element_type=F32)
            left_ref[end : end + PANEL, lost:] = left_ref[end : end + PANEL, lost:] - near
            near = jnp.dot(left[:PANEL], right[:, size - skip :], preferred_element_type=F32)
            inverse_ref[end : end + PANEL, :reach] = inverse_ref[end : end + PANEL, :reach] - near
            if end + PANEL < size:
                far = jnp.dot(left[PANEL:], right[:, apart:], preferred_element_type=F32)
                left_ref[end + PANEL :, lost:] = left_ref[end + PANEL :, lost:] - far[:, : size - lost]
                inverse_ref[end + PANEL :, :reach] = inverse_ref[end + PANEL :, :reach] - far[:, size - lost :]
        inverse = panel[:, size - skip :]
        inverse = jnp.where(iota(inverse.shape, 0) + begin >= iota(inverse.shape, 1), inverse, 0.0)
        high, low = split2(inverse)
        cells = window_ref[:reach, :]
        basis_ref[begin:end, :] = jnp.dot(
            jnp.concatenate([high, low], axis=1), jnp.concatenate([cells, cells], axis=0), preferred_element_type=F32
        )
        send(basis_ref, basis_hbm, begin, end)
        if end == LANES:
            factor_ref[:LANES, :LANES] = jnp.where(row >= col, upper_ref[:LANES, :LANES].T, 0.0)
            factor_ref[:LANES, LANES:] = jnp.zeros((LANES, LANES), F32)
            factor_ref[LANES:, :LANES] = upper_ref[:LANES, LANES:].T
            send(factor_ref, factor_hbm, 0, LANES)
    factor_ref[LANES:, LANES:] = jnp.where(row >= col, upper_ref[LANES:, LANES:].T, 0.0)
    send(factor_ref, factor_hbm, LANES, size)
    for copy in copies:
        copy.wait()


def factorise(mine, other, stored, coarse):
    old, rows_dev = stored.shape
    size = old + coarse.shape[0]
    return pl.pallas_call(
        factor_kernel,
        out_shape=[shaped(coarse.shape, BF16), shaped((size, size)), shaped((size, rows_dev))],
        in_specs=[VMEM] * 4,
        out_specs=[HBM] * 3,
        scratch_shapes=[pltpu.VMEM((size, size), F32)] * 4
        + [
            pltpu.VMEM((size, rows_dev), F32),
            pltpu.VMEM((PANEL, LANES), F32),
            pltpu.VMEM((size, rows_dev), BF16),
            pltpu.SemaphoreType.DMA((size // PANEL + 3,)),
        ],
        compiler_params=LIMIT,
        name="factor",
    )(mine, other, stored, coarse)


VMEM = pl.BlockSpec(memory_space=pltpu.VMEM)
HBM = pl.BlockSpec(memory_space=pltpu.HBM)
LIMIT = pltpu.CompilerParams(vmem_limit_bytes=48 * 2**20)


def shaped(shape, dtype=F32):
    return jax.ShapeDtypeStruct(shape, dtype)


def swap(values, axis, bit):
    count = lax.axis_size(axis)
    return lax.ppermute(values, axis, [(i, i ^ bit) for i in range(count)])


def swap_pairs(values, axis, begin):
    count = lax.axis_size(axis)
    pairs = [(i, i + 1) for i in range(begin, count - 1, 2)]
    return lax.ppermute(values, axis, pairs + [(j, i) for i, j in pairs])


def sum_over_span(values):
    count = lax.axis_size("span")
    if count & (count - 1):
        return lax.psum(values, "span")
    bit = 1
    while bit < count:
        values = values + swap(values, "span", bit)
        bit *= 2
    return values


def local(fine_field, stored, filter_taps):
    snapshots, comps, cells_y, cells_z, cells_x = fine_field.shape
    assert (snapshots, comps, cells_y, cells_z, cells_x) == (8, 3, 16, 16, 128)
    assert lax.axis_size("sect") == 2
    old, rows_dev = stored.shape
    total = rows_dev * lax.axis_size("span") * lax.axis_size("sect")
    fields = snapshots * comps
    fine = fine_field.reshape(fields, cells_y * cells_z, cells_x)
    fine = pltpu.with_memory_space_constraint(fine, pltpu.HBM)
    taps = pltpu.with_memory_space_constraint(filter_taps, pltpu.HBM)
    plane = pltpu.VMEM((4, 8 * fields, LANES), F32)
    near, far, fine, matrix, stream = pl.pallas_call(
        sent_kernel,
        out_shape=[pltpu.VMEM((9, snapshots, LANES), F32)] * 2
        + [pltpu.VMEM(fine.shape, BF16), pltpu.VMEM((64, 256), BF16), pltpu.VMEM((12 * LANES, LANES), BF16)],
        in_specs=[HBM] * 2,
        out_specs=[VMEM] * 5,
        scratch_shapes=[pltpu.SMEM(taps.shape, F32), plane, pltpu.SemaphoreType.DMA((PARTS + 1,))],
        compiler_params=LIMIT,
        name="filter_sent",
    )(fine, taps)
    from_far = swap_pairs(far, "span", 1)
    from_near = swap_pairs(near, "span", 0)
    own, kept, sent, stored = pl.pallas_call(
        functools.partial(own_kernel, total),
        out_shape=[shaped((18, snapshots, LANES))]
        + [shaped((HALF, LANES))] * 2
        + [pltpu.VMEM(stored.shape, BF16)],
        in_specs=[HBM] + [VMEM] * 3,
        out_specs=[VMEM] * 4,
        scratch_shapes=[plane, pltpu.SemaphoreType.DMA((1,))],
        compiler_params=LIMIT,
        name="filter_own",
    )(pltpu.with_memory_space_constraint(stored, pltpu.HBM), fine, matrix, stream)
    own = pl.pallas_call(
        join_far_kernel,
        out_shape=shaped((18, snapshots, LANES)),
        in_specs=[VMEM] * 2,
        out_specs=VMEM,
        compiler_params=LIMIT,
        name="join_far",
    )(own, from_far)
    cells, crossing = pl.pallas_call(
        join_near_kernel,
        out_shape=[shaped((12, snapshots, LANES)), shaped((HALF + 6 * snapshots, LANES))],
        in_specs=[VMEM] * 3,
        out_specs=[VMEM] * 2,
        compiler_params=LIMIT,
        name="join_near",
    )(own, from_near, sent)
    coarse, sums = pl.pallas_call(
        functools.partial(new_kernel, total),
        out_shape=[shaped((snapshots, rows_dev), BF16), shaped((HALF + 2 * snapshots, LANES))],
        in_specs=[VMEM] * 4,
        out_specs=[VMEM] * 2,
        compiler_params=LIMIT,
        name="gram_new",
    )(stored, cells, swap(crossing, "sect", 1), kept)
    sums = sum_over_span(sums)
    return tuple(factorise(sums, swap(sums, "sect", 1), stored, coarse))


def solution(mesh):
    in_specs = (P("case", None, "sect", "span", None), P(None, ("case", "span", "sect")), P())
    out_specs = (
        P(None, ("case", "span", "sect")),
        P("case", None),
        P(None, ("case", "span", "sect")),
    )
    return jax.shard_map(local, mesh=mesh, in_specs=in_specs, out_specs=out_specs, check_vma=False)
```

```python
import functools

import jax
import jax.numpy as jnp
from jax import lax
from jax.experimental import pallas as pl
from jax.experimental.pallas import tpu as pltpu
from jax.sharding import PartitionSpec as P

F32 = jnp.float32
BF16 = jnp.bfloat16
TAPS = 17
LANES = 128
PANEL = 64
NEAR = 8
FAR = 8
PARTS = 2
OUTSIDE = -64
HALF = LANES + 8


def iota(shape, dim):
    return lax.broadcasted_iota(jnp.int32, shape, dim)


def split2(values):
    high = values.astype(BF16)
    return high, (values - high.astype(F32)).astype(BF16)


def split3(values):
    high = values.astype(BF16)
    rest = values - high.astype(F32)
    middle = rest.astype(BF16)
    return high, middle, (rest - middle.astype(F32)).astype(BF16)


def weights_at(offset, taps_ref, row):
    total = jnp.zeros(offset.shape, F32)
    for tap in range(TAPS):
        total = jnp.where(offset == tap, taps_ref[row, tap], total)
    return total


def start_copies(pairs, sems):
    copies = [pltpu.make_async_copy(source, target, sems.at[i]) for i, (source, target) in enumerate(pairs)]
    for copy in copies:
        copy.start()
    return copies


def cells_of(fine_hbm, fine_ref):
    part = fine_ref.shape[0] // PARTS
    return [
        (fine_hbm.at[p * part : (p + 1) * part], fine_ref.at[p * part : (p + 1) * part]) for p in range(PARTS)
    ]


def plane_matrix(span_cells, sect_cells, taps_ref):
    row, cell = iota((8, 256), 0), iota((8, 256), 1)
    pick = lambda cells: sum(jnp.where(row == s, at, 0) for s, at in enumerate(cells))
    span = weights_at(cell % 16 - 4 * pick(span_cells) + 8, taps_ref, 1)
    sect = weights_at(cell // 16 - 4 * pick(sect_cells) + 8, taps_ref, 0)
    rows = [jnp.broadcast_to(span[s : s + 1], (8, 256)) * sect for s in range(len(span_cells))]
    return jnp.concatenate(split2(jnp.concatenate(rows, axis=0)), axis=0)


def stream_matrix(taps_ref):
    cell, lane = iota((LANES, LANES), 0), iota((LANES, LANES), 1)
    stream = weights_at(cell - 4 * (lane % 32) + 8, taps_ref, 2)
    high = stream.astype(BF16).astype(F32)
    parts = [
        jnp.concatenate([jnp.where(lane // 32 == s, term, 0.0) for s in range(4)], axis=0).astype(BF16)
        for term in (high, stream - high)
    ]
    return jnp.concatenate([parts[0], parts[0], parts[1]], axis=0)


def filter_plane(matrix, fine_ref, plane_ref, copies=None):
    part = fine_ref.shape[0] // PARTS
    half = matrix.shape[0] // 2
    for p in range(PARTS):
        if copies:
            copies[p].wait()
        for field in range(p * part, (p + 1) * part):
            both = jnp.dot(matrix, fine_ref[field], preferred_element_type=F32)
            summed = both[:half] + both[half:]
            for s in range(half // 8):
                plane_ref[s, 8 * field : 8 * field + 8, :] = summed[8 * s : 8 * s + 8]


def filter_stream(plane_ref, tiles, matrix):
    rows = [
        jnp.concatenate([plane_ref[s, pl.ds(8 * comp + k, 8, stride=24), :] for s, k in slots], axis=1)
        for comp, slots in tiles
    ]
    high, low = split2(jnp.concatenate(rows, axis=0))
    return jnp.dot(jnp.concatenate([high, low, high], axis=1), matrix, preferred_element_type=F32)


def sect_cells(first):
    return [0, 1, 2, 3, jnp.where(first, 4, -2), jnp.where(first, 5, -1), OUTSIDE, OUTSIDE]


def sent_kernel(
    fine_hbm, taps_hbm, near_ref, far_ref, fine_ref, own_matrix_ref, stream_ref, taps_ref, plane_ref, sems
):
    taps_copy, *copies = start_copies([(taps_hbm, taps_ref)] + cells_of(fine_hbm, fine_ref), sems)
    even = lax.axis_index("span") % 2 == 0
    span_cells = [jnp.where(even, at, at - 6) for at in (4, 5)] + [jnp.where(even, at - 6, at) for at in (4, 5)]
    taps_copy.wait()
    sect = sect_cells(lax.axis_index("sect") == 0)
    matrix = plane_matrix(span_cells, sect, taps_ref)
    stream_ref[...] = stream_matrix(taps_ref)
    own_matrix_ref[...] = plane_matrix([0, 1, 2, 3], sect, taps_ref)
    filter_plane(matrix, fine_ref, plane_ref, copies)
    matrix = stream_ref[...]
    for base, out_ref in ((0, near_ref), (2, far_ref)):
        tiles = [
            (comp, [(base + s, 2 * pair + k) for k in range(2) for s in range(2)])
            for comp in range(3)
            for pair in range(3)
        ]
        result = filter_stream(plane_ref, tiles, matrix)
        for t in range(len(tiles)):
            out_ref[t] = result[8 * t : 8 * t + 8]


def fold(gram, kept_ref, sent_ref, first):
    row, col = iota((LANES, LANES), 0), iota((LANES, LANES), 1)
    across, lower = gram[LANES:, :LANES], gram[LANES:, LANES:]
    packed = jnp.where(row <= col, gram[:LANES, :LANES], lower)
    corner = jnp.sum(jnp.where(row == col, lower, 0.0), axis=0, keepdims=True)
    corner = jnp.broadcast_to(corner, (8, LANES))
    kept_ref[:LANES] = jnp.where(first, packed, across)
    kept_ref[LANES:] = corner
    sent_ref[:LANES] = jnp.where(first, across, packed)
    sent_ref[LANES:] = corner


def own_kernel(
    total, stored_hbm, fine_ref, matrix_ref, stream_ref, own_ref, kept_ref, sent_ref, stored_ref, plane_ref, sems
):
    (copy,) = start_copies([(stored_hbm, stored_ref)], sems)
    filter_plane(matrix_ref[...], fine_ref, plane_ref)
    tiles = [(comp, [(s, k) for s in range(4)]) for comp in range(3) for k in range(6)]
    result = filter_stream(plane_ref, tiles, stream_ref[...])
    for t in range(len(tiles)):
        own_ref[t] = result[8 * t : 8 * t + 8]
    copy.wait()
    old, cells = stored_ref.shape
    rows = jnp.concatenate([stored_ref[...], jnp.zeros((8, cells), BF16)], axis=0)
    gram = lax.dot_general(rows, rows, (((1,), (1,)), ((), ())), preferred_element_type=F32) / total
    fold(gram, kept_ref, sent_ref, lax.axis_index("sect") == 0)


def place_shares(shares, before):
    lane = iota((8, LANES), 1)
    turned = pltpu.roll(shares, 64, 1)
    here = jnp.where(before, lane, LANES - 1 - lane) < 64
    return [jnp.where(here, jnp.where(before == (k == 0), shares, turned), 0.0) for k in range(2)]


def join_far_kernel(own_ref, far_ref, cells_ref):
    before = lax.axis_index("span") % 2 == 0
    for comp in range(3):
        for pair in range(3):
            shares = place_shares(far_ref[3 * comp + pair], before)
            for k in range(2):
                at = 6 * comp + 2 * pair + k
                cells_ref[at] = own_ref[at] + shares[k]


def join_near_kernel(own_ref, near_ref, sent_ref, cells_ref, swap_ref):
    before = lax.axis_index("span") % 2 == 1
    half = sent_ref.shape[0]
    swap_ref[:half] = sent_ref[...]
    for comp in range(3):
        for pair in range(3):
            shares = place_shares(near_ref[3 * comp + pair], before)
            for k in range(2):
                value = own_ref[6 * comp + 2 * pair + k] + shares[k]
                if pair < 2:
                    cells_ref[4 * comp + 2 * pair + k] = value
                else:
                    at = half + 8 * (2 * comp + k)
                    swap_ref[at : at + 8, :] = value


def new_kernel(total, stored_ref, cells_ref, partner_ref, kept_ref, coarse_ref, sums_ref):
    first = lax.axis_index("sect") == 0
    half = kept_ref.shape[0]
    cells = []
    for comp in range(3):
        for k in range(4):
            here = first if k >= 2 else jnp.logical_not(first)
            at = half + 8 * (2 * comp + k % 2)
            cells.append(cells_ref[4 * comp + k] + jnp.where(here, partner_ref[at : at + 8, :], 0.0))
    coarse = jnp.concatenate(cells, axis=1).astype(BF16)
    coarse_ref[...] = coarse
    rows = jnp.concatenate([stored_ref[...], coarse], axis=0)
    gram = lax.dot_general(coarse, rows, (((1,), (1,)), ((), ())), preferred_element_type=F32) / total
    sums_ref[:half] = kept_ref[...] + partner_ref[:half, :]
    sums_ref[half : half + 8] = gram[:, :LANES]
    sums_ref[half + 8 :] = gram[:, LANES:]


def eliminate(groups, at, lane, none, scale_ref):
    count = len(groups)
    width = groups[at].shape[1]
    wide = lambda column: jnp.concatenate([column] * (width // LANES), axis=1)
    spread = lambda values, k: jnp.broadcast_to(values[k : k + 1, :], (8, values.shape[1]))
    column = lambda g, j: jnp.broadcast_to(groups[g][:, lane + j : lane + j + 1], (8, LANES))
    sub = iota((8, LANES), 0)
    cols = {(j, g): column(g, j) for g in (at, at + 1) for j in range(8 * (g - at) + 8)}
    for g in (at, at + 1):
        cols[0, g] = cols[0, g] + none
    for k in range(16):
        home, k_sub = at + k // 8, k % 8
        for g in range(at + 2, count):
            step = NEAR if g < at + 4 else FAR
            if k % step == 0:
                for j in range(k, k + step):
                    cols[j, g] = column(g, j)
        scale = lax.rsqrt(spread(cols[k, home], k_sub))
        square = scale * scale
        scale_ref[8 * home + k_sub : 8 * home + k_sub + 1, :] = scale[k_sub : k_sub + 1, :]
        share = {g: cols[k, g] * square for g in range(home, count)}
        share[home] = jnp.where(sub > k_sub, share[home], 0.0)
        for j in range(k + 1, 16):
            j_home, j_sub = at + j // 8, j % 8
            head = spread(cols[k, j_home], j_sub)
            for g in range(j_home, count):
                step = 16 if g < at + 2 else NEAR if g < at + 4 else FAR
                if j // step == k // step:
                    if j == k + 1 and g == j_home:
                        cols[j, g] = cols[j, g] - (cols[k, g] * head) * square
                    else:
                        cols[j, g] = cols[j, g] - share[g] * head
        row = spread(groups[home], k_sub)
        for g in range(home, count):
            groups[g] = groups[g] - wide(share[g]) * row
    for g in (at, at + 1):
        groups[g] = groups[g] * wide(scale_ref[8 * g : 8 * g + 8, :])
    return groups


def factor_kernel(
    mine_ref, other_ref, stored_ref, coarse_ref, new_hbm, factor_hbm, basis_hbm,
    left_ref, inverse_ref, upper_ref, factor_ref, basis_ref, scale_ref, window_ref, sems,
):
    first = lax.axis_index("sect") == 0
    none = jnp.full((8, LANES), jnp.minimum(lax.axis_index("sect"), 0).astype(F32))
    size = left_ref.shape[0]
    row, col = iota((LANES, LANES), 0), iota((LANES, LANES), 1)
    packed = jnp.where(first, mine_ref[:LANES], other_ref[:LANES])
    across = jnp.where(first, other_ref[:LANES], mine_ref[:LANES])
    corner = jnp.where(first, mine_ref[LANES : LANES + 1], other_ref[LANES : LANES + 1])
    added = mine_ref[HALF : HALF + 8] + other_ref[HALF : HALF + 8]
    across = jnp.concatenate([across[:-8], across[-8:] + added], axis=0)
    added = mine_ref[HALF + 8 :] + other_ref[HALF + 8 :]
    added = jnp.concatenate([jnp.zeros((LANES - 8, LANES), F32), added], axis=0)
    corner = corner + jnp.sum(jnp.where(row == col, added, 0.0), axis=0, keepdims=True)
    packed = packed + jnp.where(row > col, added, 0.0)
    turned = packed.T
    copies = [pltpu.make_async_copy(coarse_ref, new_hbm, sems.at[0])]
    copies[0].start()
    window_ref[: size - 8, :] = stored_ref[...]
    window_ref[size - 8 :, :] = coarse_ref[...]
    left_ref[:LANES, :LANES] = jnp.where(row <= col, packed, turned)
    left_ref[:LANES, LANES:] = across.T
    left_ref[LANES:, :LANES] = jnp.zeros((LANES, LANES), F32)
    left_ref[LANES:, LANES:] = jnp.where(
        row == col, jnp.broadcast_to(corner, (LANES, LANES)), jnp.where(row < col, turned, packed)
    )
    inverse_ref[...] = jnp.where(iota((size, size), 0) == iota((size, size), 1), 1.0, 0.0)
    upper_ref[...] = jnp.zeros((size, size), F32)

    def send(source, target, begin, end):
        copies.append(pltpu.make_async_copy(source.at[begin:end], target.at[begin:end], sems.at[len(copies)]))
        copies[-1].start()

    for begin in range(0, size, PANEL):
        end = begin + PANEL
        skip = 0 if begin < LANES else LANES
        reach = LANES if end <= LANES else size
        groups = [
            jnp.concatenate([left_ref[g : g + 8, skip:], inverse_ref[g : g + 8, :reach]], axis=1)
            for g in range(begin, end, 8)
        ]
        for g in range(0, PANEL // 8, 2):
            groups = eliminate(groups, g, begin + 8 * g - skip, none, scale_ref)
        panel = jnp.concatenate(groups, axis=0)
        upper_ref[begin:end, skip:] = panel[:, : size - skip]
        if end < size:
            high, middle, low = split3(panel)
            right = jnp.concatenate([high, middle, high, low, high, middle], axis=0)
            lost = LANES if end == LANES else skip
            turned = panel[:, lost - skip : size - skip]
            turned = jnp.concatenate([turned, turned], axis=0).T[end - lost :, :]
            high = turned.astype(BF16).astype(F32)
            rest = turned - high
            middle = rest.astype(BF16).astype(F32)
            low = rest - middle
            early = iota(turned.shape, 1) < PANEL
            left = jnp.concatenate(
                [high, jnp.where(early, middle, high), jnp.where(early, low, middle)], axis=1
            ).astype(BF16)
            apart = lost - skip
            near = jnp.dot(left[:PANEL], right[:, apart : size - skip], preferred_element_type=F32)
            left_ref[end : end + PANEL, lost:] = left_ref[end : end + PANEL, lost:] - near
            near = jnp.dot(left[:PANEL], right[:, size - skip :], preferred_element_type=F32)
            inverse_ref[end : end + PANEL, :reach] = inverse_ref[end : end + PANEL, :reach] - near
            if end + PANEL < size:
                far = jnp.dot(left[PANEL:], right[:, apart:], preferred_element_type=F32)
                left_ref[end + PANEL :, lost:] = left_ref[end + PANEL :, lost:] - far[:, : size - lost]
                inverse_ref[end + PANEL :, :reach] = inverse_ref[end + PANEL :, :reach] - far[:, size - lost :]
        inverse = panel[:, size - skip :]
        inverse = jnp.where(iota(inverse.shape, 0) + begin >= iota(inverse.shape, 1), inverse, 0.0)
        high, low = split2(inverse)
        cells = window_ref[:reach, :]
        basis_ref[begin:end, :] = jnp.dot(
            jnp.concatenate([high, low], axis=1), jnp.concatenate([cells, cells], axis=0), preferred_element_type=F32
        )
        send(basis_ref, basis_hbm, begin, end)
        if end == LANES:
            factor_ref[:LANES, :LANES] = jnp.where(row >= col, upper_ref[:LANES, :LANES].T, 0.0)
            factor_ref[:LANES, LANES:] = jnp.zeros((LANES, LANES), F32)
            factor_ref[LANES:, :LANES] = upper_ref[:LANES, LANES:].T
            send(factor_ref, factor_hbm, 0, LANES)
    factor_ref[LANES:, LANES:] = jnp.where(row >= col, upper_ref[LANES:, LANES:].T, 0.0)
    send(factor_ref, factor_hbm, LANES, size)
    for copy in copies:
        copy.wait()


def factorise(mine, other, stored, coarse):
    old, rows_dev = stored.shape
    size = old + coarse.shape[0]
    return pl.pallas_call(
        factor_kernel,
        out_shape=[shaped(coarse.shape, BF16), shaped((size, size)), shaped((size, rows_dev))],
        in_specs=[VMEM] * 4,
        out_specs=[HBM] * 3,
        scratch_shapes=[pltpu.VMEM((size, size), F32)] * 4
        + [
            pltpu.VMEM((size, rows_dev), F32),
            pltpu.VMEM((PANEL, LANES), F32),
            pltpu.VMEM((size, rows_dev), BF16),
            pltpu.SemaphoreType.DMA((size // PANEL + 3,)),
        ],
        compiler_params=LIMIT,
        name="factor",
    )(mine, other, stored, coarse)


VMEM = pl.BlockSpec(memory_space=pltpu.VMEM)
HBM = pl.BlockSpec(memory_space=pltpu.HBM)
LIMIT = pltpu.CompilerParams(vmem_limit_bytes=48 * 2**20)


def shaped(shape, dtype=F32):
    return jax.ShapeDtypeStruct(shape, dtype)


def swap(values, axis, bit):
    count = lax.axis_size(axis)
    return lax.ppermute(values, axis, [(i, i ^ bit) for i in range(count)])


def swap_pairs(values, axis, begin):
    count = lax.axis_size(axis)
    pairs = [(i, i + 1) for i in range(begin, count - 1, 2)]
    return lax.ppermute(values, axis, pairs + [(j, i) for i, j in pairs])


def sum_over_span(values):
    count = lax.axis_size("span")
    if count & (count - 1):
        return lax.psum(values, "span")
    bit = 1
    while bit < count:
        if 2 * bit < count:
            first, second, third = (swap(values, "span", step * bit) for step in (1, 2, 3))
            values = (values + first) + (second + third)
        else:
            values = values + swap(values, "span", bit)
        bit *= 4
    return values


def local(fine_field, stored, filter_taps):
    snapshots, comps, cells_y, cells_z, cells_x = fine_field.shape
    assert (snapshots, comps, cells_y, cells_z, cells_x) == (8, 3, 16, 16, 128)
    assert lax.axis_size("sect") == 2
    old, rows_dev = stored.shape
    total = rows_dev * lax.axis_size("span") * lax.axis_size("sect")
    fields = snapshots * comps
    fine = fine_field.reshape(fields, cells_y * cells_z, cells_x)
    fine = pltpu.with_memory_space_constraint(fine, pltpu.HBM)
    taps = pltpu.with_memory_space_constraint(filter_taps, pltpu.HBM)
    plane = pltpu.VMEM((4, 8 * fields, LANES), F32)
    near, far, fine, matrix, stream = pl.pallas_call(
        sent_kernel,
        out_shape=[pltpu.VMEM((9, snapshots, LANES), F32)] * 2
        + [pltpu.VMEM(fine.shape, BF16), pltpu.VMEM((64, 256), BF16), pltpu.VMEM((12 * LANES, LANES), BF16)],
        in_specs=[HBM] * 2,
        out_specs=[VMEM] * 5,
        scratch_shapes=[pltpu.SMEM(taps.shape, F32), plane, pltpu.SemaphoreType.DMA((PARTS + 1,))],
        compiler_params=LIMIT,
        name="filter_sent",
    )(fine, taps)
    from_far = swap_pairs(far, "span", 1)
    from_near = swap_pairs(near, "span", 0)
    own, kept, sent, stored = pl.pallas_call(
        functools.partial(own_kernel, total),
        out_shape=[shaped((18, snapshots, LANES))]
        + [shaped((HALF, LANES))] * 2
        + [pltpu.VMEM(stored.shape, BF16)],
        in_specs=[HBM] + [VMEM] * 3,
        out_specs=[VMEM] * 4,
        scratch_shapes=[plane, pltpu.SemaphoreType.DMA((1,))],
        compiler_params=LIMIT,
        name="filter_own",
    )(pltpu.with_memory_space_constraint(stored, pltpu.HBM), fine, matrix, stream)
    own = pl.pallas_call(
        join_far_kernel,
        out_shape=shaped((18, snapshots, LANES)),
        in_specs=[VMEM] * 2,
        out_specs=VMEM,
        compiler_params=LIMIT,
        name="join_far",
    )(own, from_far)
    cells, crossing = pl.pallas_call(
        join_near_kernel,
        out_shape=[shaped((12, snapshots, LANES)), shaped((HALF + 6 * snapshots, LANES))],
        in_specs=[VMEM] * 3,
        out_specs=[VMEM] * 2,
        compiler_params=LIMIT,
        name="join_near",
    )(own, from_near, sent)
    coarse, sums = pl.pallas_call(
        functools.partial(new_kernel, total),
        out_shape=[shaped((snapshots, rows_dev), BF16), shaped((HALF + 2 * snapshots, LANES))],
        in_specs=[VMEM] * 4,
        out_specs=[VMEM] * 2,
        compiler_params=LIMIT,
        name="gram_new",
    )(stored, cells, swap(crossing, "sect", 1), kept)
    sums = sum_over_span(sums)
    return tuple(factorise(sums, swap(sums, "sect", 1), stored, coarse))


def solution(mesh):
    in_specs = (P("case", None, "sect", "span", None), P(None, ("case", "span", "sect")), P())
    out_specs = (
        P(None, ("case", "span", "sect")),
        P("case", None),
        P(None, ("case", "span", "sect")),
    )
    return jax.shard_map(local, mesh=mesh, in_specs=in_specs, out_specs=out_specs, check_vma=False)
```

```python
import functools

import jax
import jax.numpy as jnp
from jax import lax
from jax.experimental import pallas as pl
from jax.experimental.pallas import tpu as pltpu
from jax.sharding import PartitionSpec as P

F32 = jnp.float32
BF16 = jnp.bfloat16
TAPS = 17
LANES = 128
PANEL = 64
NEAR = 8
FAR = 8
PARTS = 2
OUTSIDE = -64
HALF = LANES


def iota(shape, dim):
    return lax.broadcasted_iota(jnp.int32, shape, dim)


def split2(values):
    high = values.astype(BF16)
    return high, (values - high.astype(F32)).astype(BF16)


def split3(values):
    high = values.astype(BF16)
    rest = values - high.astype(F32)
    middle = rest.astype(BF16)
    return high, middle, (rest - middle.astype(F32)).astype(BF16)


def weights_at(offset, taps_ref, row):
    total = jnp.zeros(offset.shape, F32)
    for tap in range(TAPS):
        total = jnp.where(offset == tap, taps_ref[row, tap], total)
    return total


def start_copies(pairs, sems):
    copies = [pltpu.make_async_copy(source, target, sems.at[i]) for i, (source, target) in enumerate(pairs)]
    for copy in copies:
        copy.start()
    return copies


def cells_of(fine_hbm, fine_ref):
    part = fine_ref.shape[0] // PARTS
    return [
        (fine_hbm.at[p * part : (p + 1) * part], fine_ref.at[p * part : (p + 1) * part]) for p in range(PARTS)
    ]


def plane_matrix(span_cells, sect_cells, taps_ref):
    row, cell = iota((8, 256), 0), iota((8, 256), 1)
    pick = lambda cells: sum(jnp.where(row == s, at, 0) for s, at in enumerate(cells))
    span = weights_at(cell % 16 - 4 * pick(span_cells) + 8, taps_ref, 1)
    sect = weights_at(cell // 16 - 4 * pick(sect_cells) + 8, taps_ref, 0)
    rows = [jnp.broadcast_to(span[s : s + 1], (8, 256)) * sect for s in range(len(span_cells))]
    return jnp.concatenate(split2(jnp.concatenate(rows, axis=0)), axis=0)


def stream_matrix(taps_ref):
    cell, lane = iota((LANES, LANES), 0), iota((LANES, LANES), 1)
    stream = weights_at(cell - 4 * (lane % 32) + 8, taps_ref, 2)
    high = stream.astype(BF16).astype(F32)
    parts = [
        jnp.concatenate([jnp.where(lane // 32 == s, term, 0.0) for s in range(4)], axis=0).astype(BF16)
        for term in (high, stream - high)
    ]
    return jnp.concatenate([parts[0], parts[0], parts[1]], axis=0)


def filter_plane(matrix, fine_ref, plane_ref, copies=None):
    part = fine_ref.shape[0] // PARTS
    half = matrix.shape[0] // 2
    for p in range(PARTS):
        if copies:
            copies[p].wait()
        for field in range(p * part, (p + 1) * part):
            both = jnp.dot(matrix, fine_ref[field], preferred_element_type=F32)
            summed = both[:half] + both[half:]
            for s in range(half // 8):
                plane_ref[s, 8 * field : 8 * field + 8, :] = summed[8 * s : 8 * s + 8]


def filter_stream(plane_ref, tiles, matrix):
    rows = [
        jnp.concatenate([plane_ref[s, pl.ds(8 * comp + k, 8, stride=24), :] for s, k in slots], axis=1)
        for comp, slots in tiles
    ]
    high, low = split2(jnp.concatenate(rows, axis=0))
    return jnp.dot(jnp.concatenate([high, low, high], axis=1), matrix, preferred_element_type=F32)


def sect_cells(first):
    return [0, 1, 2, 3, jnp.where(first, 4, -2), jnp.where(first, 5, -1), OUTSIDE, OUTSIDE]


def sent_kernel(
    fine_hbm, taps_hbm, near_ref, far_ref, fine_ref, own_matrix_ref, stream_ref, taps_ref, plane_ref, sems
):
    taps_copy, *copies = start_copies([(taps_hbm, taps_ref)] + cells_of(fine_hbm, fine_ref), sems)
    even = lax.axis_index("span") % 2 == 0
    span_cells = [jnp.where(even, at, at - 6) for at in (4, 5)] + [jnp.where(even, at - 6, at) for at in (4, 5)]
    taps_copy.wait()
    sect = sect_cells(lax.axis_index("sect") == 0)
    matrix = plane_matrix(span_cells, sect, taps_ref)
    stream_ref[...] = stream_matrix(taps_ref)
    own_matrix_ref[...] = plane_matrix([0, 1, 2, 3], sect, taps_ref)
    filter_plane(matrix, fine_ref, plane_ref, copies)
    matrix = stream_ref[...]
    for base, out_ref in ((0, near_ref), (2, far_ref)):
        tiles = [
            (comp, [(base + s, 2 * pair + k) for k in range(2) for s in range(2)])
            for comp in range(3)
            for pair in range(3)
        ]
        result = filter_stream(plane_ref, tiles, matrix)
        for t in range(len(tiles)):
            out_ref[t] = result[8 * t : 8 * t + 8]


def fold(gram, kept_ref, sent_ref, first):
    row, col = iota((LANES, LANES), 0), iota((LANES, LANES), 1)
    across, lower = gram[LANES:, :LANES], gram[LANES:, LANES:]
    corner = jnp.sum(jnp.where(row == col, lower, 0.0), axis=0, keepdims=True)
    packed = jnp.where(row <= col, gram[:LANES, :LANES], lower)
    packed = jnp.where(in_corner(row, col), jnp.broadcast_to(corner, (LANES, LANES)), packed)
    kept_ref[...] = jnp.where(first, packed, across)
    sent_ref[...] = jnp.where(first, across, packed)


def in_corner(row, col):
    return (row == LANES - 1) & (col < LANES - 8)


def own_kernel(
    total, stored_hbm, fine_ref, matrix_ref, stream_ref, own_ref, kept_ref, sent_ref, stored_ref, plane_ref, sems
):
    (copy,) = start_copies([(stored_hbm, stored_ref)], sems)
    filter_plane(matrix_ref[...], fine_ref, plane_ref)
    tiles = [(comp, [(s, k) for s in range(4)]) for comp in range(3) for k in range(6)]
    result = filter_stream(plane_ref, tiles, stream_ref[...])
    for t in range(len(tiles)):
        own_ref[t] = result[8 * t : 8 * t + 8]
    copy.wait()
    old, cells = stored_ref.shape
    rows = jnp.concatenate([stored_ref[...], jnp.zeros((8, cells), BF16)], axis=0)
    gram = lax.dot_general(rows, rows, (((1,), (1,)), ((), ())), preferred_element_type=F32) / total
    fold(gram, kept_ref, sent_ref, lax.axis_index("sect") == 0)


def place_shares(shares, before):
    lane = iota((8, LANES), 1)
    turned = pltpu.roll(shares, 64, 1)
    here = jnp.where(before, lane, LANES - 1 - lane) < 64
    return [jnp.where(here, jnp.where(before == (k == 0), shares, turned), 0.0) for k in range(2)]


def join_far_kernel(own_ref, far_ref, cells_ref):
    before = lax.axis_index("span") % 2 == 0
    for comp in range(3):
        for pair in range(3):
            shares = place_shares(far_ref[3 * comp + pair], before)
            for k in range(2):
                at = 6 * comp + 2 * pair + k
                cells_ref[at] = own_ref[at] + shares[k]


def join_near_kernel(own_ref, near_ref, sent_ref, cells_ref, swap_ref):
    before = lax.axis_index("span") % 2 == 1
    half = sent_ref.shape[0]
    swap_ref[:half] = sent_ref[...]
    for comp in range(3):
        for pair in range(3):
            shares = place_shares(near_ref[3 * comp + pair], before)
            for k in range(2):
                value = own_ref[6 * comp + 2 * pair + k] + shares[k]
                if pair < 2:
                    cells_ref[4 * comp + 2 * pair + k] = value
                else:
                    at = half + 8 * (2 * comp + k)
                    swap_ref[at : at + 8, :] = value


def new_kernel(total, stored_ref, cells_ref, partner_ref, kept_ref, coarse_ref, sums_ref):
    first = lax.axis_index("sect") == 0
    half = kept_ref.shape[0]
    cells = []
    for comp in range(3):
        for k in range(4):
            here = first if k >= 2 else jnp.logical_not(first)
            at = half + 8 * (2 * comp + k % 2)
            cells.append(cells_ref[4 * comp + k] + jnp.where(here, partner_ref[at : at + 8, :], 0.0))
    coarse = jnp.concatenate(cells, axis=1).astype(BF16)
    coarse_ref[...] = coarse
    rows = jnp.concatenate([stored_ref[...], coarse], axis=0)
    gram = lax.dot_general(coarse, rows, (((1,), (1,)), ((), ())), preferred_element_type=F32) / total
    sums_ref[:half] = kept_ref[...] + partner_ref[:half, :]
    sums_ref[half : half + 8] = gram[:, :LANES]
    sums_ref[half + 8 :] = gram[:, LANES:]


def eliminate(groups, at, lane, none, scale_ref):
    count = len(groups)
    width = groups[at].shape[1]
    wide = lambda column: jnp.concatenate([column] * (width // LANES), axis=1)
    spread = lambda values, k: jnp.broadcast_to(values[k : k + 1, :], (8, values.shape[1]))
    column = lambda g, j: jnp.broadcast_to(groups[g][:, lane + j : lane + j + 1], (8, LANES))
    sub = iota((8, LANES), 0)
    cols = {(j, g): column(g, j) for g in (at, at + 1) for j in range(8 * (g - at) + 8)}
    for g in (at, at + 1):
        cols[0, g] = cols[0, g] + none
    for k in range(16):
        home, k_sub = at + k // 8, k % 8
        for g in range(at + 2, count):
            step = NEAR if g < at + 4 else FAR
            if k % step == 0:
                for j in range(k, k + step):
                    cols[j, g] = column(g, j)
        scale = lax.rsqrt(spread(cols[k, home], k_sub))
        square = scale * scale
        scale_ref[8 * home + k_sub : 8 * home + k_sub + 1, :] = scale[k_sub : k_sub + 1, :]
        share = {g: cols[k, g] * square for g in range(home, count)}
        share[home] = jnp.where(sub > k_sub, share[home], 0.0)
        for j in range(k + 1, 16):
            j_home, j_sub = at + j // 8, j % 8
            head = spread(cols[k, j_home], j_sub)
            for g in range(j_home, count):
                step = 16 if g < at + 2 else NEAR if g < at + 4 else FAR
                if j // step == k // step:
                    if j == k + 1 and g == j_home:
                        cols[j, g] = cols[j, g] - (cols[k, g] * head) * square
                    else:
                        cols[j, g] = cols[j, g] - share[g] * head
        row = spread(groups[home], k_sub)
        for g in range(home, count):
            groups[g] = groups[g] - wide(share[g]) * row
    for g in (at, at + 1):
        groups[g] = groups[g] * wide(scale_ref[8 * g : 8 * g + 8, :])
    return groups


def factor_kernel(
    mine_ref, other_ref, stored_ref, coarse_ref, new_hbm, factor_hbm, basis_hbm,
    left_ref, inverse_ref, upper_ref, factor_ref, basis_ref, scale_ref, window_ref, sems,
):
    first = lax.axis_index("sect") == 0
    none = jnp.full((8, LANES), jnp.minimum(lax.axis_index("sect"), 0).astype(F32))
    size = left_ref.shape[0]
    row, col = iota((LANES, LANES), 0), iota((LANES, LANES), 1)
    packed = jnp.where(first, mine_ref[:LANES], other_ref[:LANES])
    across = jnp.where(first, other_ref[:LANES], mine_ref[:LANES])
    corner = jnp.where(col[:1] < LANES - 8, packed[LANES - 1 :], 0.0)
    packed = jnp.where(in_corner(row, col), 0.0, packed)
    added = mine_ref[HALF : HALF + 8] + other_ref[HALF : HALF + 8]
    across = jnp.concatenate([across[:-8], across[-8:] + added], axis=0)
    added = mine_ref[HALF + 8 :] + other_ref[HALF + 8 :]
    added = jnp.concatenate([jnp.zeros((LANES - 8, LANES), F32), added], axis=0)
    corner = corner + jnp.sum(jnp.where(row == col, added, 0.0), axis=0, keepdims=True)
    packed = packed + jnp.where(row > col, added, 0.0)
    turned = packed.T
    copies = [pltpu.make_async_copy(coarse_ref, new_hbm, sems.at[0])]
    copies[0].start()
    window_ref[: size - 8, :] = stored_ref[...]
    window_ref[size - 8 :, :] = coarse_ref[...]
    left_ref[:LANES, :LANES] = jnp.where(row <= col, packed, turned)
    left_ref[:LANES, LANES:] = across.T
    left_ref[LANES:, :LANES] = jnp.zeros((LANES, LANES), F32)
    left_ref[LANES:, LANES:] = jnp.where(
        row == col, jnp.broadcast_to(corner, (LANES, LANES)), jnp.where(row < col, turned, packed)
    )
    inverse_ref[...] = jnp.where(iota((size, size), 0) == iota((size, size), 1), 1.0, 0.0)
    upper_ref[...] = jnp.zeros((size, size), F32)

    def send(source, target, begin, end):
        copies.append(pltpu.make_async_copy(source.at[begin:end], target.at[begin:end], sems.at[len(copies)]))
        copies[-1].start()

    for begin in range(0, size, PANEL):
        end = begin + PANEL
        skip = 0 if begin < LANES else LANES
        reach = LANES if end <= LANES else size
        groups = [
            jnp.concatenate([left_ref[g : g + 8, skip:], inverse_ref[g : g + 8, :reach]], axis=1)
            for g in range(begin, end, 8)
        ]
        for g in range(0, PANEL // 8, 2):
            groups = eliminate(groups, g, begin + 8 * g - skip, none, scale_ref)
        panel = jnp.concatenate(groups, axis=0)
        upper_ref[begin:end, skip:] = panel[:, : size - skip]
        if end < size:
            high, middle, low = split3(panel)
            right = jnp.concatenate([high, middle, high, low, high, middle], axis=0)
            lost = LANES if end == LANES else skip
            turned = panel[:, lost - skip : size - skip]
            turned = jnp.concatenate([turned, turned], axis=0).T[end - lost :, :]
            high = turned.astype(BF16).astype(F32)
            rest = turned - high
            middle = rest.astype(BF16).astype(F32)
            low = rest - middle
            early = iota(turned.shape, 1) < PANEL
            left = jnp.concatenate(
                [high, jnp.where(early, middle, high), jnp.where(early, low, middle)], axis=1
            ).astype(BF16)
            apart = lost - skip
            near = jnp.dot(left[:PANEL], right[:, apart : size - skip], preferred_element_type=F32)
            left_ref[end : end + PANEL, lost:] = left_ref[end : end + PANEL, lost:] - near
            near = jnp.dot(left[:PANEL], right[:, size - skip :], preferred_element_type=F32)
            inverse_ref[end : end + PANEL, :reach] = inverse_ref[end : end + PANEL, :reach] - near
            if end + PANEL < size:
                far = jnp.dot(left[PANEL:], right[:, apart:], preferred_element_type=F32)
                left_ref[end + PANEL :, lost:] = left_ref[end + PANEL :, lost:] - far[:, : size - lost]
                inverse_ref[end + PANEL :, :reach] = inverse_ref[end + PANEL :, :reach] - far[:, size - lost :]
        inverse = panel[:, size - skip :]
        inverse = jnp.where(iota(inverse.shape, 0) + begin >= iota(inverse.shape, 1), inverse, 0.0)
        both = jnp.dot(
            jnp.concatenate(split2(inverse), axis=0), window_ref[:reach, :], preferred_element_type=F32
        )
        basis_ref[begin:end, :] = both[:PANEL] + both[PANEL:]
        send(basis_ref, basis_hbm, begin, end)
        if end == LANES:
            factor_ref[:LANES, :LANES] = jnp.where(row >= col, upper_ref[:LANES, :LANES].T, 0.0)
            factor_ref[:LANES, LANES:] = jnp.zeros((LANES, LANES), F32)
            factor_ref[LANES:, :LANES] = upper_ref[:LANES, LANES:].T
            send(factor_ref, factor_hbm, 0, LANES)
    factor_ref[LANES:, LANES:] = jnp.where(row >= col, upper_ref[LANES:, LANES:].T, 0.0)
    send(factor_ref, factor_hbm, LANES, size)
    for copy in copies:
        copy.wait()


def factorise(mine, other, stored, coarse):
    old, rows_dev = stored.shape
    size = old + coarse.shape[0]
    return pl.pallas_call(
        factor_kernel,
        out_shape=[shaped(coarse.shape, BF16), shaped((size, size)), shaped((size, rows_dev))],
        in_specs=[VMEM] * 4,
        out_specs=[HBM] * 3,
        scratch_shapes=[pltpu.VMEM((size, size), F32)] * 4
        + [
            pltpu.VMEM((size, rows_dev), F32),
            pltpu.VMEM((PANEL, LANES), F32),
            pltpu.VMEM((size, rows_dev), BF16),
            pltpu.SemaphoreType.DMA((size // PANEL + 3,)),
        ],
        compiler_params=LIMIT,
        name="factor",
    )(mine, other, stored, coarse)


VMEM = pl.BlockSpec(memory_space=pltpu.VMEM)
HBM = pl.BlockSpec(memory_space=pltpu.HBM)
LIMIT = pltpu.CompilerParams(vmem_limit_bytes=48 * 2**20)


def shaped(shape, dtype=F32):
    return jax.ShapeDtypeStruct(shape, dtype)


def swap(values, axis, bit):
    count = lax.axis_size(axis)
    return lax.ppermute(values, axis, [(i, i ^ bit) for i in range(count)])


def swap_pairs(values, axis, begin):
    count = lax.axis_size(axis)
    pairs = [(i, i + 1) for i in range(begin, count - 1, 2)]
    return lax.ppermute(values, axis, pairs + [(j, i) for i, j in pairs])


def sum_over_span(values):
    count = lax.axis_size("span")
    if count & (count - 1):
        return lax.psum(values, "span")
    bit = 1
    while bit < count:
        if 2 * bit < count:
            first, second, third = (swap(values, "span", step * bit) for step in (1, 2, 3))
            values = (values + first) + (second + third)
        else:
            values = values + swap(values, "span", bit)
        bit *= 4
    return values


def local(fine_field, stored, filter_taps):
    snapshots, comps, cells_y, cells_z, cells_x = fine_field.shape
    assert (snapshots, comps, cells_y, cells_z, cells_x) == (8, 3, 16, 16, 128)
    assert lax.axis_size("sect") == 2
    old, rows_dev = stored.shape
    total = rows_dev * lax.axis_size("span") * lax.axis_size("sect")
    fields = snapshots * comps
    fine = fine_field.reshape(fields, cells_y * cells_z, cells_x)
    fine = pltpu.with_memory_space_constraint(fine, pltpu.HBM)
    taps = pltpu.with_memory_space_constraint(filter_taps, pltpu.HBM)
    plane = pltpu.VMEM((4, 8 * fields, LANES), F32)
    near, far, fine, matrix, stream = pl.pallas_call(
        sent_kernel,
        out_shape=[pltpu.VMEM((9, snapshots, LANES), F32)] * 2
        + [pltpu.VMEM(fine.shape, BF16), pltpu.VMEM((64, 256), BF16), pltpu.VMEM((12 * LANES, LANES), BF16)],
        in_specs=[HBM] * 2,
        out_specs=[VMEM] * 5,
        scratch_shapes=[pltpu.SMEM(taps.shape, F32), plane, pltpu.SemaphoreType.DMA((PARTS + 1,))],
        compiler_params=LIMIT,
        name="filter_sent",
    )(fine, taps)
    from_far = swap_pairs(far, "span", 1)
    from_near = swap_pairs(near, "span", 0)
    own, kept, sent, stored = pl.pallas_call(
        functools.partial(own_kernel, total),
        out_shape=[shaped((18, snapshots, LANES))]
        + [shaped((HALF, LANES))] * 2
        + [pltpu.VMEM(stored.shape, BF16)],
        in_specs=[HBM] + [VMEM] * 3,
        out_specs=[VMEM] * 4,
        scratch_shapes=[plane, pltpu.SemaphoreType.DMA((1,))],
        compiler_params=LIMIT,
        name="filter_own",
    )(pltpu.with_memory_space_constraint(stored, pltpu.HBM), fine, matrix, stream)
    own = pl.pallas_call(
        join_far_kernel,
        out_shape=shaped((18, snapshots, LANES)),
        in_specs=[VMEM] * 2,
        out_specs=VMEM,
        compiler_params=LIMIT,
        name="join_far",
    )(own, from_far)
    cells, crossing = pl.pallas_call(
        join_near_kernel,
        out_shape=[shaped((12, snapshots, LANES)), shaped((HALF + 6 * snapshots, LANES))],
        in_specs=[VMEM] * 3,
        out_specs=[VMEM] * 2,
        compiler_params=LIMIT,
        name="join_near",
    )(own, from_near, sent)
    coarse, sums = pl.pallas_call(
        functools.partial(new_kernel, total),
        out_shape=[shaped((snapshots, rows_dev), BF16), shaped((HALF + 2 * snapshots, LANES))],
        in_specs=[VMEM] * 4,
        out_specs=[VMEM] * 2,
        compiler_params=LIMIT,
        name="gram_new",
    )(stored, cells, swap(crossing, "sect", 1), kept)
    sums = sum_over_span(sums)
    return tuple(factorise(sums, swap(sums, "sect", 1), stored, coarse))


def solution(mesh):
    in_specs = (P("case", None, "sect", "span", None), P(None, ("case", "span", "sect")), P())
    out_specs = (
        P(None, ("case", "span", "sect")),
        P("case", None),
        P(None, ("case", "span", "sect")),
    )
    return jax.shard_map(local, mesh=mesh, in_specs=in_specs, out_specs=out_specs, check_vma=False)
```

```python
import functools

import jax
import jax.numpy as jnp
from jax import lax
from jax.experimental import pallas as pl
from jax.experimental.pallas import tpu as pltpu
from jax.sharding import PartitionSpec as P

F32 = jnp.float32
BF16 = jnp.bfloat16
TAPS = 17
LANES = 128
PANEL = 64
NEAR = 16
FAR = 16
AHEAD = 3
PARTS = 2
OUTSIDE = -64
HALF = LANES


def iota(shape, dim):
    return lax.broadcasted_iota(jnp.int32, shape, dim)


def split2(values):
    high = values.astype(BF16)
    return high, (values - high.astype(F32)).astype(BF16)


def split3(values):
    high = values.astype(BF16)
    rest = values - high.astype(F32)
    middle = rest.astype(BF16)
    return high, middle, (rest - middle.astype(F32)).astype(BF16)


def weights_at(offset, taps_ref, row):
    total = jnp.zeros(offset.shape, F32)
    for tap in range(TAPS):
        total = jnp.where(offset == tap, taps_ref[row, tap], total)
    return total


def start_copies(pairs, sems):
    copies = [pltpu.make_async_copy(source, target, sems.at[i]) for i, (source, target) in enumerate(pairs)]
    for copy in copies:
        copy.start()
    return copies


def cells_of(fine_hbm, fine_ref):
    part = fine_ref.shape[0] // PARTS
    return [
        (fine_hbm.at[p * part : (p + 1) * part], fine_ref.at[p * part : (p + 1) * part]) for p in range(PARTS)
    ]


def plane_matrix(span_cells, sect_cells, taps_ref):
    row, cell = iota((8, 256), 0), iota((8, 256), 1)
    pick = lambda cells: sum(jnp.where(row == s, at, 0) for s, at in enumerate(cells))
    span = weights_at(cell % 16 - 4 * pick(span_cells) + 8, taps_ref, 1)
    sect = weights_at(cell // 16 - 4 * pick(sect_cells) + 8, taps_ref, 0)
    rows = [jnp.broadcast_to(span[s : s + 1], (8, 256)) * sect for s in range(len(span_cells))]
    return jnp.concatenate(split2(jnp.concatenate(rows, axis=0)), axis=0)


def stream_matrix(taps_ref):
    cell, lane = iota((LANES, LANES), 0), iota((LANES, LANES), 1)
    stream = weights_at(cell - 4 * (lane % 32) + 8, taps_ref, 2)
    high = stream.astype(BF16).astype(F32)
    parts = [
        jnp.concatenate([jnp.where(lane // 32 == s, term, 0.0) for s in range(4)], axis=0).astype(BF16)
        for term in (high, stream - high)
    ]
    return jnp.concatenate([parts[0], parts[0], parts[1]], axis=0)


def filter_plane(matrix, fine_ref, plane_ref, copies=None):
    part = fine_ref.shape[0] // PARTS
    half = matrix.shape[0] // 2
    for p in range(PARTS):
        if copies:
            copies[p].wait()
        for field in range(p * part, (p + 1) * part):
            both = jnp.dot(matrix, fine_ref[field], preferred_element_type=F32)
            summed = both[:half] + both[half:]
            for s in range(half // 8):
                plane_ref[s, 8 * field : 8 * field + 8, :] = summed[8 * s : 8 * s + 8]


def filter_stream(plane_ref, tiles, matrix):
    rows = [
        jnp.concatenate([plane_ref[s, pl.ds(8 * comp + k, 8, stride=24), :] for s, k in slots], axis=1)
        for comp, slots in tiles
    ]
    high, low = split2(jnp.concatenate(rows, axis=0))
    return jnp.dot(jnp.concatenate([high, low, high], axis=1), matrix, preferred_element_type=F32)


def sect_cells(first):
    return [0, 1, 2, 3, jnp.where(first, 4, -2), jnp.where(first, 5, -1), OUTSIDE, OUTSIDE]


def sent_kernel(
    fine_hbm, taps_hbm, stored_hbm, near_ref, far_ref, fine_ref, own_matrix_ref, stream_ref, stored_ref,
    taps_ref, plane_ref, sems,
):
    taps_copy, *copies, stored_copy = start_copies(
        [(taps_hbm, taps_ref)] + cells_of(fine_hbm, fine_ref) + [(stored_hbm, stored_ref)], sems
    )
    even = lax.axis_index("span") % 2 == 0
    span_cells = [jnp.where(even, at, at - 6) for at in (4, 5)] + [jnp.where(even, at - 6, at) for at in (4, 5)]
    taps_copy.wait()
    sect = sect_cells(lax.axis_index("sect") == 0)
    matrix = plane_matrix(span_cells, sect, taps_ref)
    stream_ref[...] = stream_matrix(taps_ref)
    own_matrix_ref[...] = plane_matrix([0, 1, 2, 3], sect, taps_ref)
    filter_plane(matrix, fine_ref, plane_ref, copies)
    matrix = stream_ref[...]
    for base, out_ref in ((0, near_ref), (2, far_ref)):
        tiles = [
            (comp, [(base + s, 2 * pair + k) for k in range(2) for s in range(2)])
            for comp in range(3)
            for pair in range(3)
        ]
        result = filter_stream(plane_ref, tiles, matrix)
        for t in range(len(tiles)):
            out_ref[t] = result[8 * t : 8 * t + 8]
    stored_copy.wait()


def fold(gram, kept_ref, sent_ref, first):
    row, col = iota((LANES, LANES), 0), iota((LANES, LANES), 1)
    across, lower = gram[LANES:, :LANES], gram[LANES:, LANES:]
    corner = jnp.sum(jnp.where(row == col, lower, 0.0), axis=0, keepdims=True)
    packed = jnp.where(row <= col, gram[:LANES, :LANES], lower)
    packed = jnp.where(in_corner(row, col), jnp.broadcast_to(corner, (LANES, LANES)), packed)
    kept_ref[...] = jnp.where(first, packed, across)
    sent_ref[...] = jnp.where(first, across, packed)


def in_corner(row, col):
    return (row == LANES - 1) & (col < LANES - 8)


def own_kernel(total, stored_ref, fine_ref, matrix_ref, stream_ref, own_ref, kept_ref, sent_ref, plane_ref):
    filter_plane(matrix_ref[...], fine_ref, plane_ref)
    tiles = [(comp, [(s, k) for s in range(4)]) for comp in range(3) for k in range(6)]
    result = filter_stream(plane_ref, tiles, stream_ref[...])
    for t in range(len(tiles)):
        own_ref[t] = result[8 * t : 8 * t + 8]
    old, cells = stored_ref.shape
    rows = jnp.concatenate([stored_ref[...], jnp.zeros((8, cells), BF16)], axis=0)
    gram = lax.dot_general(rows, rows, (((1,), (1,)), ((), ())), preferred_element_type=F32) / total
    fold(gram, kept_ref, sent_ref, lax.axis_index("sect") == 0)


def place_shares(shares, before):
    lane = iota((8, LANES), 1)
    turned = pltpu.roll(shares, 64, 1)
    here = jnp.where(before, lane, LANES - 1 - lane) < 64
    return [jnp.where(here, jnp.where(before == (k == 0), shares, turned), 0.0) for k in range(2)]


def join_far_kernel(own_ref, far_ref, cells_ref):
    before = lax.axis_index("span") % 2 == 0
    for comp in range(3):
        for pair in range(3):
            shares = place_shares(far_ref[3 * comp + pair], before)
            for k in range(2):
                at = 6 * comp + 2 * pair + k
                cells_ref[at] = own_ref[at] + shares[k]


def join_near_kernel(own_ref, near_ref, sent_ref, cells_ref, swap_ref):
    before = lax.axis_index("span") % 2 == 1
    half = sent_ref.shape[0]
    swap_ref[:half] = sent_ref[...]
    for comp in range(3):
        for pair in range(3):
            shares = place_shares(near_ref[3 * comp + pair], before)
            for k in range(2):
                value = own_ref[6 * comp + 2 * pair + k] + shares[k]
                if pair < 2:
                    cells_ref[4 * comp + 2 * pair + k] = value
                else:
                    at = half + 8 * (2 * comp + k)
                    swap_ref[at : at + 8, :] = value


def new_kernel(total, stored_ref, cells_ref, partner_ref, kept_ref, coarse_ref, sums_ref):
    first = lax.axis_index("sect") == 0
    half = kept_ref.shape[0]
    cells = []
    for comp in range(3):
        for k in range(4):
            here = first if k >= 2 else jnp.logical_not(first)
            at = half + 8 * (2 * comp + k % 2)
            cells.append(cells_ref[4 * comp + k] + jnp.where(here, partner_ref[at : at + 8, :], 0.0))
    coarse = jnp.concatenate(cells, axis=1).astype(BF16)
    coarse_ref[...] = coarse
    rows = jnp.concatenate([stored_ref[...], coarse], axis=0)
    gram = lax.dot_general(coarse, rows, (((1,), (1,)), ((), ())), preferred_element_type=F32) / total
    sums_ref[:half] = kept_ref[...] + partner_ref[:half, :]
    sums_ref[half : half + 8] = gram[:, :LANES]
    sums_ref[half + 8 :] = gram[:, LANES:]


def eliminate(active, lead, lane, parts, none, scale_ref):
    spread = lambda values, k: jnp.broadcast_to(values[k : k + 1, :], (8, LANES))
    column = lambda g, j: jnp.broadcast_to(active[g][lead][:, lane + j : lane + j + 1], (8, LANES))
    sub = iota((8, LANES), 0)
    cols = {(j, g): column(g, j) for g in (0, 1) for j in range(8 * g + 8)}
    for g in (0, 1):
        cols[0, g] = cols[0, g] + none
    for k in range(16):
        home, k_sub = k // 8, k % 8
        for g in range(2, len(active)):
            step = NEAR if g < 4 else FAR
            if k % step == 0:
                for j in range(k, k + step):
                    cols[j, g] = column(g, j)
        scale = lax.rsqrt(spread(cols[k, home], k_sub))
        square = scale * scale
        scale_ref[k : k + 1, :] = scale[k_sub : k_sub + 1, :]
        share = {g: cols[k, g] * square for g in range(home, len(active))}
        share[home] = jnp.where(sub > k_sub, share[home], 0.0)
        for j in range(k + 1, 16):
            j_home, j_sub = j // 8, j % 8
            head = spread(cols[k, j_home], j_sub)
            for g in range(j_home, len(active)):
                step = 16 if g < 2 else NEAR if g < 4 else FAR
                if j // step == k // step:
                    if j == k + 1 and g == j_home:
                        cols[j, g] = cols[j, g] - (cols[k, g] * head) * square
                    else:
                        cols[j, g] = cols[j, g] - share[g] * head
        for v in parts:
            row = spread(active[home][v], k_sub)
            for g in range(home, len(active) if v < 2 else min(len(active), 4)):
                active[g][v] = active[g][v] - share[g] * row
    for g in (0, 1):
        for v in parts:
            active[g][v] = active[g][v] * scale_ref[8 * g : 8 * g + 8, :]


def factor_kernel(
    mine_ref, other_ref, stored_ref, coarse_ref, new_hbm, factor_hbm, basis_hbm,
    work_ref, upper_ref, inverse_ref, factor_ref, basis_ref, scale_ref, window_ref, sems,
):
    first = lax.axis_index("sect") == 0
    none = jnp.full((8, LANES), jnp.minimum(lax.axis_index("sect"), 0).astype(F32))
    size = work_ref.shape[0]
    copies = []

    def send(source, target):
        copies.append(pltpu.make_async_copy(source, target, sems.at[len(copies)]))
        copies[-1].start()

    send(coarse_ref, new_hbm)
    row, col = iota((LANES, LANES), 0), iota((LANES, LANES), 1)
    packed = jnp.where(first, mine_ref[:LANES], other_ref[:LANES])
    across = jnp.where(first, other_ref[:LANES], mine_ref[:LANES])
    corner = jnp.where(col[:1] < LANES - 8, packed[LANES - 1 :], 0.0)
    packed = jnp.where(in_corner(row, col), 0.0, packed)
    added = mine_ref[HALF : HALF + 8] + other_ref[HALF : HALF + 8]
    across = jnp.concatenate([across[:-8], across[-8:] + added], axis=0)
    added = mine_ref[HALF + 8 :] + other_ref[HALF + 8 :]
    added = jnp.concatenate([jnp.zeros((LANES - 8, LANES), F32), added], axis=0)
    corner = corner + jnp.sum(jnp.where(row == col, added, 0.0), axis=0, keepdims=True)
    packed = packed + jnp.where(row > col, added, 0.0)
    turned = packed.T
    work_ref[:LANES, :LANES] = jnp.where(row <= col, packed, turned)
    work_ref[:LANES, LANES:size] = across.T
    work_ref[LANES:, :LANES] = across
    work_ref[LANES:, LANES:size] = jnp.where(
        row == col, jnp.broadcast_to(corner, (LANES, LANES)), jnp.where(row < col, turned, packed)
    )
    work_ref[:, size:] = jnp.where(iota((size, size), 0) == iota((size, size), 1), 1.0, 0.0)
    window_ref[: size - 8, :] = stored_ref[...]
    window_ref[size - 8 :, :] = coarse_ref[...]
    upper_ref[...] = jnp.zeros((size, size), F32)
    inverse_ref[...] = jnp.zeros((size, size), F32)
    fetch = lambda at: [work_ref[at : at + 8, LANES * v : LANES * (v + 1)] for v in range(4)]
    active = [fetch(g) for g in range(0, 16 * AHEAD, 8)]
    for begin in range(0, size, 16):
        lead = begin // LANES
        parts = (0, 1, 2) if lead == 0 else (1, 2, 3)
        for i in range(0 if begin == 0 else 2, min(len(active), 4)):
            at = begin + 8 * i
            for v in (2, 3):
                active[i][v] = work_ref[at : at + 8, LANES * v : LANES * (v + 1)]
        eliminate(active, lead, begin % LANES, parts, none, scale_ref)
        done = {v: jnp.concatenate([active[0][v], active[1][v]], axis=0) for v in parts}
        active = active[2:]
        for v in parts:
            target, at = (upper_ref, v) if v < 2 else (inverse_ref, v - 2)
            target[begin : begin + 16, LANES * at : LANES * (at + 1)] = done[v]
        far, near = begin + 16 * AHEAD, begin + 32
        if near < size:
            terms = {v: split3(done[v]) for v in parts}
            right = jnp.concatenate(
                [jnp.concatenate([terms[v][t] for v in parts], axis=1) for t in (0, 1, 0, 2, 0, 1)], axis=0
            )
            left = []
            for v in range(near // LANES, 2):
                stack = jnp.concatenate([terms[v][t].astype(F32) for t in (0, 0, 1, 0, 2, 1)], axis=0)
                left.append(stack.T[max(near - LANES * v, 0) :].astype(BF16))
            share = jnp.dot(jnp.concatenate(left, axis=0), right, preferred_element_type=F32)
            for i, v in enumerate(parts):
                lanes = slice(LANES * v, LANES * (v + 1))
                top = far if v < 2 else near
                if top < size:
                    work_ref[top:, lanes] = work_ref[top:, lanes] - share[top - near :, LANES * i : LANES * (i + 1)]
            if far < size:
                active += [fetch(far), fetch(far + 8)]
        end = begin + 16
        if end % PANEL == 0:
            reach = LANES if end <= LANES else size
            inverse = inverse_ref[end - PANEL : end, :reach]
            inverse = jnp.where(iota(inverse.shape, 0) + (end - PANEL) >= iota(inverse.shape, 1), inverse, 0.0)
            both = jnp.dot(
                jnp.concatenate(split2(inverse), axis=0), window_ref[:reach, :], preferred_element_type=F32
            )
            basis_ref[end - PANEL : end, :] = both[:PANEL] + both[PANEL:]
            send(basis_ref.at[end - PANEL : end], basis_hbm.at[end - PANEL : end])
        if end == LANES:
            factor_ref[:LANES, :LANES] = jnp.where(row >= col, upper_ref[:LANES, :LANES].T, 0.0)
            factor_ref[:LANES, LANES:] = jnp.zeros((LANES, LANES), F32)
            factor_ref[LANES:, :LANES] = upper_ref[:LANES, LANES:].T
            send(factor_ref.at[:LANES], factor_hbm.at[:LANES])
    factor_ref[LANES:, LANES:] = jnp.where(row >= col, upper_ref[LANES:, LANES:].T, 0.0)
    send(factor_ref.at[LANES:], factor_hbm.at[LANES:])
    for copy in copies:
        copy.wait()


def factorise(mine, other, stored, coarse):
    old, rows_dev = stored.shape
    size = old + coarse.shape[0]
    return pl.pallas_call(
        factor_kernel,
        out_shape=[shaped(coarse.shape, BF16), shaped((size, size)), shaped((size, rows_dev))],
        in_specs=[VMEM] * 4,
        out_specs=[HBM] * 3,
        scratch_shapes=[pltpu.VMEM((size, 2 * size), F32)]
        + [pltpu.VMEM((size, size), F32)] * 3
        + [
            pltpu.VMEM((size, rows_dev), F32),
            pltpu.VMEM((16, LANES), F32),
            pltpu.VMEM((size, rows_dev), BF16),
            pltpu.SemaphoreType.DMA((size // PANEL + 3,)),
        ],
        compiler_params=LIMIT,
        name="factor",
    )(mine, other, stored, coarse)


VMEM = pl.BlockSpec(memory_space=pltpu.VMEM)
HBM = pl.BlockSpec(memory_space=pltpu.HBM)
LIMIT = pltpu.CompilerParams(vmem_limit_bytes=48 * 2**20)


def shaped(shape, dtype=F32):
    return jax.ShapeDtypeStruct(shape, dtype)


def swap(values, axis, bit):
    count = lax.axis_size(axis)
    return lax.ppermute(values, axis, [(i, i ^ bit) for i in range(count)])


def swap_pairs(values, axis, begin):
    count = lax.axis_size(axis)
    pairs = [(i, i + 1) for i in range(begin, count - 1, 2)]
    return lax.ppermute(values, axis, pairs + [(j, i) for i, j in pairs])


def sum_over_span(values):
    count = lax.axis_size("span")
    if count & (count - 1):
        return lax.psum(values, "span")
    bit = 1
    while bit < count:
        if 2 * bit < count:
            first, second, third = (swap(values, "span", step * bit) for step in (1, 2, 3))
            values = (values + first) + (second + third)
        else:
            values = values + swap(values, "span", bit)
        bit *= 4
    return values


def local(fine_field, stored, filter_taps):
    snapshots, comps, cells_y, cells_z, cells_x = fine_field.shape
    assert (snapshots, comps, cells_y, cells_z, cells_x) == (8, 3, 16, 16, 128)
    assert lax.axis_size("sect") == 2
    old, rows_dev = stored.shape
    total = rows_dev * lax.axis_size("span") * lax.axis_size("sect")
    fields = snapshots * comps
    fine = fine_field.reshape(fields, cells_y * cells_z, cells_x)
    fine = pltpu.with_memory_space_constraint(fine, pltpu.HBM)
    taps = pltpu.with_memory_space_constraint(filter_taps, pltpu.HBM)
    plane = pltpu.VMEM((4, 8 * fields, LANES), F32)
    near, far, fine, matrix, stream, stored = pl.pallas_call(
        sent_kernel,
        out_shape=[pltpu.VMEM((9, snapshots, LANES), F32)] * 2
        + [pltpu.VMEM(fine.shape, BF16), pltpu.VMEM((64, 256), BF16), pltpu.VMEM((12 * LANES, LANES), BF16)]
        + [pltpu.VMEM(stored.shape, BF16)],
        in_specs=[HBM] * 3,
        out_specs=[VMEM] * 6,
        scratch_shapes=[pltpu.SMEM(taps.shape, F32), plane, pltpu.SemaphoreType.DMA((PARTS + 2,))],
        compiler_params=LIMIT,
        name="filter_sent",
    )(fine, taps, pltpu.with_memory_space_constraint(stored, pltpu.HBM))
    from_far = swap_pairs(far, "span", 1)
    from_near = swap_pairs(near, "span", 0)
    own, kept, sent = pl.pallas_call(
        functools.partial(own_kernel, total),
        out_shape=[shaped((18, snapshots, LANES))]
        + [shaped((HALF, LANES))] * 2,
        in_specs=[VMEM] * 4,
        out_specs=[VMEM] * 3,
        scratch_shapes=[plane],
        compiler_params=LIMIT,
        name="filter_own",
    )(stored, fine, matrix, stream)
    own = pl.pallas_call(
        join_far_kernel,
        out_shape=shaped((18, snapshots, LANES)),
        in_specs=[VMEM] * 2,
        out_specs=VMEM,
        compiler_params=LIMIT,
        name="join_far",
    )(own, from_far)
    cells, crossing = pl.pallas_call(
        join_near_kernel,
        out_shape=[shaped((12, snapshots, LANES)), shaped((HALF + 6 * snapshots, LANES))],
        in_specs=[VMEM] * 3,
        out_specs=[VMEM] * 2,
        compiler_params=LIMIT,
        name="join_near",
    )(own, from_near, sent)
    coarse, sums = pl.pallas_call(
        functools.partial(new_kernel, total),
        out_shape=[shaped((snapshots, rows_dev), BF16), shaped((HALF + 2 * snapshots, LANES))],
        in_specs=[VMEM] * 4,
        out_specs=[VMEM] * 2,
        compiler_params=LIMIT,
        name="gram_new",
    )(stored, cells, swap(crossing, "sect", 1), kept)
    sums = sum_over_span(sums)
    return tuple(factorise(sums, swap(sums, "sect", 1), stored, coarse))


def solution(mesh):
    in_specs = (P("case", None, "sect", "span", None), P(None, ("case", "span", "sect")), P())
    out_specs = (
        P(None, ("case", "span", "sect")),
        P("case", None),
        P(None, ("case", "span", "sect")),
    )
    return jax.shard_map(local, mesh=mesh, in_specs=in_specs, out_specs=out_specs, check_vma=False)
```

```python
import functools

import jax
import jax.numpy as jnp
from jax import lax
from jax.experimental import pallas as pl
from jax.experimental.pallas import tpu as pltpu
from jax.sharding import PartitionSpec as P

F32 = jnp.float32
BF16 = jnp.bfloat16
TAPS = 17
LANES = 128
PANEL = 64
NEAR = 16
FAR = 16
AHEAD = 3
PARTS = 2
OUTSIDE = -64
HALF = LANES


def iota(shape, dim):
    return lax.broadcasted_iota(jnp.int32, shape, dim)


def split2(values):
    high = values.astype(BF16)
    return high, (values - high.astype(F32)).astype(BF16)


def split3(values):
    high = values.astype(BF16)
    rest = values - high.astype(F32)
    middle = rest.astype(BF16)
    return high, middle, (rest - middle.astype(F32)).astype(BF16)


def weights_at(offset, taps_ref, row):
    total = jnp.zeros(offset.shape, F32)
    for tap in range(TAPS):
        total = jnp.where(offset == tap, taps_ref[row, tap], total)
    return total


def start_copies(pairs, sems):
    copies = [pltpu.make_async_copy(source, target, sems.at[i]) for i, (source, target) in enumerate(pairs)]
    for copy in copies:
        copy.start()
    return copies


def cells_of(fine_hbm, fine_ref):
    part = fine_ref.shape[0] // PARTS
    return [
        (fine_hbm.at[p * part : (p + 1) * part], fine_ref.at[p * part : (p + 1) * part]) for p in range(PARTS)
    ]


def plane_matrix(span_cells, sect_cells, taps_ref):
    row, cell = iota((8, 256), 0), iota((8, 256), 1)
    pick = lambda cells: sum(jnp.where(row == s, at, 0) for s, at in enumerate(cells))
    span = weights_at(cell % 16 - 4 * pick(span_cells) + 8, taps_ref, 1)
    sect = weights_at(cell // 16 - 4 * pick(sect_cells) + 8, taps_ref, 0)
    rows = [jnp.broadcast_to(span[s : s + 1], (8, 256)) * sect for s in range(len(span_cells))]
    return jnp.concatenate(split2(jnp.concatenate(rows, axis=0)), axis=0)


def stream_matrix(taps_ref):
    cell, lane = iota((LANES, LANES), 0), iota((LANES, LANES), 1)
    stream = weights_at(cell - 4 * (lane % 32) + 8, taps_ref, 2)
    high = stream.astype(BF16).astype(F32)
    parts = [
        jnp.concatenate([jnp.where(lane // 32 == s, term, 0.0) for s in range(4)], axis=0).astype(BF16)
        for term in (high, stream - high)
    ]
    return jnp.concatenate([parts[0], parts[0], parts[1]], axis=0)


def filter_plane(matrix, fine_ref, plane_ref, copies=None):
    part = fine_ref.shape[0] // PARTS
    half = matrix.shape[0] // 2
    for p in range(PARTS):
        if copies:
            copies[p].wait()
        for field in range(p * part, (p + 1) * part):
            both = jnp.dot(matrix, fine_ref[field], preferred_element_type=F32)
            summed = both[:half] + both[half:]
            for s in range(half // 8):
                plane_ref[s, 8 * field : 8 * field + 8, :] = summed[8 * s : 8 * s + 8]


def filter_stream(plane_ref, tiles, matrix):
    rows = [
        jnp.concatenate([plane_ref[s, pl.ds(8 * comp + k, 8, stride=24), :] for s, k in slots], axis=1)
        for comp, slots in tiles
    ]
    high, low = split2(jnp.concatenate(rows, axis=0))
    return jnp.dot(jnp.concatenate([high, low, high], axis=1), matrix, preferred_element_type=F32)


def sect_cells(first):
    return [0, 1, 2, 3, jnp.where(first, 4, -2), jnp.where(first, 5, -1), OUTSIDE, OUTSIDE]


def sent_kernel(
    fine_hbm, taps_hbm, stored_hbm, near_ref, far_ref, fine_ref, own_matrix_ref, stream_ref, stored_ref,
    taps_ref, plane_ref, sems,
):
    taps_copy, *copies, stored_copy = start_copies(
        [(taps_hbm, taps_ref)] + cells_of(fine_hbm, fine_ref) + [(stored_hbm, stored_ref)], sems
    )
    even = lax.axis_index("span") % 2 == 0
    span_cells = [jnp.where(even, at, at - 6) for at in (4, 5)] + [jnp.where(even, at - 6, at) for at in (4, 5)]
    taps_copy.wait()
    sect = sect_cells(lax.axis_index("sect") == 0)
    matrix = plane_matrix(span_cells, sect, taps_ref)
    stream_ref[...] = stream_matrix(taps_ref)
    own_matrix_ref[...] = plane_matrix([0, 1, 2, 3], sect, taps_ref)
    filter_plane(matrix, fine_ref, plane_ref, copies)
    matrix = stream_ref[...]
    for base, out_ref in ((0, near_ref), (2, far_ref)):
        tiles = [
            (comp, [(base + s, 2 * pair + k) for k in range(2) for s in range(2)])
            for comp in range(3)
            for pair in range(3)
        ]
        result = filter_stream(plane_ref, tiles, matrix)
        for t in range(len(tiles)):
            out_ref[t] = result[8 * t : 8 * t + 8]
    stored_copy.wait()


def fold(gram, kept_ref, sent_ref, first):
    row, col = iota((LANES, LANES), 0), iota((LANES, LANES), 1)
    across, lower = gram[LANES:, :LANES], gram[LANES:, LANES:]
    corner = jnp.sum(jnp.where(row == col, lower, 0.0), axis=0, keepdims=True)
    packed = jnp.where(row <= col, gram[:LANES, :LANES], lower)
    packed = jnp.where(in_corner(row, col), jnp.broadcast_to(corner, (LANES, LANES)), packed)
    kept_ref[...] = jnp.where(first, packed, across)
    sent_ref[...] = jnp.where(first, across, packed)


def in_corner(row, col):
    return (row == LANES - 1) & (col < LANES - 8)


def own_kernel(total, stored_ref, fine_ref, matrix_ref, stream_ref, own_ref, kept_ref, sent_ref, plane_ref):
    filter_plane(matrix_ref[...], fine_ref, plane_ref)
    tiles = [(comp, [(s, k) for s in range(4)]) for comp in range(3) for k in range(6)]
    result = filter_stream(plane_ref, tiles, stream_ref[...])
    for t in range(len(tiles)):
        own_ref[t] = result[8 * t : 8 * t + 8]
    old, cells = stored_ref.shape
    rows = jnp.concatenate([stored_ref[...], jnp.zeros((8, cells), BF16)], axis=0)
    gram = lax.dot_general(rows, rows, (((1,), (1,)), ((), ())), preferred_element_type=F32) / total
    fold(gram, kept_ref, sent_ref, lax.axis_index("sect") == 0)


def place_shares(shares, before):
    lane = iota((8, LANES), 1)
    turned = pltpu.roll(shares, 64, 1)
    here = jnp.where(before, lane, LANES - 1 - lane) < 64
    return [jnp.where(here, jnp.where(before == (k == 0), shares, turned), 0.0) for k in range(2)]


def join_far_kernel(own_ref, far_ref, cells_ref):
    before = lax.axis_index("span") % 2 == 0
    for comp in range(3):
        for pair in range(3):
            shares = place_shares(far_ref[3 * comp + pair], before)
            for k in range(2):
                at = 6 * comp + 2 * pair + k
                cells_ref[at] = own_ref[at] + shares[k]


def join_near_kernel(own_ref, near_ref, sent_ref, cells_ref, swap_ref):
    before = lax.axis_index("span") % 2 == 1
    half = sent_ref.shape[0]
    swap_ref[:half] = sent_ref[...]
    for comp in range(3):
        for pair in range(3):
            shares = place_shares(near_ref[3 * comp + pair], before)
            for k in range(2):
                value = own_ref[6 * comp + 2 * pair + k] + shares[k]
                if pair < 2:
                    cells_ref[4 * comp + 2 * pair + k] = value
                else:
                    at = half + 8 * (2 * comp + k)
                    swap_ref[at : at + 8, :] = value


def new_kernel(total, stored_ref, cells_ref, partner_ref, kept_ref, coarse_ref, sums_ref):
    first = lax.axis_index("sect") == 0
    half = kept_ref.shape[0]
    cells = []
    for comp in range(3):
        for k in range(4):
            here = first if k >= 2 else jnp.logical_not(first)
            at = half + 8 * (2 * comp + k % 2)
            cells.append(cells_ref[4 * comp + k] + jnp.where(here, partner_ref[at : at + 8, :], 0.0))
    coarse = jnp.concatenate(cells, axis=1).astype(BF16)
    coarse_ref[...] = coarse
    rows = jnp.concatenate([stored_ref[...], coarse], axis=0)
    gram = lax.dot_general(coarse, rows, (((1,), (1,)), ((), ())), preferred_element_type=F32) / total
    sums_ref[:half] = kept_ref[...] + partner_ref[:half, :]
    sums_ref[half : half + 8] = gram[:, :LANES]
    sums_ref[half + 8 :] = gram[:, LANES:]


def eliminate(active, lead, lane, parts, whole, none, scale_ref):
    spread = lambda values, k: jnp.broadcast_to(values[k : k + 1, :], (8, LANES))
    column = lambda g, j: jnp.broadcast_to(active[g][lead][:, lane + j : lane + j + 1], (8, LANES))
    sub = iota((8, LANES), 0)
    cols = {(j, g): column(g, j) for g in (0, 1) for j in range(8 * g + 8)}
    for g in (0, 1):
        cols[0, g] = cols[0, g] + none
    for k in range(16):
        home, k_sub = k // 8, k % 8
        for g in range(2, len(active)):
            step = NEAR if g < 4 else FAR
            if k % step == 0:
                for j in range(k, k + step):
                    cols[j, g] = column(g, j)
        scale = lax.rsqrt(spread(cols[k, home], k_sub))
        square = scale * scale
        scale_ref[k : k + 1, :] = scale[k_sub : k_sub + 1, :]
        share = {g: cols[k, g] * square for g in range(home, len(active))}
        share[home] = jnp.where(sub > k_sub, share[home], 0.0)
        for j in range(k + 1, 16):
            j_home, j_sub = j // 8, j % 8
            head = spread(cols[k, j_home], j_sub)
            for g in range(j_home, len(active)):
                step = 16 if g < 2 else NEAR if g < 4 else FAR
                if j // step == k // step:
                    if j == k + 1 and g == j_home:
                        cols[j, g] = cols[j, g] - (cols[k, g] * head) * square
                    else:
                        cols[j, g] = cols[j, g] - share[g] * head
        for v in parts:
            row = spread(active[home][v], k_sub)
            for g in range(home, len(active) if v in whole else min(len(active), 4)):
                active[g][v] = active[g][v] - share[g] * row
    for g in (0, 1):
        for v in parts:
            active[g][v] = active[g][v] * scale_ref[8 * g : 8 * g + 8, :]


def factor_kernel(
    mine_ref, other_ref, stored_ref, coarse_ref, new_hbm, factor_hbm, basis_hbm,
    work_ref, upper_ref, inverse_ref, factor_ref, basis_ref, scale_ref, window_ref, sems,
):
    first = lax.axis_index("sect") == 0
    none = jnp.full((8, LANES), jnp.minimum(lax.axis_index("sect"), 0).astype(F32))
    size = work_ref.shape[0]
    copies = []

    def send(source, target):
        copies.append(pltpu.make_async_copy(source, target, sems.at[len(copies)]))
        copies[-1].start()

    send(coarse_ref, new_hbm)
    row, col = iota((LANES, LANES), 0), iota((LANES, LANES), 1)
    packed = jnp.where(first, mine_ref[:LANES], other_ref[:LANES])
    across = jnp.where(first, other_ref[:LANES], mine_ref[:LANES])
    corner = jnp.where(col[:1] < LANES - 8, packed[LANES - 1 :], 0.0)
    packed = jnp.where(in_corner(row, col), 0.0, packed)
    added = mine_ref[HALF : HALF + 8] + other_ref[HALF : HALF + 8]
    across = jnp.concatenate([across[:-8], across[-8:] + added], axis=0)
    added = mine_ref[HALF + 8 :] + other_ref[HALF + 8 :]
    added = jnp.concatenate([jnp.zeros((LANES - 8, LANES), F32), added], axis=0)
    corner = corner + jnp.sum(jnp.where(row == col, added, 0.0), axis=0, keepdims=True)
    packed = packed + jnp.where(row > col, added, 0.0)
    turned = packed.T
    work_ref[:LANES, :LANES] = jnp.where(row <= col, packed, turned)
    work_ref[:LANES, LANES:size] = across.T
    work_ref[LANES:, :LANES] = across
    work_ref[LANES:, LANES:size] = jnp.where(
        row == col, jnp.broadcast_to(corner, (LANES, LANES)), jnp.where(row < col, turned, packed)
    )
    work_ref[:, size:] = jnp.where(iota((size, size), 0) == iota((size, size), 1), 1.0, 0.0)
    window_ref[: size - 8, :] = stored_ref[...]
    window_ref[size - 8 :, :] = coarse_ref[...]
    upper_ref[...] = jnp.zeros((size, size), F32)
    inverse_ref[...] = jnp.zeros((size, size), F32)
    fetch = lambda at: [work_ref[at : at + 8, LANES * v : LANES * (v + 1)] for v in range(4)]
    active = [fetch(g) for g in range(0, 16 * AHEAD, 8)]
    for begin in range(0, size, 16):
        lead = begin // LANES
        parts = (0, 1, 2) if lead == 0 else (1, 2, 3)
        for i in range(0 if begin == 0 else 2, min(len(active), 4)):
            at = begin + 8 * i
            for v in (2, 3) if begin > LANES - 16 else (1, 2, 3):
                active[i][v] = work_ref[at : at + 8, LANES * v : LANES * (v + 1)]
        whole = (0, 1) if begin == LANES - 16 else (lead,)
        eliminate(active, lead, begin % LANES, parts, whole, none, scale_ref)
        done = {v: jnp.concatenate([active[0][v], active[1][v]], axis=0) for v in parts}
        active = active[2:]
        for v in parts:
            target, at = (upper_ref, v) if v < 2 else (inverse_ref, v - 2)
            target[begin : begin + 16, LANES * at : LANES * (at + 1)] = done[v]
        far, near = begin + 16 * AHEAD, begin + 32
        if near < size:
            terms = {v: split3(done[v]) for v in parts}
            right = jnp.concatenate(
                [jnp.concatenate([terms[v][t] for v in parts], axis=1) for t in (0, 1, 0, 2, 0, 1)], axis=0
            )
            left = []
            for v in range(near // LANES, 2):
                stack = jnp.concatenate([terms[v][t].astype(F32) for t in (0, 0, 1, 0, 2, 1)], axis=0)
                left.append(stack.T[max(near - LANES * v, 0) :].astype(BF16))
            share = jnp.dot(jnp.concatenate(left, axis=0), right, preferred_element_type=F32)
            for i, v in enumerate(parts):
                lanes = slice(LANES * v, LANES * (v + 1))
                top = far if v in whole else near
                if top < size:
                    work_ref[top:, lanes] = work_ref[top:, lanes] - share[top - near :, LANES * i : LANES * (i + 1)]
            if far < size:
                active += [fetch(far), fetch(far + 8)]
        end = begin + 16
        if end % PANEL == 0:
            reach = LANES if end <= LANES else size
            inverse = inverse_ref[end - PANEL : end, :reach]
            inverse = jnp.where(iota(inverse.shape, 0) + (end - PANEL) >= iota(inverse.shape, 1), inverse, 0.0)
            both = jnp.dot(
                jnp.concatenate(split2(inverse), axis=0), window_ref[:reach, :], preferred_element_type=F32
            )
            basis_ref[end - PANEL : end, :] = both[:PANEL] + both[PANEL:]
            send(basis_ref.at[end - PANEL : end], basis_hbm.at[end - PANEL : end])
        if end == LANES:
            factor_ref[:LANES, :LANES] = jnp.where(row >= col, upper_ref[:LANES, :LANES].T, 0.0)
            factor_ref[:LANES, LANES:] = jnp.zeros((LANES, LANES), F32)
            factor_ref[LANES:, :LANES] = upper_ref[:LANES, LANES:].T
            send(factor_ref.at[:LANES], factor_hbm.at[:LANES])
    factor_ref[LANES:, LANES:] = jnp.where(row >= col, upper_ref[LANES:, LANES:].T, 0.0)
    send(factor_ref.at[LANES:], factor_hbm.at[LANES:])
    for copy in copies:
        copy.wait()


def factorise(mine, other, stored, coarse):
    old, rows_dev = stored.shape
    size = old + coarse.shape[0]
    return pl.pallas_call(
        factor_kernel,
        out_shape=[shaped(coarse.shape, BF16), shaped((size, size)), shaped((size, rows_dev))],
        in_specs=[VMEM] * 4,
        out_specs=[HBM] * 3,
        scratch_shapes=[pltpu.VMEM((size, 2 * size), F32)]
        + [pltpu.VMEM((size, size), F32)] * 3
        + [
            pltpu.VMEM((size, rows_dev), F32),
            pltpu.VMEM((16, LANES), F32),
            pltpu.VMEM((size, rows_dev), BF16),
            pltpu.SemaphoreType.DMA((size // PANEL + 3,)),
        ],
        compiler_params=LIMIT,
        name="factor",
    )(mine, other, stored, coarse)


VMEM = pl.BlockSpec(memory_space=pltpu.VMEM)
HBM = pl.BlockSpec(memory_space=pltpu.HBM)
LIMIT = pltpu.CompilerParams(vmem_limit_bytes=48 * 2**20)


def shaped(shape, dtype=F32):
    return jax.ShapeDtypeStruct(shape, dtype)


def swap(values, axis, bit):
    count = lax.axis_size(axis)
    return lax.ppermute(values, axis, [(i, i ^ bit) for i in range(count)])


def swap_pairs(values, axis, begin):
    count = lax.axis_size(axis)
    pairs = [(i, i + 1) for i in range(begin, count - 1, 2)]
    return lax.ppermute(values, axis, pairs + [(j, i) for i, j in pairs])


def sum_over_span(values):
    count = lax.axis_size("span")
    if count & (count - 1):
        return lax.psum(values, "span")
    bit = 1
    while bit < count:
        if 2 * bit < count:
            first, second, third = (swap(values, "span", step * bit) for step in (1, 2, 3))
            values = (values + first) + (second + third)
        else:
            values = values + swap(values, "span", bit)
        bit *= 4
    return values


def local(fine_field, stored, filter_taps):
    snapshots, comps, cells_y, cells_z, cells_x = fine_field.shape
    assert (snapshots, comps, cells_y, cells_z, cells_x) == (8, 3, 16, 16, 128)
    assert lax.axis_size("sect") == 2
    old, rows_dev = stored.shape
    total = rows_dev * lax.axis_size("span") * lax.axis_size("sect")
    fields = snapshots * comps
    fine = fine_field.reshape(fields, cells_y * cells_z, cells_x)
    fine = pltpu.with_memory_space_constraint(fine, pltpu.HBM)
    taps = pltpu.with_memory_space_constraint(filter_taps, pltpu.HBM)
    plane = pltpu.VMEM((4, 8 * fields, LANES), F32)
    near, far, fine, matrix, stream, stored = pl.pallas_call(
        sent_kernel,
        out_shape=[pltpu.VMEM((9, snapshots, LANES), F32)] * 2
        + [pltpu.VMEM(fine.shape, BF16), pltpu.VMEM((64, 256), BF16), pltpu.VMEM((12 * LANES, LANES), BF16)]
        + [pltpu.VMEM(stored.shape, BF16)],
        in_specs=[HBM] * 3,
        out_specs=[VMEM] * 6,
        scratch_shapes=[pltpu.SMEM(taps.shape, F32), plane, pltpu.SemaphoreType.DMA((PARTS + 2,))],
        compiler_params=LIMIT,
        name="filter_sent",
    )(fine, taps, pltpu.with_memory_space_constraint(stored, pltpu.HBM))
    from_far = swap_pairs(far, "span", 1)
    from_near = swap_pairs(near, "span", 0)
    own, kept, sent = pl.pallas_call(
        functools.partial(own_kernel, total),
        out_shape=[shaped((18, snapshots, LANES))]
        + [shaped((HALF, LANES))] * 2,
        in_specs=[VMEM] * 4,
        out_specs=[VMEM] * 3,
        scratch_shapes=[plane],
        compiler_params=LIMIT,
        name="filter_own",
    )(stored, fine, matrix, stream)
    own = pl.pallas_call(
        join_far_kernel,
        out_shape=shaped((18, snapshots, LANES)),
        in_specs=[VMEM] * 2,
        out_specs=VMEM,
        compiler_params=LIMIT,
        name="join_far",
    )(own, from_far)
    cells, crossing = pl.pallas_call(
        join_near_kernel,
        out_shape=[shaped((12, snapshots, LANES)), shaped((HALF + 6 * snapshots, LANES))],
        in_specs=[VMEM] * 3,
        out_specs=[VMEM] * 2,
        compiler_params=LIMIT,
        name="join_near",
    )(own, from_near, sent)
    coarse, sums = pl.pallas_call(
        functools.partial(new_kernel, total),
        out_shape=[shaped((snapshots, rows_dev), BF16), shaped((HALF + 2 * snapshots, LANES))],
        in_specs=[VMEM] * 4,
        out_specs=[VMEM] * 2,
        compiler_params=LIMIT,
        name="gram_new",
    )(stored, cells, swap(crossing, "sect", 1), kept)
    sums = sum_over_span(sums)
    return tuple(factorise(sums, swap(sums, "sect", 1), stored, coarse))


def solution(mesh):
    in_specs = (P("case", None, "sect", "span", None), P(None, ("case", "span", "sect")), P())
    out_specs = (
        P(None, ("case", "span", "sect")),
        P("case", None),
        P(None, ("case", "span", "sect")),
    )
    return jax.shard_map(local, mesh=mesh, in_specs=in_specs, out_specs=out_specs, check_vma=False)
```

```python
import functools

import jax
import jax.numpy as jnp
from jax import lax
from jax.experimental import pallas as pl
from jax.experimental.pallas import tpu as pltpu
from jax.sharding import PartitionSpec as P

F32 = jnp.float32
BF16 = jnp.bfloat16
TAPS = 17
LANES = 128
PANEL = 64
NEAR = 16
FAR = 16
AHEAD = 3
PARTS = 2
OUTSIDE = -64
HALF = LANES


def iota(shape, dim):
    return lax.broadcasted_iota(jnp.int32, shape, dim)


def split2(values):
    high = values.astype(BF16)
    return high, (values - high.astype(F32)).astype(BF16)


def split3(values):
    high = values.astype(BF16)
    rest = values - high.astype(F32)
    middle = rest.astype(BF16)
    return high, middle, (rest - middle.astype(F32)).astype(BF16)


def weights_at(offset, taps_ref, row):
    total = jnp.zeros(offset.shape, F32)
    for tap in range(TAPS):
        total = jnp.where(offset == tap, taps_ref[row, tap], total)
    return total


def start_copies(pairs, sems):
    copies = [pltpu.make_async_copy(source, target, sems.at[i]) for i, (source, target) in enumerate(pairs)]
    for copy in copies:
        copy.start()
    return copies


def cells_of(fine_hbm, fine_ref):
    part = fine_ref.shape[0] // PARTS
    return [
        (fine_hbm.at[p * part : (p + 1) * part], fine_ref.at[p * part : (p + 1) * part]) for p in range(PARTS)
    ]


def plane_matrix(span_cells, sect_cells, taps_ref):
    row, cell = iota((8, 256), 0), iota((8, 256), 1)
    pick = lambda cells: sum(jnp.where(row == s, at, 0) for s, at in enumerate(cells))
    span = weights_at(cell % 16 - 4 * pick(span_cells) + 8, taps_ref, 1)
    sect = weights_at(cell // 16 - 4 * pick(sect_cells) + 8, taps_ref, 0)
    rows = [jnp.broadcast_to(span[s : s + 1], (8, 256)) * sect for s in range(len(span_cells))]
    return jnp.concatenate(split2(jnp.concatenate(rows, axis=0)), axis=0)


def stream_matrix(taps_ref):
    cell, lane = iota((LANES, LANES), 0), iota((LANES, LANES), 1)
    stream = weights_at(cell - 4 * (lane % 32) + 8, taps_ref, 2)
    high = stream.astype(BF16).astype(F32)
    parts = [
        jnp.concatenate([jnp.where(lane // 32 == s, term, 0.0) for s in range(4)], axis=0).astype(BF16)
        for term in (high, stream - high)
    ]
    return jnp.concatenate([parts[0], parts[0], parts[1]], axis=0)


def filter_plane(matrix, fine_ref, plane_ref, copies=None):
    part = fine_ref.shape[0] // PARTS
    half = matrix.shape[0] // 2
    for p in range(PARTS):
        if copies:
            copies[p].wait()
        for field in range(p * part, (p + 1) * part):
            both = jnp.dot(matrix, fine_ref[field], preferred_element_type=F32)
            summed = both[:half] + both[half:]
            for s in range(half // 8):
                plane_ref[s, 8 * field : 8 * field + 8, :] = summed[8 * s : 8 * s + 8]


def filter_stream(plane_ref, tiles, matrix):
    rows = [
        jnp.concatenate([plane_ref[s, pl.ds(8 * comp + k, 8, stride=24), :] for s, k in slots], axis=1)
        for comp, slots in tiles
    ]
    high, low = split2(jnp.concatenate(rows, axis=0))
    return jnp.dot(jnp.concatenate([high, low, high], axis=1), matrix, preferred_element_type=F32)


def sect_cells(first):
    return [0, 1, 2, 3, jnp.where(first, 4, -2), jnp.where(first, 5, -1), OUTSIDE, OUTSIDE]


def sent_kernel(
    fine_hbm, taps_hbm, near_ref, far_ref, fine_ref, own_matrix_ref, stream_ref, taps_ref, plane_ref, sems
):
    taps_copy, *copies = start_copies([(taps_hbm, taps_ref)] + cells_of(fine_hbm, fine_ref), sems)
    even = lax.axis_index("span") % 2 == 0
    span_cells = [jnp.where(even, at, at - 6) for at in (4, 5)] + [jnp.where(even, at - 6, at) for at in (4, 5)]
    taps_copy.wait()
    sect = sect_cells(lax.axis_index("sect") == 0)
    matrix = plane_matrix(span_cells, sect, taps_ref)
    stream_ref[...] = stream_matrix(taps_ref)
    own_matrix_ref[...] = plane_matrix([0, 1, 2, 3], sect, taps_ref)
    filter_plane(matrix, fine_ref, plane_ref, copies)
    matrix = stream_ref[...]
    for base, out_ref in ((0, near_ref), (2, far_ref)):
        tiles = [
            (comp, [(base + s, 2 * pair + k) for k in range(2) for s in range(2)])
            for comp in range(3)
            for pair in range(3)
        ]
        result = filter_stream(plane_ref, tiles, matrix)
        for t in range(len(tiles)):
            out_ref[t] = result[8 * t : 8 * t + 8]


def fold(gram, kept_ref, sent_ref, first):
    row, col = iota((LANES, LANES), 0), iota((LANES, LANES), 1)
    across, lower = gram[LANES:, :LANES], gram[LANES:, LANES:]
    corner = jnp.sum(jnp.where(row == col, lower, 0.0), axis=0, keepdims=True)
    packed = jnp.where(row <= col, gram[:LANES, :LANES], lower)
    packed = jnp.where(in_corner(row, col), jnp.broadcast_to(corner, (LANES, LANES)), packed)
    kept_ref[...] = jnp.where(first, packed, across)
    sent_ref[...] = jnp.where(first, across, packed)


def in_corner(row, col):
    return (row == LANES - 1) & (col < LANES - 8)


def own_kernel(
    total, stored_hbm, fine_ref, matrix_ref, stream_ref, own_ref, kept_ref, sent_ref, stored_ref, plane_ref, sems
):
    (copy,) = start_copies([(stored_hbm, stored_ref)], sems)
    filter_plane(matrix_ref[...], fine_ref, plane_ref)
    tiles = [(comp, [(s, k) for s in range(4)]) for comp in range(3) for k in range(6)]
    result = filter_stream(plane_ref, tiles, stream_ref[...])
    for t in range(len(tiles)):
        own_ref[t] = result[8 * t : 8 * t + 8]
    copy.wait()
    old, cells = stored_ref.shape
    rows = jnp.concatenate([stored_ref[...], jnp.zeros((8, cells), BF16)], axis=0)
    gram = lax.dot_general(rows, rows, (((1,), (1,)), ((), ())), preferred_element_type=F32) / total
    fold(gram, kept_ref, sent_ref, lax.axis_index("sect") == 0)


def place_shares(shares, before):
    lane = iota((8, LANES), 1)
    turned = pltpu.roll(shares, 64, 1)
    here = jnp.where(before, lane, LANES - 1 - lane) < 64
    return [jnp.where(here, jnp.where(before == (k == 0), shares, turned), 0.0) for k in range(2)]


def join_far_kernel(own_ref, far_ref, cells_ref):
    before = lax.axis_index("span") % 2 == 0
    for comp in range(3):
        for pair in range(3):
            shares = place_shares(far_ref[3 * comp + pair], before)
            for k in range(2):
                at = 6 * comp + 2 * pair + k
                cells_ref[at] = own_ref[at] + shares[k]


def join_near_kernel(own_ref, near_ref, sent_ref, cells_ref, swap_ref):
    before = lax.axis_index("span") % 2 == 1
    half = sent_ref.shape[0]
    swap_ref[:half] = sent_ref[...]
    for comp in range(3):
        for pair in range(3):
            shares = place_shares(near_ref[3 * comp + pair], before)
            for k in range(2):
                value = own_ref[6 * comp + 2 * pair + k] + shares[k]
                if pair < 2:
                    cells_ref[4 * comp + 2 * pair + k] = value
                else:
                    at = half + 8 * (2 * comp + k)
                    swap_ref[at : at + 8, :] = value


def new_kernel(total, stored_ref, cells_ref, partner_ref, kept_ref, coarse_ref, sums_ref):
    first = lax.axis_index("sect") == 0
    half = kept_ref.shape[0]
    cells = []
    for comp in range(3):
        for k in range(4):
            here = first if k >= 2 else jnp.logical_not(first)
            at = half + 8 * (2 * comp + k % 2)
            cells.append(cells_ref[4 * comp + k] + jnp.where(here, partner_ref[at : at + 8, :], 0.0))
    coarse = jnp.concatenate(cells, axis=1).astype(BF16)
    coarse_ref[...] = coarse
    rows = jnp.concatenate([stored_ref[...], coarse], axis=0)
    gram = lax.dot_general(coarse, rows, (((1,), (1,)), ((), ())), preferred_element_type=F32) / total
    sums_ref[:half] = kept_ref[...] + partner_ref[:half, :]
    sums_ref[half : half + 8] = gram[:, :LANES]
    sums_ref[half + 8 :] = gram[:, LANES:]


def eliminate(active, lead, lane, parts, whole, none, scale_ref):
    spread = lambda values, k: jnp.broadcast_to(values[k : k + 1, :], (8, LANES))
    column = lambda g, j: jnp.broadcast_to(active[g][lead][:, lane + j : lane + j + 1], (8, LANES))
    sub = iota((8, LANES), 0)
    cols = {(j, g): column(g, j) for g in (0, 1) for j in range(8 * g + 8)}
    for g in (0, 1):
        cols[0, g] = cols[0, g] + none
    for k in range(16):
        home, k_sub = k // 8, k % 8
        for g in range(2, len(active)):
            step = NEAR if g < 4 else FAR
            if k % step == 0:
                for j in range(k, k + step):
                    cols[j, g] = column(g, j)
        scale = lax.rsqrt(spread(cols[k, home], k_sub))
        square = scale * scale
        scale_ref[k : k + 1, :] = scale[k_sub : k_sub + 1, :]
        share = {g: cols[k, g] * square for g in range(home, len(active))}
        share[home] = jnp.where(sub > k_sub, share[home], 0.0)
        for j in range(k + 1, 16):
            j_home, j_sub = j // 8, j % 8
            head = spread(cols[k, j_home], j_sub)
            for g in range(j_home, len(active)):
                step = 16 if g < 2 else NEAR if g < 4 else FAR
                if j // step == k // step:
                    if j == k + 1 and g == j_home:
                        cols[j, g] = cols[j, g] - (cols[k, g] * head) * square
                    else:
                        cols[j, g] = cols[j, g] - share[g] * head
        for v in parts:
            row = spread(active[home][v], k_sub)
            for g in range(home, len(active) if v in whole else min(len(active), 4)):
                active[g][v] = active[g][v] - share[g] * row
    for g in (0, 1):
        for v in parts:
            active[g][v] = active[g][v] * scale_ref[8 * g : 8 * g + 8, :]


def factor_kernel(
    mine_ref, other_ref, stored_ref, coarse_ref, new_hbm, factor_hbm, basis_hbm,
    work_ref, upper_ref, inverse_ref, factor_ref, basis_ref, scale_ref, window_ref, sems,
):
    first = lax.axis_index("sect") == 0
    none = jnp.full((8, LANES), jnp.minimum(lax.axis_index("sect"), 0).astype(F32))
    size = work_ref.shape[0]
    copies = []

    def send(source, target):
        copies.append(pltpu.make_async_copy(source, target, sems.at[len(copies)]))
        copies[-1].start()

    send(coarse_ref, new_hbm)
    row, col = iota((LANES, LANES), 0), iota((LANES, LANES), 1)
    packed = jnp.where(first, mine_ref[:LANES], other_ref[:LANES])
    across = jnp.where(first, other_ref[:LANES], mine_ref[:LANES])
    corner = jnp.where(col[:1] < LANES - 8, packed[LANES - 1 :], 0.0)
    packed = jnp.where(in_corner(row, col), 0.0, packed)
    added = mine_ref[HALF : HALF + 8] + other_ref[HALF : HALF + 8]
    across = jnp.concatenate([across[:-8], across[-8:] + added], axis=0)
    added = mine_ref[HALF + 8 :] + other_ref[HALF + 8 :]
    added = jnp.concatenate([jnp.zeros((LANES - 8, LANES), F32), added], axis=0)
    corner = corner + jnp.sum(jnp.where(row == col, added, 0.0), axis=0, keepdims=True)
    packed = packed + jnp.where(row > col, added, 0.0)
    turned = packed.T
    work_ref[:LANES, :LANES] = jnp.where(row <= col, packed, turned)
    work_ref[:LANES, LANES:size] = across.T
    work_ref[LANES:, :LANES] = across
    work_ref[LANES:, LANES:size] = jnp.where(
        row == col, jnp.broadcast_to(corner, (LANES, LANES)), jnp.where(row < col, turned, packed)
    )
    work_ref[:, size:] = jnp.where(iota((size, size), 0) == iota((size, size), 1), 1.0, 0.0)
    window_ref[: size - 8, :] = stored_ref[...]
    window_ref[size - 8 :, :] = coarse_ref[...]
    upper_ref[...] = jnp.zeros((size, size), F32)
    inverse_ref[...] = jnp.zeros((size, size), F32)
    fetch = lambda at: [work_ref[at : at + 8, LANES * v : LANES * (v + 1)] for v in range(4)]
    active = [fetch(g) for g in range(0, 16 * AHEAD, 8)]
    for begin in range(0, size, 16):
        lead = begin // LANES
        parts = (0, 1, 2) if lead == 0 else (1, 2, 3)
        for i in range(0 if begin == 0 else 2, min(len(active), 4)):
            at = begin + 8 * i
            for v in (2, 3) if begin > LANES - 16 else (1, 2, 3):
                active[i][v] = work_ref[at : at + 8, LANES * v : LANES * (v + 1)]
        whole = (0, 1) if begin == LANES - 16 else (lead,)
        eliminate(active, lead, begin % LANES, parts, whole, none, scale_ref)
        done = {v: jnp.concatenate([active[0][v], active[1][v]], axis=0) for v in parts}
        active = active[2:]
        for v in parts:
            target, at = (upper_ref, v) if v < 2 else (inverse_ref, v - 2)
            target[begin : begin + 16, LANES * at : LANES * (at + 1)] = done[v]
        far, near = begin + 16 * AHEAD, begin + 32
        if near < size:
            terms = {v: split3(done[v]) for v in parts}
            right = jnp.concatenate(
                [jnp.concatenate([terms[v][t] for v in parts], axis=1) for t in (0, 1, 0, 2, 0, 1)], axis=0
            )
            left = []
            for v in range(near // LANES, 2):
                stack = jnp.concatenate([terms[v][t].astype(F32) for t in (0, 0, 1, 0, 2, 1)], axis=0)
                left.append(stack.T[max(near - LANES * v, 0) :].astype(BF16))
            share = jnp.dot(jnp.concatenate(left, axis=0), right, preferred_element_type=F32)
            for i, v in enumerate(parts):
                lanes = slice(LANES * v, LANES * (v + 1))
                top = far if v in whole else near
                if top < size:
                    work_ref[top:, lanes] = work_ref[top:, lanes] - share[top - near :, LANES * i : LANES * (i + 1)]
            if far < size:
                active += [fetch(far), fetch(far + 8)]
        end = begin + 16
        if end % PANEL == 0:
            reach = LANES if end <= LANES else size
            inverse = inverse_ref[end - PANEL : end, :reach]
            inverse = jnp.where(iota(inverse.shape, 0) + (end - PANEL) >= iota(inverse.shape, 1), inverse, 0.0)
            both = jnp.dot(
                jnp.concatenate(split2(inverse), axis=0), window_ref[:reach, :], preferred_element_type=F32
            )
            basis_ref[end - PANEL : end, :] = both[:PANEL] + both[PANEL:]
            send(basis_ref.at[end - PANEL : end], basis_hbm.at[end - PANEL : end])
        if end == LANES:
            factor_ref[:LANES, :LANES] = jnp.where(row >= col, upper_ref[:LANES, :LANES].T, 0.0)
            factor_ref[:LANES, LANES:] = jnp.zeros((LANES, LANES), F32)
            factor_ref[LANES:, :LANES] = upper_ref[:LANES, LANES:].T
            send(factor_ref.at[:LANES], factor_hbm.at[:LANES])
    factor_ref[LANES:, LANES:] = jnp.where(row >= col, upper_ref[LANES:, LANES:].T, 0.0)
    send(factor_ref.at[LANES:], factor_hbm.at[LANES:])
    for copy in copies:
        copy.wait()


def factorise(mine, other, stored, coarse):
    old, rows_dev = stored.shape
    size = old + coarse.shape[0]
    return pl.pallas_call(
        factor_kernel,
        out_shape=[shaped(coarse.shape, BF16), shaped((size, size)), shaped((size, rows_dev))],
        in_specs=[VMEM] * 4,
        out_specs=[HBM] * 3,
        scratch_shapes=[pltpu.VMEM((size, 2 * size), F32)]
        + [pltpu.VMEM((size, size), F32)] * 3
        + [
            pltpu.VMEM((size, rows_dev), F32),
            pltpu.VMEM((16, LANES), F32),
            pltpu.VMEM((size, rows_dev), BF16),
            pltpu.SemaphoreType.DMA((size // PANEL + 3,)),
        ],
        compiler_params=LIMIT,
        name="factor",
    )(mine, other, stored, coarse)


VMEM = pl.BlockSpec(memory_space=pltpu.VMEM)
HBM = pl.BlockSpec(memory_space=pltpu.HBM)
LIMIT = pltpu.CompilerParams(vmem_limit_bytes=48 * 2**20)


def shaped(shape, dtype=F32):
    return jax.ShapeDtypeStruct(shape, dtype)


def swap(values, axis, bit):
    count = lax.axis_size(axis)
    return lax.ppermute(values, axis, [(i, i ^ bit) for i in range(count)])


def swap_pairs(values, axis, begin):
    count = lax.axis_size(axis)
    pairs = [(i, i + 1) for i in range(begin, count - 1, 2)]
    return lax.ppermute(values, axis, pairs + [(j, i) for i, j in pairs])


def sum_over_span(values):
    count = lax.axis_size("span")
    if count & (count - 1):
        return lax.psum(values, "span")
    bit = 1
    while bit < count:
        if 2 * bit < count:
            first, second, third = (swap(values, "span", step * bit) for step in (1, 2, 3))
            values = (values + first) + (second + third)
        else:
            values = values + swap(values, "span", bit)
        bit *= 4
    return values


def local(fine_field, stored, filter_taps):
    snapshots, comps, cells_y, cells_z, cells_x = fine_field.shape
    assert (snapshots, comps, cells_y, cells_z, cells_x) == (8, 3, 16, 16, 128)
    assert lax.axis_size("sect") == 2
    old, rows_dev = stored.shape
    total = rows_dev * lax.axis_size("span") * lax.axis_size("sect")
    fields = snapshots * comps
    fine = fine_field.reshape(fields, cells_y * cells_z, cells_x)
    fine = pltpu.with_memory_space_constraint(fine, pltpu.HBM)
    taps = pltpu.with_memory_space_constraint(filter_taps, pltpu.HBM)
    plane = pltpu.VMEM((4, 8 * fields, LANES), F32)
    near, far, fine, matrix, stream = pl.pallas_call(
        sent_kernel,
        out_shape=[pltpu.VMEM((9, snapshots, LANES), F32)] * 2
        + [pltpu.VMEM(fine.shape, BF16), pltpu.VMEM((64, 256), BF16), pltpu.VMEM((12 * LANES, LANES), BF16)],
        in_specs=[HBM] * 2,
        out_specs=[VMEM] * 5,
        scratch_shapes=[pltpu.SMEM(taps.shape, F32), plane, pltpu.SemaphoreType.DMA((PARTS + 1,))],
        compiler_params=LIMIT,
        name="filter_sent",
    )(fine, taps)
    from_far = swap_pairs(far, "span", 1)
    from_near = swap_pairs(near, "span", 0)
    own, kept, sent, stored = pl.pallas_call(
        functools.partial(own_kernel, total),
        out_shape=[shaped((18, snapshots, LANES))]
        + [shaped((HALF, LANES))] * 2
        + [pltpu.VMEM(stored.shape, BF16)],
        in_specs=[HBM] + [VMEM] * 3,
        out_specs=[VMEM] * 4,
        scratch_shapes=[plane, pltpu.SemaphoreType.DMA((1,))],
        compiler_params=LIMIT,
        name="filter_own",
    )(pltpu.with_memory_space_constraint(stored, pltpu.HBM), fine, matrix, stream)
    own = pl.pallas_call(
        join_far_kernel,
        out_shape=shaped((18, snapshots, LANES)),
        in_specs=[VMEM] * 2,
        out_specs=VMEM,
        compiler_params=LIMIT,
        name="join_far",
    )(own, from_far)
    cells, crossing = pl.pallas_call(
        join_near_kernel,
        out_shape=[shaped((12, snapshots, LANES)), shaped((HALF + 6 * snapshots, LANES))],
        in_specs=[VMEM] * 3,
        out_specs=[VMEM] * 2,
        compiler_params=LIMIT,
        name="join_near",
    )(own, from_near, sent)
    coarse, sums = pl.pallas_call(
        functools.partial(new_kernel, total),
        out_shape=[shaped((snapshots, rows_dev), BF16), shaped((HALF + 2 * snapshots, LANES))],
        in_specs=[VMEM] * 4,
        out_specs=[VMEM] * 2,
        compiler_params=LIMIT,
        name="gram_new",
    )(stored, cells, swap(crossing, "sect", 1), kept)
    sums = sum_over_span(sums)
    return tuple(factorise(sums, swap(sums, "sect", 1), stored, coarse))


def solution(mesh):
    in_specs = (P("case", None, "sect", "span", None), P(None, ("case", "span", "sect")), P())
    out_specs = (
        P(None, ("case", "span", "sect")),
        P("case", None),
        P(None, ("case", "span", "sect")),
    )
    return jax.shard_map(local, mesh=mesh, in_specs=in_specs, out_specs=out_specs, check_vma=False)
```
